32 devices in a mesh: task: 4 (over x, core), row: 8 (over z, y).
Axes of the slice: x: 2, y: 2, z: 4, core: 2. Of those that a mesh axis runs over, the one named last changes fastest.
Arguments:
- task_delta: bfloat16 [4, 28672, 4096], P('task', 'row'), may hold values from -16 to 16
- start_block: float32 [4, 4096, 32], P('task'), may hold values from -6 to 6
Outputs:
- merged: bfloat16 [28672, 4096], P(('row', 'task'))
The draws below stay inside these ranges and needn't reach their ends.
All inputs are finite; a program needn't handle non-finite values.
Results may differ from the reference program's by a relative error of at most 0.013.
Values may be sent and summed in bfloat16 or wider, within the bound.
No kernel may reach another device: no remote copies, remote signals or barrier semaphores. Data moves between devices by JAX's collectives and lax.ppermute only.
A program may use at most 128 MiB of HBM per device.

```python
import math
import jax
import jax.numpy as jnp
from jax import lax

ROWS = 28672
COLS = 4096
RANK = 32
ITERS = 4
ROOT_STEPS = 12
TASKS = 4


def draw_task_delta(key, part):
    key_base, key_own, key_first, key_last = jax.random.split(jax.random.fold_in(key, 7101), 4)
    first_cols = jax.random.uniform(key_first, (COLS,), jnp.float32, math.log(0.5), math.log(2.0))
    last_cols = jax.random.uniform(key_last, (COLS,), jnp.float32, math.log(0.5), math.log(2.0))
    position = jnp.arange(ROWS, dtype=jnp.float32) / (ROWS - 1)
    col_scale = jnp.exp((1.0 - position)[:, None] * first_cols[None, :] + position[:, None] * last_cols[None, :])
    row_amp = jnp.exp(math.log(0.6) + position * (0.5 * math.log(3.0)))
    shared = jnp.clip(jax.random.normal(key_base, (ROWS, COLS), jnp.float32), -4.0, 4.0)
    own_part = jnp.clip(jax.random.normal(key_own, (TASKS, ROWS, COLS), jnp.float32), -4.0, 4.0)
    shared_weight = 0.2 + 0.9 * position
    values = (shared_weight[:, None] * shared)[None] + own_part
    values = values * row_amp[None, :, None] * col_scale[None]
    return jnp.clip(values, -16.0, 16.0).astype(jnp.bfloat16)


def steps_of(own_key, shape, shards, low, top_value):
    loudness, own = 1.0, jax.random.fold_in(own_key, 6)
    for axis_at, shards_of in shards:
        heights = jnp.exp(jax.random.uniform(jax.random.fold_in(own, axis_at), (shards_of,), jnp.float32, low / len(shards), top_value / len(shards)))
        loudness = loudness * jnp.repeat(heights, shape[axis_at] // shards_of).reshape([-1 if axis == axis_at else 1 for axis in range(len(shape))])
    return loudness


def normal_values(stream_key, extent, scale, bound, cuts=(), kind=jnp.bfloat16):
    entries = scale * jax.random.normal(stream_key, extent, jnp.float32)
    if cuts:
        entries = entries * steps_of(stream_key, extent, cuts, -0.22, 0.18)
    return jnp.clip(entries, -bound, bound).astype(kind)


def setup_inputs(seed: int = 0) -> dict:
    key_of = jax.random.split(jax.random.key(seed), 3)
    task_delta = draw_task_delta(jax.random.fold_in(key_of[2], 71), 0)
    start_block = normal_values(key_of[1], (TASKS, COLS, RANK), 1.0, 6.0, ((0, 4),), jnp.float32)
    return dict(task_delta=task_delta, start_block=start_block)


def matmul(left, right):
    return jnp.dot(left.astype(jnp.float32), right.astype(jnp.float32), precision=lax.Precision.HIGHEST, preferred_element_type=jnp.float32)

def inverse_root(gram):
    frob_norm = jnp.sqrt(jnp.sum(gram * gram))
    identity = jnp.eye(gram.shape[0], dtype=jnp.float32)
    upper = gram / frob_norm
    lower = identity
    for step in range(ROOT_STEPS):
        middle = 0.5 * (3.0 * identity - matmul(lower, upper))
        upper = matmul(upper, middle)
        lower = matmul(middle, lower)
    return lower / jnp.sqrt(frob_norm)

def refine(task_rows, start):
    current = start
    for step in range(ITERS):
        narrow = current.astype(jnp.bfloat16)
        images = jnp.dot(task_rows.astype(jnp.float32), narrow.astype(jnp.float32), preferred_element_type=jnp.float32).astype(jnp.bfloat16)
        backs = lax.dot_general(task_rows.astype(jnp.float32), images.astype(jnp.float32), (((0,), (0,)), ((), ())), preferred_element_type=jnp.float32)
        factor = jnp.linalg.cholesky(matmul(backs.T, backs))
        current = lax.linalg.triangular_solve(factor, backs, left_side=False, lower=True, transpose_a=True)
    projected = jnp.dot(task_rows.astype(jnp.float32), current.astype(jnp.bfloat16).astype(jnp.float32), preferred_element_type=jnp.float32).astype(jnp.bfloat16)
    return (current, projected)

def reference(task_delta, start_block):
    basis_list = []
    proj_list = []
    for number in range(TASKS):
        current, projected = refine(task_delta[number], start_block[number])
        basis_list.append(current)
        proj_list.append(projected)
    bases = jnp.concatenate(basis_list, axis=1)
    wide_proj = jnp.concatenate(proj_list, axis=1).astype(jnp.float32)
    left_gram = matmul(wide_proj.T, wide_proj)
    sing = jnp.sqrt(jnp.diagonal(left_gram))
    left_norm = left_gram / (sing[:, None] * sing[None, :])
    left_root = inverse_root(left_norm)
    right_root = inverse_root(matmul(bases.T, bases))
    mixing = left_root / sing[:, None] * sing[None, :]
    left_side = matmul(wide_proj, mixing)
    right_side = matmul(bases, right_root)
    return matmul(left_side, right_side.T).astype(jnp.bfloat16)
```

```python
import functools

import jax
import jax.numpy as jnp
from jax import lax
from jax.experimental import pallas as pl
from jax.experimental.pallas import tpu as pltpu
from jax.sharding import PartitionSpec as P

ITERS = 4
ROOT_STEPS = 12
LANES = 128
F32 = jnp.float32
BF16 = jnp.bfloat16
ROWS_BY_ROWS = (((1,), (1,)), ((), ()))
VMEM_BYTES = 56 * 1024 * 1024


def params():
    return pltpu.CompilerParams(vmem_limit_bytes=VMEM_BYTES)


def exact(left, right, dims=(((1,), (0,)), ((), ()))):
    return lax.dot_general(left, right, dims, precision=lax.Precision.HIGHEST, preferred_element_type=F32)


def split_two(value):
    high = value.astype(BF16)
    return high, (value - high.astype(F32)).astype(BF16)


def split_three(value):
    high = value.astype(BF16)
    rest = value - high.astype(F32)
    middle = rest.astype(BF16)
    return high, middle, (rest - middle.astype(F32)).astype(BF16)


def spread(value, order, axis):
    pieces = split_three(value)
    return jnp.concatenate([pieces[at] for at in order], axis=axis)


def square(left, right):
    return jnp.dot(
        spread(left, (0, 0, 1, 0, 2, 1), 1), spread(right, (0, 1, 0, 2, 0, 1), 0), preferred_element_type=F32
    )


def lower_inverse(gram):
    count, size, _ = gram.shape
    rows = lax.broadcasted_iota(jnp.int32, (size, 1), 0)
    eye = (
        lax.broadcasted_iota(jnp.int32, (size, size), 0) == lax.broadcasted_iota(jnp.int32, (size, size), 1)
    ).astype(F32)
    work = [jnp.concatenate([gram[at], eye], axis=1) for at in range(count)]
    scale = [jnp.zeros((size, 1), F32) for _ in range(count)]
    for step in range(size):
        for at in range(count):
            pivot = work[at][step : step + 1, step : step + 1]
            row = work[at][step : step + 1, :] / pivot
            col = jnp.where(rows > step, work[at][:, step : step + 1], 0.0)
            scale[at] = jnp.where(rows == step, lax.rsqrt(pivot), scale[at])
            work[at] = work[at] - col * row
    return [work[at][:, size:] * scale[at] for at in range(count)]


def sweep_kernel(parts, x_ref, d_ref, out_ref, wide, total, gram):
    step = pl.program_id(0)
    rank = x_ref.shape[1]
    chunk = x_ref.shape[2]

    @pl.when(step == 0)
    def _():
        for part in range(parts):
            wide[:, part * chunk : (part + 1) * chunk] = x_ref[part]
        total[...] = jnp.zeros_like(total)
        gram[...] = jnp.zeros_like(gram)

    images = lax.dot_general(d_ref[...], wide[...], ROWS_BY_ROWS, preferred_element_type=F32)
    flipped = images.T.astype(BF16)
    total[...] += jnp.dot(flipped, d_ref[...], preferred_element_type=F32)
    gram[...] += lax.dot_general(flipped, flipped, ROWS_BY_ROWS, preferred_element_type=F32)

    @pl.when(step == pl.num_programs(0) - 1)
    def _():
        spare = jnp.zeros((rank, LANES - 3 * rank), BF16)
        pieces = jnp.concatenate([*split_three(gram[...]), spare], axis=1)
        for part in range(parts):
            out_ref[part, :, :chunk] = total[:, part * chunk : (part + 1) * chunk].astype(BF16)
            out_ref[part, :, chunk:] = pieces


def sweep(delta, block):
    rows, cols = delta.shape
    parts, rank, chunk = block.shape
    tall = next(size for size in (512, 448, rows) if rows % size == 0)
    return pl.pallas_call(
        functools.partial(sweep_kernel, parts),
        out_shape=jax.ShapeDtypeStruct((parts, rank, chunk + LANES), BF16),
        grid=(rows // tall,),
        in_specs=[
            pl.BlockSpec((parts, rank, chunk), lambda at: (0, 0, 0)),
            pl.BlockSpec((tall, cols), lambda at: (at, 0)),
        ],
        out_specs=pl.BlockSpec((parts, rank, chunk + LANES), lambda at: (0, 0, 0)),
        scratch_shapes=[
            pltpu.VMEM((rank, cols), BF16),
            pltpu.VMEM((rank, cols), F32),
            pltpu.VMEM((rank, rank), F32),
        ],
        cost_estimate=pl.CostEstimate(flops=4 * rows * cols * rank, bytes_accessed=2 * rows * cols, transcendentals=0),
        compiler_params=params(),
        name="sweep",
    )(block, delta)


def settle_kernel(in_ref, out_ref):
    parts, rank, wide = in_ref.shape
    chunk = wide - LANES
    total = in_ref[0].astype(F32)
    for part in range(1, parts):
        total = total + in_ref[part].astype(F32)
    tail = total[:, chunk:]
    gram = tail[:, :rank] + tail[:, rank : 2 * rank] + tail[:, 2 * rank : 3 * rank]
    out_ref[...] = exact(lower_inverse(gram[None])[0], total[:, :chunk]).astype(BF16)


def settle(pieces):
    parts, rank, wide = pieces.shape
    return pl.pallas_call(
        settle_kernel,
        out_shape=jax.ShapeDtypeStruct((rank, wide - LANES), BF16),
        compiler_params=params(),
        name="settle",
    )(pieces)


def project_kernel(parts, x_ref, d_ref, out_ref, wide):
    chunk = x_ref.shape[2]

    @pl.when(pl.program_id(0) == 0)
    def _():
        for part in range(parts):
            wide[:, part * chunk : (part + 1) * chunk] = x_ref[part]

    images = lax.dot_general(d_ref[...], wide[...], ROWS_BY_ROWS, preferred_element_type=F32)
    out_ref[0] = images.T.astype(BF16)


def project(delta, block, tasks):
    rows, cols = delta.shape
    parts, rank, chunk = block.shape
    tall = rows // tasks
    return pl.pallas_call(
        functools.partial(project_kernel, parts),
        out_shape=jax.ShapeDtypeStruct((tasks, rank, tall), BF16),
        grid=(tasks,),
        in_specs=[
            pl.BlockSpec((parts, rank, chunk), lambda at: (0, 0, 0)),
            pl.BlockSpec((tall, cols), lambda at: (at, 0)),
        ],
        out_specs=pl.BlockSpec((1, rank, tall), lambda at: (at, 0, 0)),
        scratch_shapes=[pltpu.VMEM((rank, cols), BF16)],
        cost_estimate=pl.CostEstimate(flops=2 * rows * cols * rank, bytes_accessed=2 * rows * cols, transcendentals=0),
        compiler_params=params(),
        name="project",
    )(block, delta)


def gram_kernel(in_ref, out_ref):
    flat = in_ref[...].reshape(-1, in_ref.shape[2])
    out_ref[...] = lax.dot_general(flat, flat, ROWS_BY_ROWS, preferred_element_type=F32).reshape(out_ref.shape)


def left_partial(images, parts):
    tasks, rank, _ = images.shape
    size = tasks * rank
    return pl.pallas_call(
        gram_kernel,
        out_shape=jax.ShapeDtypeStruct((parts, size // parts, size), F32),
        compiler_params=params(),
        name="left_partial",
    )(images)


def roots_of(grams):
    size = grams[0].shape[0]
    identity = (
        lax.broadcasted_iota(jnp.int32, (size, size), 0) == lax.broadcasted_iota(jnp.int32, (size, size), 1)
    ).astype(F32)
    norms = [jnp.sqrt(jnp.sum(gram * gram)) for gram in grams]
    state = tuple((gram / norm, identity) for gram, norm in zip(grams, norms))

    def step(_, state):
        out = []
        for upper, lower in state:
            middle = 0.5 * (3.0 * identity - square(lower, upper))
            out.append((square(upper, middle), square(middle, lower)))
        return tuple(out)

    state = lax.fori_loop(0, ROOT_STEPS, step, state)
    return [lower / jnp.sqrt(norm) for (_, lower), norm in zip(state, norms)]


def mix_kernel(tasks, left_ref, y_ref, out_ref, lower):
    parts, rows, size = left_ref.shape[1:]
    rank = size // tasks
    left_raw = left_ref[0]
    for task in range(1, tasks):
        left_raw = left_raw + left_ref[task]
    left_raw = left_raw.reshape(size, size)
    right_raw = jnp.zeros((size, size), F32)
    for part in range(y_ref.shape[1]):
        piece = y_ref[:, part].reshape(size, y_ref.shape[3])
        right_raw = right_raw + lax.dot_general(piece, piece, ROWS_BY_ROWS, preferred_element_type=F32)
    blocks = jnp.stack(
        [
            right_raw[task * rank : (task + 1) * rank, task * rank : (task + 1) * rank]
            for task in range(tasks)
        ]
    )
    lower[...] = jnp.zeros_like(lower)
    for task, inverse in enumerate(lower_inverse(blocks)):
        lower[task * rank : (task + 1) * rank, task * rank : (task + 1) * rank] = inverse
    change = lower[...]
    right_gram = square(square(change, right_raw), change.T)
    left_gram = square(square(change, left_raw), change.T)
    diagonal = lax.broadcasted_iota(jnp.int32, (size, size), 0) == lax.broadcasted_iota(jnp.int32, (size, size), 1)
    on_diagonal = jnp.where(diagonal, left_gram, 0.0)
    sing_down = jnp.sqrt(jnp.sum(on_diagonal, axis=1, keepdims=True))
    sing_across = jnp.sqrt(jnp.sum(on_diagonal, axis=0, keepdims=True))
    left_root, right_root = roots_of([left_gram / (sing_down * sing_across), right_gram])
    mixing = left_root / sing_down * sing_across
    inner = square(mixing, right_root.T)
    out_ref[...] = square(square(change.T, inner), change)


def mix(left_pieces, bases):
    tasks, parts, rows, size = left_pieces.shape
    return pl.pallas_call(
        functools.partial(mix_kernel, tasks),
        out_shape=jax.ShapeDtypeStruct((size, size), F32),
        scratch_shapes=[pltpu.VMEM((size, size), F32)],
        compiler_params=params(),
        name="mix",
    )(left_pieces, bases)


def merge_kernel(mix_ref, p_ref, y_ref, out_ref, left):
    size = mix_ref.shape[0]

    @pl.when(pl.program_id(0) == 0)
    def _():
        images = p_ref[...].reshape(size, p_ref.shape[2]).T
        high, low = split_two(mix_ref[...])
        side = jnp.dot(images, high, preferred_element_type=F32) + jnp.dot(images, low, preferred_element_type=F32)
        left[...] = jnp.concatenate(split_two(side), axis=1)

    bases = y_ref[...].reshape(size, y_ref.shape[3])
    bases = jnp.concatenate([bases, bases], axis=0)
    out_ref[...] = jnp.dot(left[...], bases, preferred_element_type=F32).astype(BF16)


def merge(mixed, images, bases):
    tasks, parts, rank, chunk = bases.shape
    rows = images.shape[2]
    size = tasks * rank
    return pl.pallas_call(
        merge_kernel,
        out_shape=jax.ShapeDtypeStruct((rows, parts * chunk), BF16),
        grid=(parts,),
        in_specs=[
            pl.BlockSpec((size, size), lambda at: (0, 0)),
            pl.BlockSpec((tasks, rank, rows), lambda at: (0, 0, 0)),
            pl.BlockSpec((tasks, 1, rank, chunk), lambda at: (0, at, 0, 0)),
        ],
        out_specs=pl.BlockSpec((rows, chunk), lambda at: (0, at)),
        scratch_shapes=[pltpu.VMEM((rows, 2 * size), BF16)],
        compiler_params=params(),
        name="merge",
    )(mixed, images, bases)


def swap(pieces, axis):
    return lax.all_to_all(pieces, axis, split_axis=0, concat_axis=0, tiled=True)


def share(piece, axis, count):
    return swap(jnp.broadcast_to(piece[None], (count, *piece.shape)), axis)


def local(tasks, parts, task_delta, start_block):
    delta = task_delta[0]
    cols, rank = start_block.shape[1:]
    block = start_block[0].T.astype(BF16).reshape(rank, parts, cols // parts).transpose(1, 0, 2)
    for step in range(ITERS):
        block = share(settle(swap(sweep(delta, block), "row")), "row", parts)
    gathered = [block]
    for shift in range(1, tasks):
        gathered.append(lax.ppermute(block, "task", [(at, (at + shift) % tasks) for at in range(tasks)]))
    images = swap(project(delta, block, tasks), "task")
    own = lax.axis_index("task")
    bases = jnp.stack(gathered)[(own - jnp.arange(tasks)) % tasks]
    partial = jnp.sum(swap(left_partial(images, parts), "row"), axis=0)
    left_pieces = share(partial, ("task", "row"), tasks * parts).reshape(tasks, parts, *partial.shape)
    return merge(mix(left_pieces, bases), images, bases)


def solution(mesh):
    tasks, parts = mesh.shape["task"], mesh.shape["row"]
    placed = (P("task", "row", None), P("task", None, None))
    return jax.shard_map(
        functools.partial(local, tasks, parts),
        mesh=mesh,
        in_specs=placed,
        out_specs=P(("row", "task"), None),
        check_vma=False,
    )
```

```python
import functools

import jax
import jax.numpy as jnp
from jax import lax
from jax.experimental import pallas as pl
from jax.experimental.pallas import tpu as pltpu
from jax.sharding import PartitionSpec as P

ITERS = 4
ROOT_STEPS = 12
HALVES = 2
LANES = 128
F32 = jnp.float32
BF16 = jnp.bfloat16
ROWS_BY_ROWS = (((1,), (1,)), ((), ()))
VMEM_BYTES = 26 * 1024 * 1024
IN_VMEM = pl.BlockSpec(memory_space=pltpu.VMEM)


def params():
    return pltpu.CompilerParams(vmem_limit_bytes=VMEM_BYTES)


def cost(flops, moved):
    return pl.CostEstimate(flops=flops, bytes_accessed=moved, transcendentals=0)


def split_two(value):
    high = value.astype(BF16)
    return high, (value - high.astype(F32)).astype(BF16)


def split_three(value):
    high = value.astype(BF16)
    rest = value - high.astype(F32)
    middle = rest.astype(BF16)
    return high, middle, (rest - middle.astype(F32)).astype(BF16)


def spread(value, order, axis):
    pieces = split_three(value)
    return jnp.concatenate([pieces[at] for at in order], axis=axis)


def square(left, right):
    return jnp.dot(
        spread(left, (0, 0, 1, 0, 2, 1), 1), spread(right, (0, 1, 0, 2, 0, 1), 0), preferred_element_type=F32
    )


def eye_of(size):
    return lax.broadcasted_iota(jnp.int32, (size, size), 0) == lax.broadcasted_iota(jnp.int32, (size, size), 1)


def lower_inverse(grams):
    size = grams[0].shape[0]
    rows = lax.broadcasted_iota(jnp.int32, (size, 1), 0)
    eye = eye_of(size).astype(F32)
    work = [jnp.concatenate([gram, eye], axis=1) for gram in grams]
    scale = [jnp.zeros((size, 1), F32) for _ in grams]
    for step in range(0, size, 2):
        after = step + 1
        for at, now in enumerate(work):
            first, second = now[step:after, :], now[after : after + 1, :]
            pivot, beside = now[step:after, step:after], now[step:after, after : after + 1]
            inverse = 1.0 / pivot
            ratio = beside * inverse
            second = second - ratio * first
            below = now[after : after + 1, after : after + 1] - ratio * beside
            col, col_after = now[:, step:after], now[:, after : after + 1]
            scale[at] = jnp.where(rows == step, lax.rsqrt(pivot), scale[at])
            scale[at] = jnp.where(rows == after, lax.rsqrt(below), scale[at])
            work[at] = (
                now
                - jnp.where(rows > step, col, 0.0) * (first * inverse)
                - jnp.where(rows > after, col_after - col * ratio, 0.0) * (second * (1.0 / below))
            )
    return [now[:, size:] * down for now, down in zip(work, scale)]


def tall_of(rows, *sizes):
    return next(size for size in (*sizes, rows) if rows % size == 0)


def first_kernel(tall, x_ref, d_ref, held_ref, out_ref, start, wide, sems, start_sem):
    count = d_ref.shape[0] // tall

    def copy(at):
        span = pl.ds(pl.multiple_of(at * tall, tall), tall)
        return pltpu.make_async_copy(d_ref.at[span], held_ref.at[span], sems.at[at])

    start_copy = pltpu.make_async_copy(x_ref, start, start_sem)
    start_copy.start()
    for at in range(count):
        copy(at).start()
    start_copy.wait()
    wide[...] = start[...].astype(BF16)

    def body(at, carry):
        copy(at).wait()
        span = pl.ds(pl.multiple_of(at * tall, tall), tall)
        out_ref[:, span] = lax.dot_general(
            wide[...], held_ref[span, :], ROWS_BY_ROWS, preferred_element_type=F32
        ).astype(BF16)
        return carry

    lax.fori_loop(0, count, body, 0)


def first(delta, start):
    rows, cols = delta.shape
    rank = start.shape[0]
    tall = tall_of(rows, 256, 128)
    return pl.pallas_call(
        functools.partial(first_kernel, tall),
        out_shape=(pltpu.VMEM((rows, cols), BF16), jax.ShapeDtypeStruct((rank, rows), BF16)),
        in_specs=[pl.BlockSpec(memory_space=pl.ANY)] * 2,
        out_specs=(IN_VMEM, IN_VMEM),
        scratch_shapes=[
            pltpu.VMEM((rank, cols), F32),
            pltpu.VMEM((rank, cols), BF16),
            pltpu.SemaphoreType.DMA((rows // tall,)),
            pltpu.SemaphoreType.DMA,
        ],
        cost_estimate=cost(2 * rows * cols * rank, 2 * rows * cols),
        compiler_params=params(),
        name="first",
    )(start, delta)


def backs_kernel(half, across, with_gram, images_ref, d_ref, _, out_ref):
    parts, rank, wide = out_ref.shape
    chunk = wide - LANES if with_gram else wide
    skip = wide - chunk
    images = images_ref[...]
    if with_gram:
        gram = lax.dot_general(images, images, ROWS_BY_ROWS, preferred_element_type=F32)
        spare = jnp.zeros((rank, LANES - 3 * rank), BF16)
        pieces = jnp.concatenate([*split_three(gram), spare], axis=1)
        for part in range(parts):
            out_ref[part, :, :skip] = pieces

    def body(at, carry):
        span = pl.ds(pl.multiple_of(half * parts * chunk + at * across, across), across)
        total = jnp.dot(images_ref[...], d_ref[:, span], preferred_element_type=F32).astype(BF16)
        for inner in range(across // chunk):
            out_ref[at * (across // chunk) + inner, :, skip:] = total[:, inner * chunk : (inner + 1) * chunk]
        return carry

    lax.fori_loop(0, parts * chunk // across, body, 0)


def backs(held, images, half, parts, with_gram):
    rows, cols = held.shape
    rank = images.shape[0]
    chunk = cols // HALVES // parts
    return pl.pallas_call(
        functools.partial(backs_kernel, half, max(chunk, 512), with_gram),
        out_shape=(
            pltpu.VMEM(held.shape, BF16),
            jax.ShapeDtypeStruct((parts, rank, chunk + (LANES if with_gram else 0)), BF16),
        ),
        in_specs=[IN_VMEM, IN_VMEM],
        out_specs=(IN_VMEM, IN_VMEM),
        input_output_aliases={1: 0},
        cost_estimate=cost(2 * rows * cols // HALVES * rank, 2 * rows * cols // HALVES),
        compiler_params=params(),
        name="backs",
    )(images, held)


def settle_first_kernel(in_ref, held_ref, after_ref, _, out_ref, lower_ref):
    parts, rank, wide = in_ref.shape
    total = in_ref[0].astype(F32)
    for part in range(1, parts):
        total = total + in_ref[part].astype(F32)
    gram = total[:, :rank] + total[:, rank : 2 * rank] + total[:, 2 * rank : 3 * rank]
    lower = lower_inverse([gram])[0]
    lower_ref[...] = lower
    block = square(lower, total[:, LANES:]).astype(BF16)
    for part in range(parts):
        out_ref[part] = block


def settle_next_kernel(in_ref, held_ref, lower_ref, _, out_ref):
    parts = in_ref.shape[0]
    total = in_ref[0].astype(F32)
    for part in range(1, parts):
        total = total + in_ref[part].astype(F32)
    block = square(lower_ref[...], total).astype(BF16)
    for part in range(parts):
        out_ref[part] = block


def settle_first(held, pieces, after):
    parts, rank, wide = pieces.shape
    return pl.pallas_call(
        settle_first_kernel,
        out_shape=(
            pltpu.VMEM(held.shape, BF16),
            jax.ShapeDtypeStruct((parts, rank, wide - LANES), BF16),
            jax.ShapeDtypeStruct((rank, rank), F32),
        ),
        in_specs=[IN_VMEM, IN_VMEM, pl.BlockSpec(memory_space=pl.ANY)],
        out_specs=(IN_VMEM, IN_VMEM, IN_VMEM),
        input_output_aliases={1: 0},
        cost_estimate=cost(10**8, 4 * 10**6),
        compiler_params=params(),
        name="settle_first",
    )(pieces, held, after)


def settle_next(held, pieces, lower):
    return pl.pallas_call(
        settle_next_kernel,
        out_shape=(pltpu.VMEM(held.shape, BF16), jax.ShapeDtypeStruct(pieces.shape, BF16)),
        in_specs=[IN_VMEM, IN_VMEM, IN_VMEM],
        out_specs=(IN_VMEM, IN_VMEM),
        input_output_aliases={1: 0},
        cost_estimate=cost(10**8, 2 * 10**6),
        compiler_params=params(),
        name="settle_next",
    )(pieces, held, lower)


def images_kernel(half, tall, partial, *refs):
    x_ref, d_ref = refs[:2]
    _, out_ref, wide, flat = refs[-4:]
    parts, _, chunk = x_ref.shape
    for part in range(parts):
        wide[:, part * chunk : (part + 1) * chunk] = x_ref[part]
    width = parts * chunk
    target = out_ref if len(out_ref.shape) == 2 else flat

    def body(at, carry):
        span = pl.ds(pl.multiple_of(at * tall, tall), tall)
        product = lax.dot_general(
            wide[...], d_ref[span, half * width : (half + 1) * width], ROWS_BY_ROWS, preferred_element_type=F32
        )
        if partial:
            product = product + refs[2][:, span]
        target[:, span] = product.astype(target.dtype)
        return carry

    lax.fori_loop(0, d_ref.shape[0] // tall, body, 0)
    if target is flat:
        each = out_ref.shape[2]
        for at in range(out_ref.shape[0]):
            out_ref[at] = flat[:, at * each : (at + 1) * each]


def images(held, block, half, partial=None, pieces=None):
    rows, cols = held.shape
    rank = block.shape[1]
    tall = tall_of(rows, 512, 896, 256, 128)
    shape = (rank, rows) if pieces is None else (pieces, rank, rows // pieces)
    operands = (block, held) if partial is None else (block, held, partial)
    return pl.pallas_call(
        functools.partial(images_kernel, half, tall, partial is not None),
        out_shape=(pltpu.VMEM(held.shape, BF16), jax.ShapeDtypeStruct(shape, F32 if partial is None else BF16)),
        in_specs=[IN_VMEM] * len(operands),
        out_specs=(IN_VMEM, IN_VMEM),
        input_output_aliases={1: 0},
        scratch_shapes=[pltpu.VMEM((rank, cols // HALVES), BF16), pltpu.VMEM((rank, rows), BF16)],
        cost_estimate=cost(2 * rows * cols // HALVES * rank, 2 * rows * cols // HALVES),
        compiler_params=params(),
        name="images",
    )(*operands)


def gram_kernel(in_ref, out_ref):
    flat = in_ref[...].reshape(-1, in_ref.shape[2])
    out_ref[...] = lax.dot_general(flat, flat, ROWS_BY_ROWS, preferred_element_type=F32).reshape(out_ref.shape)


def left_partial(panel, parts):
    tasks, rank, _ = panel.shape
    size = tasks * rank
    return pl.pallas_call(
        gram_kernel,
        out_shape=jax.ShapeDtypeStruct((parts, size // parts, size), F32),
        in_specs=[IN_VMEM],
        out_specs=IN_VMEM,
        compiler_params=params(),
        name="left_partial",
    )(panel)


def inverse_root(gram):
    identity = eye_of(gram.shape[0]).astype(F32)
    norm = jnp.sqrt(jnp.sum(gram * gram))

    def step(_, state):
        upper, lower = state
        middle = 0.5 * (3.0 * identity - square(lower, upper))
        return square(upper, middle), square(middle, lower)

    _, lower = lax.fori_loop(0, ROOT_STEPS, step, (gram / norm, identity))
    return lower / jnp.sqrt(norm)


def right_kernel(masks, parts, own_ref, *refs):
    blocks, (wide_ref, lower_ref, right_ref) = refs[:-3], refs[-3:]
    rank, chunk = blocks[0].shape[1:]
    tasks = len(masks)
    size = tasks * rank
    own = own_ref[0]
    for at, block in enumerate(blocks):
        half, place = divmod(at, tasks)
        down = pl.ds(pl.multiple_of(lax.bitwise_xor(own, masks[place]) * rank, rank), rank)
        for part in range(parts):
            left = (half * parts + part) * chunk
            wide_ref[down, left : left + chunk] = block[part]
    wide = wide_ref[...]
    raw = lax.dot_general(wide, wide, ROWS_BY_ROWS, preferred_element_type=F32)
    spans = [slice(task * rank, (task + 1) * rank) for task in range(tasks)]
    lower_ref[...] = jnp.zeros_like(lower_ref)
    for span, inverse in zip(spans, lower_inverse([raw[span, span] for span in spans])):
        lower_ref[span, span] = inverse
    lower = lower_ref[...]
    root = inverse_root(square(square(lower, raw), lower.T))
    right_ref[...] = square(root.T, lower)


def right(own, blocks, masks):
    parts, rank, chunk = blocks[0].shape
    size = len(masks) * rank
    return pl.pallas_call(
        functools.partial(right_kernel, masks, parts),
        out_shape=(
            jax.ShapeDtypeStruct((size, HALVES * parts * chunk), BF16),
            jax.ShapeDtypeStruct((size, size), F32),
            jax.ShapeDtypeStruct((size, size), F32),
        ),
        in_specs=[pl.BlockSpec(memory_space=pltpu.SMEM)] + [IN_VMEM] * len(blocks),
        out_specs=(IN_VMEM,) * 3,
        cost_estimate=cost(10**10, 10**6),
        compiler_params=params(),
        name="right",
    )(own, *blocks)


def finish_kernel(tasks, gram_ref, panel_ref, wide_ref, lower_ref, right_ref, out_ref, side):
    size = lower_ref.shape[0]

    @pl.when(pl.program_id(0) == 0)
    def _():
        raw = gram_ref[0]
        for task in range(1, tasks):
            raw = raw + gram_ref[task]
        raw = raw.reshape(size, size)
        lower = lower_ref[...]
        gram = square(square(lower, raw), lower.T)
        diagonal = jnp.where(eye_of(size), gram, 0.0)
        down = jnp.sqrt(jnp.sum(diagonal, axis=1, keepdims=True))
        across = jnp.sqrt(jnp.sum(diagonal, axis=0, keepdims=True))
        mixing = inverse_root(gram / (down * across)) / down * across
        mixed = square(square(lower.T, mixing), right_ref[...])
        panel = panel_ref[...].reshape(size, panel_ref.shape[2]).T
        product = jnp.dot(
            jnp.concatenate([panel, panel], axis=1),
            jnp.concatenate(split_two(mixed), axis=0),
            preferred_element_type=F32,
        )
        side[...] = jnp.concatenate(split_two(product), axis=1)

    wide = wide_ref[...]
    out_ref[...] = jnp.dot(
        side[...], jnp.concatenate([wide, wide], axis=0), preferred_element_type=F32
    ).astype(BF16)


def finish(grams, panel, wide, lower, right_side):
    tasks, parts, each, size = grams.shape
    rows, cols = panel.shape[2], wide.shape[1]
    across = 512

    def whole(shape):
        return pl.BlockSpec(shape, lambda at: (0,) * len(shape))

    return pl.pallas_call(
        functools.partial(finish_kernel, tasks),
        out_shape=jax.ShapeDtypeStruct((rows, cols), BF16),
        grid=(cols // across,),
        in_specs=[
            whole(grams.shape),
            whole(panel.shape),
            pl.BlockSpec((size, across), lambda at: (0, at)),
            whole(lower.shape),
            whole(right_side.shape),
        ],
        out_specs=pl.BlockSpec((rows, across), lambda at: (0, at)),
        scratch_shapes=[pltpu.VMEM((rows, 2 * size), BF16)],
        compiler_params=params(),
        name="finish",
    )(grams, panel, wide, lower, right_side)


def swap(pieces, axis):
    return lax.all_to_all(pieces, axis, split_axis=0, concat_axis=0, tiled=True)


def spread_over_tasks(block, tasks):
    masks, blocks = [0], [block]
    bit = tasks // 2
    while bit:
        pairs = [(at, at ^ bit) for at in range(tasks)]
        blocks = blocks + [lax.ppermute(each, "task", pairs) for each in blocks]
        masks = masks + [mask ^ bit for mask in masks]
        bit //= 2
    return tuple(masks), blocks


def local(tasks, parts, task_delta, start_block):
    held, panel = first(task_delta[0], start_block[0].T)
    for step in range(ITERS):
        held, near = backs(held, panel, 0, parts, True)
        held, far = backs(held, panel, 1, parts, False)
        held, near, lower = settle_first(held, swap(near, "row"), far)
        near = swap(near, "row")
        held, far = settle_next(held, swap(far, "row"), lower)
        far = swap(far, "row")
        held, panel = images(held, near, 0)
        held, panel = images(held, far, 1, panel, tasks if step == ITERS - 1 else None)
    masks, near_all = spread_over_tasks(near, tasks)
    _, far_all = spread_over_tasks(far, tasks)
    panel = swap(panel, "task")
    partial = jnp.sum(swap(left_partial(panel, parts), "row"), axis=0)
    grams = swap(jnp.broadcast_to(partial[None], (tasks * parts, *partial.shape)), ("task", "row"))
    own = lax.axis_index("task").astype(jnp.int32).reshape(1)
    wide, lower, right_side = right(own, near_all + far_all, masks)
    return finish(grams.reshape(tasks, parts, *partial.shape), panel, wide, lower, right_side)


def solution(mesh):
    tasks, parts = mesh.shape["task"], mesh.shape["row"]
    placed = (P("task", "row", None), P("task", None, None))
    return jax.shard_map(
        functools.partial(local, tasks, parts),
        mesh=mesh,
        in_specs=placed,
        out_specs=P(("row", "task"), None),
        check_vma=False,
    )
```

```python
import functools

import jax
import jax.numpy as jnp
from jax import lax
from jax.experimental import pallas as pl
from jax.experimental.pallas import tpu as pltpu
from jax.sharding import PartitionSpec as P

ITERS = 4
ROOT_STEPS = 12
LANES = 128
TILE = 8
F32 = jnp.float32
BF16 = jnp.bfloat16
ROWS_BY_ROWS = (((1,), (1,)), ((), ()))
VMEM_BYTES = 16 * 1024 * 1024
IN_VMEM = pl.BlockSpec(memory_space=pltpu.VMEM)
ANYWHERE = pl.BlockSpec(memory_space=pl.ANY)


def shape_of(shape, kind):
    return jax.ShapeDtypeStruct(shape, kind)


def call(kernel, name, operands, shapes, scratch=(), held=None, idle=(), flops=10**8):
    operands = [*operands, *idle]
    specs = [IN_VMEM] * (len(operands) - len(idle)) + [ANYWHERE] * len(idle)
    if held is not None:
        operands, specs = [held, *operands], [IN_VMEM, *specs]
    return pl.pallas_call(
        kernel,
        out_shape=tuple(shapes),
        in_specs=specs,
        out_specs=(IN_VMEM,) * len(shapes),
        scratch_shapes=list(scratch),
        cost_estimate=pl.CostEstimate(flops=flops, bytes_accessed=10**6, transcendentals=0),
        compiler_params=pltpu.CompilerParams(vmem_limit_bytes=VMEM_BYTES),
        name=name,
    )(*operands)


def split_two(value):
    high = value.astype(BF16)
    return high, (value - high.astype(F32)).astype(BF16)


def split_three(value):
    high = value.astype(BF16)
    rest = value - high.astype(F32)
    middle = rest.astype(BF16)
    return high, middle, (rest - middle.astype(F32)).astype(BF16)


def spread(value, order, axis):
    pieces = split_three(value)
    return jnp.concatenate([pieces[at] for at in order], axis=axis)


def square(left, right):
    return jnp.dot(
        spread(left, (0, 0, 1, 0, 2, 1), 1), spread(right, (0, 1, 0, 2, 0, 1), 0), preferred_element_type=F32
    )


def eye_of(size):
    return lax.broadcasted_iota(jnp.int32, (size, size), 0) == lax.broadcasted_iota(jnp.int32, (size, size), 1)


def tree_sum(values):
    while len(values) > 1:
        values = [values[at] + values[at + 1] for at in range(0, len(values), 2)]
    return values[0]


def lower_inverse(grams):
    size = grams[0].shape[0]
    tiles = size // TILE
    rows = lax.broadcasted_iota(jnp.int32, (TILE, LANES), 0)
    lanes = lax.broadcasted_iota(jnp.int32, (TILE, LANES), 1)
    columns, inverses, scales = [], [], []
    for gram in grams:
        wide = [jnp.broadcast_to(gram[:, at : at + 1], (size, LANES)) for at in range(size)]
        columns.append([[one[TILE * tile : TILE * (tile + 1)] for tile in range(tiles)] for one in wide])
        inverses.append([(rows + TILE * tile == lanes).astype(F32) for tile in range(tiles)])
        scales.append([jnp.zeros((TILE, LANES), F32) for _ in range(tiles)])
    for step in range(size):
        top, place = divmod(step, TILE)
        for cols, inverse, scale in zip(columns, inverses, scales):
            pivot = cols[step][top][place : place + 1]
            reciprocal = 1.0 / pivot
            ratio = [None] * top + [cols[step][tile] * reciprocal for tile in range(top, tiles)]
            for later in range(step + 1, size):
                first, inner = divmod(later, TILE)
                factor = ratio[first][inner : inner + 1]
                for tile in range(first, tiles):
                    cols[later][tile] = cols[later][tile] - cols[step][tile] * factor
            own = inverse[top][place : place + 1]
            for tile in range(top, tiles):
                factor = jnp.where(rows > place, ratio[tile], 0.0) if tile == top else ratio[tile]
                inverse[tile] = inverse[tile] - factor * own
            scale[top] = jnp.where(rows == place, lax.rsqrt(pivot), scale[top])
    return [
        jnp.concatenate([one * down for one, down in zip(inverse, scale)], axis=0)[:, :size]
        for inverse, scale in zip(inverses, scales)
    ]


def gram_pieces(images):
    rank = images.shape[0]
    gram = lax.dot_general(images, images, ROWS_BY_ROWS, preferred_element_type=F32)
    return jnp.concatenate([*split_three(gram), jnp.zeros((rank, LANES - 3 * rank), BF16)], axis=1)


def tall_of(rows, *sizes):
    return next(size for size in (*sizes, rows) if rows % size == 0)


def partner(axis, mask):
    return lax.bitwise_xor(lax.axis_index(axis).astype(jnp.int32), jnp.int32(mask))


def block_at(index, size):
    return pl.ds(pl.multiple_of(index * size, size), size)


def first_kernel(tall, d_ref, x_ref, out_ref, gram_ref, wide):
    wide[...] = x_ref[...].astype(BF16)

    def body(at, carry):
        span = block_at(at, tall)
        product = lax.dot_general(wide[...], d_ref[span, :], ROWS_BY_ROWS, preferred_element_type=F32)
        out_ref[:, span] = product.astype(BF16)
        return carry

    lax.fori_loop(0, d_ref.shape[0] // tall, body, 0)
    gram_ref[...] = gram_pieces(out_ref[...])


def first(held, start):
    rows, cols = held.shape
    rank = start.shape[0]
    return call(
        functools.partial(first_kernel, tall_of(rows, 512, 896, 256, 128)),
        "first",
        [start],
        [shape_of((rank, rows), BF16), shape_of((rank, LANES), BF16)],
        [pltpu.VMEM((rank, cols), BF16)],
        held=held,
        flops=2 * rows * cols * 384,
    )


def backs_kernel(masks, d_ref, images_ref, gram_ref, *out_refs):
    for mask, out_ref in zip(masks, out_refs[-len(masks) :]):
        chunk = out_ref.shape[1] - LANES
        span = block_at(partner("row", mask), chunk)
        out_ref[:, :LANES] = gram_ref[...]
        out_ref[:, LANES:] = jnp.dot(images_ref[...], d_ref[:, span], preferred_element_type=F32).astype(BF16)


def backs(held, panel, gram, masks, parts, *after):
    rows, cols = held.shape
    rank = panel.shape[0]
    pieces = call(
        functools.partial(backs_kernel, masks),
        "backs",
        [panel, gram],
        [shape_of((rank, cols // parts + LANES), BF16)] * len(masks),
        held=held,
        idle=after,
        flops=2 * rows * cols * 256 // parts * len(masks),
    )
    return dict(zip(masks, pieces))


def settle_kernel(_, *refs):
    *in_refs, out_ref = refs
    total = tree_sum([ref[...].astype(F32) for ref in in_refs])
    rank = total.shape[0]
    gram = total[:, :rank] + total[:, rank : 2 * rank] + total[:, 2 * rank : 3 * rank]
    out_ref[...] = square(lower_inverse([gram])[0], total[:, LANES:]).astype(BF16)


def settle(held, pieces):
    rank, wide = pieces[0].shape
    return call(settle_kernel, "settle", pieces, [shape_of((rank, wide - LANES), BF16)], held=held)


def images_kernel(masks, tall, partial, tasks, d_ref, *refs):
    x_refs, refs = refs[: len(masks)], refs[len(masks) :]
    if partial:
        sum_ref, refs = refs[0], refs[1:]
    target = refs[-2] if tasks else refs[0]
    chunk = x_refs[0].shape[1]

    def body(at, carry):
        span = block_at(at, tall)
        product = sum_ref[:, span] if partial else None
        for mask, x_ref in zip(masks, x_refs):
            term = lax.dot_general(
                x_ref[...],
                d_ref[span, block_at(partner("row", mask), chunk)],
                ROWS_BY_ROWS,
                preferred_element_type=F32,
            )
            product = term if product is None else product + term
        target[:, span] = product.astype(target.dtype)
        return carry

    lax.fori_loop(0, d_ref.shape[0] // tall, body, 0)
    if tasks:
        *out_refs, flat, stacked = refs
        each = stacked.shape[2]
        for at in range(tasks):
            stacked[at] = flat[:, at * each : (at + 1) * each]
        for mask, out_ref in enumerate(out_refs):
            out_ref[...] = stacked[partner("task", mask)]
    elif len(refs) == 2:
        refs[1][...] = gram_pieces(refs[0][...])


def images(held, blocks, masks, partial=None, last=False, tasks=0):
    rows, cols = held.shape
    rank = blocks[0].shape[0]
    scratch = ()
    if tasks:
        shapes = [shape_of((rank, rows // tasks), BF16)] * tasks
        scratch = [pltpu.VMEM((rank, rows), BF16), pltpu.VMEM((tasks, rank, rows // tasks), BF16)]
    elif last:
        shapes = [shape_of((rank, rows), BF16), shape_of((rank, LANES), BF16)]
    else:
        shapes = [shape_of((rank, rows), F32)]
    return call(
        functools.partial(images_kernel, masks, tall_of(rows, 512, 896, 256, 128), partial is not None, tasks),
        "images",
        [blocks[mask] for mask in masks] + ([] if partial is None else [partial]),
        shapes,
        scratch,
        held=held,
        flops=2 * rows * cols * 384 * len(masks) // len(blocks),
    )


def pack_kernel(_, *refs):
    *in_refs, out_ref = refs
    chunk = in_refs[0].shape[1]
    for mask, in_ref in enumerate(in_refs):
        out_ref[:, block_at(partner("row", mask), chunk)] = in_ref[...]


def left_kernel(*refs):
    tasks = next(at for at, ref in enumerate(refs) if ref.shape != refs[0].shape)
    in_refs, panel_ref, out_refs, gram = refs[:tasks], refs[tasks], refs[tasks + 1 : -1], refs[-1]
    rank = in_refs[0].shape[0]
    for mask, in_ref in enumerate(in_refs):
        panel_ref[block_at(partner("task", mask), rank), :] = in_ref[...]
    gram[...] = lax.dot_general(panel_ref[...], panel_ref[...], ROWS_BY_ROWS, preferred_element_type=F32)
    for mask, out_ref in enumerate(out_refs):
        out_ref[...] = gram[block_at(partner("row", mask), out_ref.shape[0]), :]


def left(pieces, parts):
    tasks = len(pieces)
    rank, each = pieces[0].shape
    size = tasks * rank
    return call(
        left_kernel,
        "left",
        pieces,
        [shape_of((size, each), BF16)] + [shape_of((size // parts, size), F32)] * parts,
        [pltpu.VMEM((size, size), F32)],
    )


def total_kernel(count, *refs):
    refs[-1][...] = tree_sum([ref[...] for ref in refs[:count]])


def total(pieces, after):
    return call(
        functools.partial(total_kernel, len(pieces)),
        "total",
        pieces,
        [shape_of(pieces[0].shape, F32)],
        idle=[after],
        flops=10**6,
    )[0]


def root_begin(gram):
    return gram / jnp.sqrt(jnp.sum(gram * gram)), eye_of(gram.shape[0]).astype(F32)


def root_steps(state, count):
    identity = eye_of(state[0].shape[0]).astype(F32)

    def step(_, state):
        upper, lower = state
        middle = 0.5 * (3.0 * identity - square(lower, upper))
        return square(upper, middle), square(middle, lower)

    return lax.fori_loop(0, count, step, state)


def root_end(state, gram):
    return state[1] / jnp.sqrt(jnp.sqrt(jnp.sum(gram * gram)))


def right_first_kernel(*refs):
    in_refs, (wide_ref, lower_ref, gram_ref) = refs[:-3], refs[-3:]
    rank = in_refs[0].shape[0]
    for mask, in_ref in enumerate(in_refs):
        wide_ref[block_at(partner("task", mask), rank), :] = in_ref[...]
    wide = wide_ref[...]
    raw = lax.dot_general(wide, wide, ROWS_BY_ROWS, preferred_element_type=F32)
    spans = [slice(task * rank, (task + 1) * rank) for task in range(len(in_refs))]
    lower_ref[...] = jnp.zeros_like(lower_ref)
    for span, inverse in zip(spans, lower_inverse([raw[span, span] for span in spans])):
        lower_ref[span, span] = inverse
    lower = lower_ref[...]
    gram_ref[...] = square(square(lower, raw), lower.T)


def right_second_kernel(gram_ref, upper_ref, lower_ref):
    upper_ref[...], lower_ref[...] = root_steps(root_begin(gram_ref[...]), ROOT_STEPS // 2)


def right_third_kernel(gram_ref, upper_ref, lower_ref, change_ref, out_ref):
    state = root_steps((upper_ref[...], lower_ref[...]), ROOT_STEPS - ROOT_STEPS // 2)
    out_ref[...] = square(root_end(state, gram_ref[...]).T, change_ref[...])


def finish_kernel(parts, *refs):
    gram_refs, (panel_ref, wide_ref, lower_ref, right_ref, out_ref, raw, side) = refs[:parts], refs[parts:]
    size = lower_ref.shape[0]

    @pl.when(pl.program_id(0) == 0)
    def _():
        for mask, gram_ref in enumerate(gram_refs):
            raw[block_at(partner("row", mask), gram_ref.shape[0]), :] = gram_ref[...]
        lower = lower_ref[...]
        gram = square(square(lower, raw[...]), lower.T)
        diagonal = jnp.where(eye_of(size), gram, 0.0)
        down = jnp.sqrt(jnp.sum(diagonal, axis=1, keepdims=True))
        across = jnp.sqrt(jnp.sum(diagonal, axis=0, keepdims=True))
        normed = gram / (down * across)
        mixing = root_end(root_steps(root_begin(normed), ROOT_STEPS), normed) / down * across
        mixed = square(square(lower.T, mixing), right_ref[...])
        panel = panel_ref[...].T
        product = jnp.dot(
            jnp.concatenate([panel, panel], axis=1),
            jnp.concatenate(split_two(mixed), axis=0),
            preferred_element_type=F32,
        )
        side[...] = jnp.concatenate(split_two(product), axis=1)

    wide = wide_ref[...]
    out_ref[...] = jnp.dot(
        side[...], jnp.concatenate([wide, wide], axis=0), preferred_element_type=F32
    ).astype(BF16)


def finish(grams, panel, wide, lower, right_side):
    size, rows = panel.shape
    cols = wide.shape[1]
    across = 512

    def whole(array):
        return pl.BlockSpec(array.shape, lambda at: (0, 0))

    return pl.pallas_call(
        functools.partial(finish_kernel, len(grams)),
        out_shape=shape_of((rows, cols), BF16),
        grid=(cols // across,),
        in_specs=[
            *map(whole, grams),
            whole(panel),
            pl.BlockSpec((size, across), lambda at: (0, at)),
            whole(lower),
            whole(right_side),
        ],
        out_specs=pl.BlockSpec((rows, across), lambda at: (0, at)),
        scratch_shapes=[pltpu.VMEM((size, size), F32), pltpu.VMEM((rows, 2 * size), BF16)],
        compiler_params=pltpu.CompilerParams(vmem_limit_bytes=VMEM_BYTES),
        name="finish",
    )(*grams, panel, wide, lower, right_side)


def send(piece, axis, mask, count):
    return lax.ppermute(piece, axis, [(at, at ^ mask) for at in range(count)]) if mask else piece


def swap(pieces, axis):
    return [send(pieces[mask], axis, mask, len(pieces)) for mask in range(len(pieces))]


def share(piece, axis, count):
    return [send(piece, axis, mask, count) for mask in range(count)]


def spread_over_tasks(block, tasks):
    masks, blocks = [0], [block]
    bit = tasks // 2
    while bit:
        blocks = blocks + [send(each, "task", bit, tasks) for each in blocks]
        masks = masks + [mask ^ bit for mask in masks]
        bit //= 2
    return [block for _, block in sorted(zip(masks, blocks), key=lambda pair: pair[0])]


def local(tasks, parts, task_delta, start_block):
    near, far = tuple(range(1, parts // 2)), tuple(range(parts // 2, parts))
    size = tasks * start_block.shape[2]
    held = pltpu.with_memory_space_constraint(task_delta[0], pltpu.VMEM)
    panel, gram = first(held, start_block[0].T)
    for step in range(ITERS):
        last = step == ITERS - 1
        away = backs(held, panel, gram, far, parts)
        close = backs(held, panel, gram, (*near, 0), parts, away[far[0]])
        (block,) = settle(held, swap({**away, **close}, "row"))
        blocks = share(block, "row", parts)
        (partial,) = images(held, blocks, (0,))
        (partial,) = images(held, blocks, near, partial)
        if last:
            (own,) = call(
                pack_kernel, "pack", blocks, [shape_of((block.shape[0], held.shape[1]), BF16)], held=held
            )
            pieces = images(held, blocks, far, partial, tasks=tasks)
        else:
            panel, gram = images(held, blocks, far, partial, last=True)
    panel, *grams = left(swap(pieces, "task"), parts)
    square_shape = shape_of((size, size), F32)
    wide, lower, right_gram = call(
        right_first_kernel,
        "right_first",
        spread_over_tasks(own, tasks),
        [shape_of((size, held.shape[1]), BF16), square_shape, square_shape],
    )
    part = total(swap(grams, "row"), lower)
    state = call(right_second_kernel, "right_second", [right_gram], [square_shape] * 2)
    part = total(share(part, "task", tasks), state[0])
    right_side = call(right_third_kernel, "right_third", [right_gram, *state, lower], [square_shape])[0]
    return finish(share(part, "row", parts), panel, wide, lower, right_side)


def solution(mesh):
    tasks, parts = mesh.shape["task"], mesh.shape["row"]
    placed = (P("task", "row", None), P("task", None, None))
    return jax.shard_map(
        functools.partial(local, tasks, parts),
        mesh=mesh,
        in_specs=placed,
        out_specs=P(("row", "task"), None),
        check_vma=False,
    )
```

```python
import functools

import jax
import jax.numpy as jnp
from jax import lax
from jax.experimental import pallas as pl
from jax.experimental.pallas import tpu as pltpu
from jax.sharding import PartitionSpec as P

ITERS = 4
ROOT_STEPS = 12
LANES = 128
TILE = 8
F32 = jnp.float32
BF16 = jnp.bfloat16
ROWS_BY_ROWS = (((1,), (1,)), ((), ()))
VMEM_BYTES = 16 * 1024 * 1024
IN_VMEM = pl.BlockSpec(memory_space=pltpu.VMEM)
ANYWHERE = pl.BlockSpec(memory_space=pl.ANY)


def shape_of(shape, kind):
    return jax.ShapeDtypeStruct(shape, kind)


def call(kernel, name, operands, shapes, scratch=(), held=None, idle=(), flops=10**8):
    operands = [*operands, *idle]
    specs = [IN_VMEM] * (len(operands) - len(idle)) + [ANYWHERE] * len(idle)
    if held is not None:
        operands, specs = [held, *operands], [IN_VMEM, *specs]
    return pl.pallas_call(
        kernel,
        out_shape=tuple(shapes),
        in_specs=specs,
        out_specs=(IN_VMEM,) * len(shapes),
        scratch_shapes=list(scratch),
        cost_estimate=pl.CostEstimate(flops=flops, bytes_accessed=10**6, transcendentals=0),
        compiler_params=pltpu.CompilerParams(vmem_limit_bytes=VMEM_BYTES),
        name=name,
    )(*operands)


def split_two(value):
    high = value.astype(BF16)
    return high, (value - high.astype(F32)).astype(BF16)


def split_three(value):
    high = value.astype(BF16)
    rest = value - high.astype(F32)
    middle = rest.astype(BF16)
    return high, middle, (rest - middle.astype(F32)).astype(BF16)


def spread(value, order, axis):
    pieces = split_three(value)
    return jnp.concatenate([pieces[at] for at in order], axis=axis)


def square(left, right):
    return jnp.dot(
        spread(left, (0, 0, 1, 0, 2, 1), 1), spread(right, (0, 1, 0, 2, 0, 1), 0), preferred_element_type=F32
    )


def eye_of(size):
    return lax.broadcasted_iota(jnp.int32, (size, size), 0) == lax.broadcasted_iota(jnp.int32, (size, size), 1)


def tree_sum(values):
    while len(values) > 1:
        values = [values[at] + values[at + 1] for at in range(0, len(values), 2)]
    return values[0]


def lower_inverse(grams):
    size = grams[0].shape[0]
    tiles = size // TILE
    rows = lax.broadcasted_iota(jnp.int32, (TILE, LANES), 0)
    lanes = lax.broadcasted_iota(jnp.int32, (TILE, LANES), 1)
    columns, inverses, scales = [], [], []
    for gram in grams:
        wide = [jnp.broadcast_to(gram[:, at : at + 1], (size, LANES)) for at in range(size)]
        columns.append([[one[TILE * tile : TILE * (tile + 1)] for tile in range(tiles)] for one in wide])
        inverses.append([(rows + TILE * tile == lanes).astype(F32) for tile in range(tiles)])
        scales.append([jnp.zeros((TILE, LANES), F32) for _ in range(tiles)])
    for step in range(size):
        top, place = divmod(step, TILE)
        for cols, inverse, scale in zip(columns, inverses, scales):
            pivot = cols[step][top][place : place + 1]
            reciprocal = 1.0 / pivot
            ratio = [None] * top + [cols[step][tile] * reciprocal for tile in range(top, tiles)]
            for later in range(step + 1, size):
                first, inner = divmod(later, TILE)
                factor = ratio[first][inner : inner + 1]
                for tile in range(first, tiles):
                    cols[later][tile] = cols[later][tile] - cols[step][tile] * factor
            own = inverse[top][place : place + 1]
            for tile in range(top, tiles):
                factor = jnp.where(rows > place, ratio[tile], 0.0) if tile == top else ratio[tile]
                inverse[tile] = inverse[tile] - factor * own
            scale[top] = jnp.where(rows == place, lax.rsqrt(pivot), scale[top])
    return [
        jnp.concatenate([one * down for one, down in zip(inverse, scale)], axis=0)[:, :size]
        for inverse, scale in zip(inverses, scales)
    ]


def gram_pieces(images):
    return with_pieces(lax.dot_general(images, images, ROWS_BY_ROWS, preferred_element_type=F32))


def tall_of(rows, *sizes):
    return next(size for size in (*sizes, rows) if rows % size == 0)


def partner(axis, mask):
    return lax.bitwise_xor(lax.axis_index(axis).astype(jnp.int32), jnp.int32(mask))


def block_at(index, size):
    return pl.ds(pl.multiple_of(index * size, size), size)


def first_kernel(tall, d_ref, x_ref, out_ref, gram_ref, wide):
    wide[...] = x_ref[...].astype(BF16)

    def body(at, carry):
        span = block_at(at, tall)
        product = lax.dot_general(wide[...], d_ref[span, :], ROWS_BY_ROWS, preferred_element_type=F32)
        out_ref[:, span] = product.astype(BF16)
        return carry

    lax.fori_loop(0, d_ref.shape[0] // tall, body, 0)
    gram_ref[...] = gram_pieces(out_ref[...])


def first(held, start):
    rows, cols = held.shape
    rank = start.shape[0]
    return call(
        functools.partial(first_kernel, tall_of(rows, 512, 896, 256, 128)),
        "first",
        [start],
        [shape_of((rank, rows), BF16), shape_of((rank, LANES), BF16)],
        [pltpu.VMEM((rank, cols), BF16)],
        held=held,
        flops=2 * rows * cols * 384,
    )


def with_pieces(gram):
    rank = gram.shape[0]
    return jnp.concatenate([*split_three(gram), jnp.zeros((rank, LANES - 3 * rank), BF16)], axis=1)


def from_pieces(pieces):
    rank = pieces.shape[0]
    pieces = pieces.astype(F32)
    return pieces[:, :rank] + pieces[:, rank : 2 * rank] + pieces[:, 2 * rank : 3 * rank]


def backs_kernel(masks, d_ref, images_ref, gram_ref, *refs):
    out_ref = refs[-1]
    chunk = (out_ref.shape[1] - LANES) // len(masks)
    out_ref[:, :LANES] = gram_ref[...].astype(out_ref.dtype)
    for at, mask in enumerate(masks):
        span = block_at(partner("row", mask), chunk)
        out_ref[:, LANES + at * chunk : LANES + (at + 1) * chunk] = jnp.dot(
            images_ref[...], d_ref[:, span], preferred_element_type=F32
        ).astype(out_ref.dtype)


def backs(held, panel, gram, masks, parts, kind, *after):
    rows, cols = held.shape
    rank = panel.shape[0]
    return call(
        functools.partial(backs_kernel, masks),
        "backs",
        [panel, gram],
        [shape_of((rank, LANES + cols // parts * len(masks)), kind)],
        held=held,
        idle=after,
        flops=2 * rows * cols * 256 // parts * len(masks),
    )[0]


def combine_kernel(count, _, own_ref, in_ref, keep_ref, *out_refs):
    chunk = (own_ref.shape[1] - LANES) // count
    rank = own_ref.shape[0]
    gram = from_pieces(own_ref[:, :LANES]) + from_pieces(in_ref[:, :LANES])
    keep_ref[:, :rank] = gram
    pieces = with_pieces(gram)
    for at in range(count):
        span = slice(LANES + at * chunk, LANES + (at + 1) * chunk)
        total = own_ref[:, span] + in_ref[:, span].astype(F32)
        if at:
            out_refs[at - 1][:, :LANES] = pieces
            out_refs[at - 1][:, LANES:] = total.astype(BF16)
        else:
            keep_ref[:, LANES:] = total


def combine(held, own, received, count):
    rank, wide = own.shape
    shape = (rank, LANES + (wide - LANES) // count)
    keep, *pieces = call(
        functools.partial(combine_kernel, count),
        "combine",
        [own, received],
        [shape_of(shape, F32)] + [shape_of(shape, BF16)] * (count - 1),
        held=held,
    )
    return [keep, *pieces]


def settle_kernel(_, own_ref, *refs):
    *in_refs, out_ref = refs
    rank = own_ref.shape[0]
    gram = tree_sum([own_ref[:, :rank], *[from_pieces(ref[:, :LANES]) for ref in in_refs]])
    total = tree_sum([own_ref[:, LANES:], *[ref[:, LANES:].astype(F32) for ref in in_refs]])
    out_ref[...] = square(lower_inverse([gram])[0], total).astype(BF16)


def settle(held, pieces):
    rank, wide = pieces[0].shape
    return call(settle_kernel, "settle", pieces, [shape_of((rank, wide - LANES), BF16)], held=held)[0]


def images_kernel(masks, tall, partial, tasks, d_ref, x_ref, *refs):
    if partial:
        sum_ref, refs = refs[0], refs[1:]
    target = refs[1] if tasks else refs[0]
    chunk = x_ref.shape[1] // len(masks)
    for at in range(0, d_ref.shape[0], tall):
        product = sum_ref[:, at : at + tall] if partial else None
        for place, mask in enumerate(masks):
            term = lax.dot_general(
                x_ref[:, place * chunk : (place + 1) * chunk],
                d_ref[at : at + tall, block_at(partner("row", mask), chunk)],
                ROWS_BY_ROWS,
                preferred_element_type=F32,
            )
            product = term if product is None else product + term
        target[:, at : at + tall] = product.astype(target.dtype)
    if tasks:
        out_ref, flat = refs
        each = out_ref.shape[2]
        for at in range(tasks):
            out_ref[at] = flat[:, at * each : (at + 1) * each]
    elif len(refs) == 2:
        refs[1][...] = gram_pieces(refs[0][...])


def images(held, block, masks, parts, partial=None, last=False, tasks=0):
    rows, cols = held.shape
    rank = block.shape[0]
    scratch = ()
    if tasks:
        shapes = [shape_of((tasks, rank, rows // tasks), BF16)]
        scratch = [pltpu.VMEM((rank, rows), BF16)]
    elif last:
        shapes = [shape_of((rank, rows), BF16), shape_of((rank, LANES), BF16)]
    else:
        shapes = [shape_of((rank, rows), F32)]
    return call(
        functools.partial(images_kernel, masks, tall_of(rows, 512, 896, 256, 128), partial is not None, tasks),
        "images",
        [block] + ([] if partial is None else [partial]),
        shapes,
        scratch,
        held=held,
        flops=2 * rows * cols * 384 * len(masks) // parts,
    )


def join_kernel(first, *refs):
    in_refs, out_ref = refs[first : first + 2], refs[-1]
    if len(out_ref.shape) == 2:
        out_ref[...] = jnp.concatenate([ref[...] for ref in in_refs], axis=1)
    else:
        for at, ref in enumerate(in_refs):
            out_ref[at * ref.shape[0] : (at + 1) * ref.shape[0]] = ref[...]


def join(one, other, held=None, axis=0, after=()):
    shape = list(one.shape)
    shape[axis] *= 2
    kernel = functools.partial(join_kernel, 0 if held is None else 1)
    return call(kernel, "join", [one, other], [shape_of(tuple(shape), one.dtype)], held=held, idle=after)[0]


def pack_kernel(groups, _, *refs):
    *in_refs, out_ref = refs
    for masks, in_ref in zip(groups, in_refs):
        chunk = in_ref.shape[1] // len(masks)
        for place, mask in enumerate(masks):
            out_ref[0, :, block_at(partner("row", mask), chunk)] = in_ref[:, place * chunk : (place + 1) * chunk]


def left_kernel(groups, *refs):
    in_refs, (gram_ref, panel_ref, whole) = refs[: len(groups)], refs[-3:]
    tasks, rank, each = in_refs[0].shape[-3:]
    for masks, in_ref in zip(groups, in_refs):
        for place, mask in enumerate(masks):
            down = block_at(partner("task", mask), rank)
            for at in range(tasks):
                whole[down, at * each : (at + 1) * each] = in_ref[place, at]
            panel_ref[down, :] = in_ref[place, partner("task", 0)]
    gram_ref[...] = lax.dot_general(whole[...], whole[...], ROWS_BY_ROWS, preferred_element_type=F32)


def left(blocks, groups, after):
    _, tasks, rank, each = blocks[0].shape
    size = tasks * rank
    return call(
        functools.partial(left_kernel, groups),
        "left",
        blocks,
        [shape_of((size, size), F32), shape_of((size, each), BF16)],
        [pltpu.VMEM((size, tasks * each), BF16)],
        idle=[after],
    )


def add_kernel(one_ref, other_ref, *refs):
    refs[-1][...] = one_ref[...] + other_ref[...]


def add(one, other, *after):
    return call(add_kernel, "add", [one, other], [shape_of(one.shape, F32)], idle=after, flops=10**6)[0]


def root_begin(gram):
    return gram / jnp.sqrt(jnp.sum(gram * gram)), eye_of(gram.shape[0]).astype(F32)


def root_steps(state, count):
    identity = eye_of(state[0].shape[0]).astype(F32)

    def step(_, state):
        upper, lower = state
        middle = 0.5 * (3.0 * identity - square(lower, upper))
        return square(upper, middle), square(middle, lower)

    return lax.fori_loop(0, count, step, state)


def root_end(state, gram):
    return state[1] / jnp.sqrt(jnp.sqrt(jnp.sum(gram * gram)))


def right_first_kernel(groups, *refs):
    in_refs, (wide_ref, lower_ref, gram_ref) = refs[: len(groups)], refs[-3:]
    rank = in_refs[0].shape[1]
    for masks, in_ref in zip(groups, in_refs):
        for place, mask in enumerate(masks):
            wide_ref[block_at(partner("task", mask), rank), :] = in_ref[place]
    wide = wide_ref[...]
    raw = lax.dot_general(wide, wide, ROWS_BY_ROWS, preferred_element_type=F32)
    spans = [slice(task * rank, (task + 1) * rank) for task in range(wide.shape[0] // rank)]
    lower_ref[...] = jnp.zeros_like(lower_ref)
    for span, inverse in zip(spans, lower_inverse([raw[span, span] for span in spans])):
        lower_ref[span, span] = inverse
    lower = lower_ref[...]
    gram_ref[...] = square(square(lower, raw), lower.T)


def right_second_kernel(gram_ref, upper_ref, lower_ref):
    upper_ref[...], lower_ref[...] = root_steps(root_begin(gram_ref[...]), ROOT_STEPS // 2)


def right_third_kernel(gram_ref, upper_ref, lower_ref, change_ref, out_ref):
    state = root_steps((upper_ref[...], lower_ref[...]), ROOT_STEPS - ROOT_STEPS // 2)
    out_ref[...] = square(root_end(state, gram_ref[...]).T, change_ref[...])


def finish_kernel(one_ref, other_ref, panel_ref, wide_ref, lower_ref, right_ref, out_ref, side):
    size = lower_ref.shape[0]

    @pl.when(pl.program_id(0) == 0)
    def _():
        lower = lower_ref[...]
        gram = square(square(lower, one_ref[...] + other_ref[...]), lower.T)
        diagonal = jnp.where(eye_of(size), gram, 0.0)
        down = jnp.sqrt(jnp.sum(diagonal, axis=1, keepdims=True))
        across = jnp.sqrt(jnp.sum(diagonal, axis=0, keepdims=True))
        normed = gram / (down * across)
        mixing = root_end(root_steps(root_begin(normed), ROOT_STEPS), normed) / down * across
        mixed = square(square(lower.T, mixing), right_ref[...])
        panel = panel_ref[...].T
        product = jnp.dot(
            jnp.concatenate([panel, panel], axis=1),
            jnp.concatenate(split_two(mixed), axis=0),
            preferred_element_type=F32,
        )
        side[...] = jnp.concatenate(split_two(product), axis=1)

    wide = wide_ref[...]
    out_ref[...] = jnp.dot(
        side[...], jnp.concatenate([wide, wide], axis=0), preferred_element_type=F32
    ).astype(BF16)


def finish(one, other, panel, wide, lower, right_side):
    size, rows = panel.shape
    cols = wide.shape[1]
    across = 512

    def whole(array):
        return pl.BlockSpec(array.shape, lambda at: (0, 0))

    return pl.pallas_call(
        finish_kernel,
        out_shape=shape_of((rows, cols), BF16),
        grid=(cols // across,),
        in_specs=[
            whole(one),
            whole(other),
            whole(panel),
            pl.BlockSpec((size, across), lambda at: (0, at)),
            whole(lower),
            whole(right_side),
        ],
        out_specs=pl.BlockSpec((rows, across), lambda at: (0, at)),
        scratch_shapes=[pltpu.VMEM((rows, 2 * size), BF16)],
        compiler_params=pltpu.CompilerParams(vmem_limit_bytes=VMEM_BYTES),
        name="finish",
    )(one, other, panel, wide, lower, right_side)


def send(piece, axis, mask, count):
    return lax.ppermute(piece, axis, [(at, at ^ mask) for at in range(count)])


def gather(piece, axis, count, joining):
    masks, groups, blocks, block = [0], [(0,)], [piece], piece
    bit = count // 2
    while bit:
        received = send(block, axis, bit, count)
        groups.append(tuple(mask ^ bit for mask in masks))
        blocks.append(received)
        masks = masks + [mask ^ bit for mask in masks]
        bit //= 2
        if bit:
            block = joining(block, received)
    return groups, blocks


def local(tasks, parts, task_delta, start_block):
    held = pltpu.with_memory_space_constraint(task_delta[0], pltpu.VMEM)
    panel, gram = first(held, start_block[0].T)
    near = [0]
    bit = parts // 2
    while bit > 1:
        near = near + [mask ^ bit for mask in near]
        bit //= 2
    away = tuple(mask ^ 1 for mask in near)
    for step in range(ITERS):
        last = step == ITERS - 1
        there = backs(held, panel, gram, away, parts, BF16)
        here = backs(held, panel, gram, tuple(near), parts, F32, there)
        keep, *pieces = combine(held, here, send(there, "row", 1, parts), len(near))
        received = [send(piece, "row", mask, parts) for mask, piece in zip(near[1:], pieces)]
        block = settle(held, [keep, *received])
        groups, blocks = gather(block, "row", parts, lambda one, other: join(one, other, held, 1))
        partial = None
        for masks, block in zip(groups[:-1], blocks[:-1]):
            (partial,) = images(held, block, masks, parts, partial)
        if last:
            (own,) = call(
                functools.partial(pack_kernel, groups),
                "pack",
                blocks,
                [shape_of((1, block.shape[0], held.shape[1]), BF16)],
                held=held,
            )
            (panel,) = images(held, blocks[-1], groups[-1], parts, partial, tasks=tasks)
        else:
            panel, gram = images(held, blocks[-1], groups[-1], parts, partial, last=True)
    task_groups, bases = gather(own, "task", tasks, join)
    size = tasks * start_block.shape[2]
    square_shape = shape_of((size, size), F32)
    wide, lower, right_gram = call(
        functools.partial(right_first_kernel, task_groups),
        "right_first",
        bases,
        [shape_of((size, held.shape[1]), BF16), square_shape, square_shape],
    )
    state = call(right_second_kernel, "right_second", [right_gram], [square_shape] * 2)
    _, panels = gather(panel[None], "task", tasks, lambda one, other: join(one, other, after=[lower]))
    gram, panel = left(panels, task_groups, state[0])
    right_side = call(right_third_kernel, "right_third", [right_gram, *state, lower], [square_shape])[0]
    bit, after = parts // 2, [right_side]
    while bit > 1:
        gram, after = add(gram, send(gram, "row", bit, parts), *after), []
        bit //= 2
    return finish(gram, send(gram, "row", 1, parts), panel, wide, lower, right_side)


def solution(mesh):
    tasks, parts = mesh.shape["task"], mesh.shape["row"]
    placed = (P("task", "row", None), P("task", None, None))
    return jax.shard_map(
        functools.partial(local, tasks, parts),
        mesh=mesh,
        in_specs=placed,
        out_specs=P(("row", "task"), None),
        check_vma=False,
    )
```

```python
import functools

import jax
import jax.numpy as jnp
from jax import lax
from jax.experimental import pallas as pl
from jax.experimental.pallas import tpu as pltpu
from jax.sharding import PartitionSpec as P

ITERS = 4
ROOT_STEPS = 12
LANES = 128
TILE = 8
F32 = jnp.float32
BF16 = jnp.bfloat16
ROWS_BY_ROWS = (((1,), (1,)), ((), ()))
VMEM_BYTES = 16 * 1024 * 1024
IN_VMEM = pl.BlockSpec(memory_space=pltpu.VMEM)
ANYWHERE = pl.BlockSpec(memory_space=pl.ANY)


def shape_of(shape, kind):
    return jax.ShapeDtypeStruct(shape, kind)


def call(kernel, name, operands, shapes, scratch=(), held=None, idle=(), flops=10**8):
    operands = [*operands, *idle]
    specs = [IN_VMEM] * (len(operands) - len(idle)) + [ANYWHERE] * len(idle)
    if held is not None:
        operands, specs = [held, *operands], [IN_VMEM, *specs]
    return pl.pallas_call(
        kernel,
        out_shape=tuple(shapes),
        in_specs=specs,
        out_specs=(IN_VMEM,) * len(shapes),
        scratch_shapes=list(scratch),
        cost_estimate=pl.CostEstimate(flops=flops, bytes_accessed=10**6, transcendentals=0),
        compiler_params=pltpu.CompilerParams(vmem_limit_bytes=VMEM_BYTES),
        name=name,
    )(*operands)


def split_two(value):
    high = value.astype(BF16)
    return high, (value - high.astype(F32)).astype(BF16)


def split_three(value):
    high = value.astype(BF16)
    rest = value - high.astype(F32)
    middle = rest.astype(BF16)
    return high, middle, (rest - middle.astype(F32)).astype(BF16)


def spread(value, order, axis):
    pieces = split_three(value)
    return jnp.concatenate([pieces[at] for at in order], axis=axis)


def square(left, right):
    return jnp.dot(
        spread(left, (0, 0, 1, 0, 2, 1), 1), spread(right, (0, 1, 0, 2, 0, 1), 0), preferred_element_type=F32
    )


def eye_of(size):
    return lax.broadcasted_iota(jnp.int32, (size, size), 0) == lax.broadcasted_iota(jnp.int32, (size, size), 1)


def tree_sum(values):
    while len(values) > 1:
        values = [values[at] + values[at + 1] for at in range(0, len(values), 2)]
    return values[0]


def lower_inverse(grams):
    size = grams[0].shape[0]
    tiles = size // TILE
    rows = lax.broadcasted_iota(jnp.int32, (TILE, LANES), 0)
    lanes = lax.broadcasted_iota(jnp.int32, (TILE, LANES), 1)
    columns, inverses, scales = [], [], []
    for gram in grams:
        wide = [jnp.broadcast_to(gram[:, at : at + 1], (size, LANES)) for at in range(size)]
        columns.append([[one[TILE * tile : TILE * (tile + 1)] for tile in range(tiles)] for one in wide])
        inverses.append([(rows + TILE * tile == lanes).astype(F32) for tile in range(tiles)])
        scales.append([jnp.zeros((TILE, LANES), F32) for _ in range(tiles)])
    for step in range(size):
        top, place = divmod(step, TILE)
        for cols, inverse, scale in zip(columns, inverses, scales):
            pivot = cols[step][top][place : place + 1]
            reciprocal = 1.0 / pivot
            ratio = [None] * top + [cols[step][tile] * reciprocal for tile in range(top, tiles)]
            for later in range(step + 1, size):
                first, inner = divmod(later, TILE)
                factor = ratio[first][inner : inner + 1]
                for tile in range(first, tiles):
                    cols[later][tile] = cols[later][tile] - cols[step][tile] * factor
            own = inverse[top][place : place + 1]
            for tile in range(top, tiles):
                factor = jnp.where(rows > place, ratio[tile], 0.0) if tile == top else ratio[tile]
                inverse[tile] = inverse[tile] - factor * own
            scale[top] = jnp.where(rows == place, lax.rsqrt(pivot), scale[top])
    return [
        jnp.concatenate([one * down for one, down in zip(inverse, scale)], axis=0)[:, :size]
        for inverse, scale in zip(inverses, scales)
    ]


def gram_pieces(images):
    return with_pieces(lax.dot_general(images, images, ROWS_BY_ROWS, preferred_element_type=F32))


def tall_of(rows, *sizes):
    return next(size for size in (*sizes, rows) if rows % size == 0)


def partner(axis, mask):
    return lax.bitwise_xor(lax.axis_index(axis).astype(jnp.int32), jnp.int32(mask))


def block_at(index, size):
    return pl.ds(pl.multiple_of(index * size, size), size)


def sweep_kernel(masks, across, x_ref, d_ref, *refs):
    out_refs, (wide, total, gram) = refs[: len(masks)], refs[-3:]
    step = pl.program_id(0)
    chunk = out_refs[0].shape[1] - LANES
    cols = d_ref.shape[1]

    @pl.when(step == 0)
    def _():
        wide[...] = x_ref[...].astype(BF16)
        total[...] = jnp.zeros_like(total)
        gram[...] = jnp.zeros_like(gram)

    panel = lax.dot_general(wide[...], d_ref[...], ROWS_BY_ROWS, preferred_element_type=F32).astype(BF16)
    gram[...] += lax.dot_general(panel, panel, ROWS_BY_ROWS, preferred_element_type=F32)
    for at in range(0, cols, across):
        total[:, at : at + across] += jnp.dot(panel, d_ref[:, at : at + across], preferred_element_type=F32)

    @pl.when(step == pl.num_programs(0) - 1)
    def _():
        pieces = with_pieces(gram[...])
        for mask, out_ref in zip(masks, out_refs):
            out_ref[:, :LANES] = pieces.astype(out_ref.dtype)
            out_ref[:, LANES:] = total[:, block_at(lax.div(partner("row", mask), 2), chunk)].astype(out_ref.dtype)


def sweep(delta, start, masks, parts):
    rows, cols = delta.shape
    rank = start.shape[0]
    tall = tall_of(rows, 256, 128)
    shape = (rank, LANES + cols // len(masks))
    kinds = [BF16] * (len(masks) - 1) + [F32]
    return pl.pallas_call(
        functools.partial(sweep_kernel, masks, tall_of(cols, 1024)),
        out_shape=tuple(shape_of(shape, kind) for kind in kinds),
        grid=(rows // tall,),
        in_specs=[
            pl.BlockSpec((rank, cols), lambda at: (0, 0)),
            pl.BlockSpec((tall, cols), lambda at: (at, 0)),
        ],
        out_specs=tuple(pl.BlockSpec(shape, lambda at: (0, 0)) for _ in masks),
        scratch_shapes=[pltpu.VMEM((rank, cols), BF16), pltpu.VMEM((rank, cols), F32), pltpu.VMEM((rank, rank), F32)],
        cost_estimate=pl.CostEstimate(
            flops=4 * rows * cols * 300, bytes_accessed=2 * rows * cols, transcendentals=0
        ),
        compiler_params=pltpu.CompilerParams(vmem_limit_bytes=VMEM_BYTES),
        name="sweep",
    )(start, delta)


def with_pieces(gram):
    rank = gram.shape[0]
    return jnp.concatenate([*split_three(gram), jnp.zeros((rank, LANES - 3 * rank), BF16)], axis=1)


def from_pieces(pieces):
    rank = pieces.shape[0]
    pieces = pieces.astype(F32)
    return pieces[:, :rank] + pieces[:, rank : 2 * rank] + pieces[:, 2 * rank : 3 * rank]


def backs_kernel(mask, d_ref, images_ref, gram_ref, *refs):
    out_ref = refs[-1]
    chunk = out_ref.shape[1] - LANES
    across = tall_of(chunk, 512)
    out_ref[:, :LANES] = gram_ref[...].astype(out_ref.dtype)
    for at in range(0, chunk, across):
        span = block_at(lax.div(partner("row", mask), 2) * (chunk // across) + at // across, across)
        out_ref[:, LANES + at : LANES + at + across] = jnp.dot(
            images_ref[...], d_ref[:, span], preferred_element_type=F32
        ).astype(out_ref.dtype)


def backs(held, panel, gram, mask, count, *after):
    rows, cols = held.shape
    rank = panel.shape[0]
    return call(
        functools.partial(backs_kernel, mask),
        "backs",
        [panel, gram],
        [shape_of((rank, LANES + cols // count), BF16 if mask else F32)],
        held=held,
        idle=after,
        flops=2 * rows * cols * 256 // count,
    )[0]


def combine_kernel(first, *refs):
    *in_refs, out_ref = refs[first:]
    gram = tree_sum([from_pieces(ref[:, :LANES]) for ref in in_refs])
    out_ref[:, :LANES] = with_pieces(gram)
    out_ref[:, LANES:] = tree_sum([ref[:, LANES:].astype(F32) for ref in in_refs]).astype(BF16)


def settle_kernel(*refs):
    one_ref, other_ref, out_ref = refs[-3:]
    rank = one_ref.shape[0]
    gram = from_pieces(one_ref[:, :LANES]) + from_pieces(other_ref[:, :LANES])
    total = one_ref[:, LANES:].astype(F32) + other_ref[:, LANES:].astype(F32)
    out_ref[...] = square(lower_inverse([gram])[0], total).astype(BF16)


def combine(held, pieces):
    kernel = functools.partial(combine_kernel, 0 if held is None else 1)
    return call(kernel, "combine", pieces, [shape_of(pieces[0].shape, BF16)], held=held)[0]


def settle(held, one, other):
    rank, wide = one.shape
    return call(settle_kernel, "settle", [one, other], [shape_of((rank, wide - LANES), BF16)], held=held)[0]


def images_kernel(masks, tall, partial, tasks, d_ref, *refs):
    x_refs, refs = refs[: len(masks)], refs[len(masks) :]
    if partial:
        sum_ref, refs = refs[0], refs[1:]
    target = refs[1] if tasks else refs[0]
    chunk = x_refs[0].shape[1]
    for at in range(0, d_ref.shape[0], tall):
        product = sum_ref[:, at : at + tall] if partial else None
        for mask, x_ref in zip(masks, x_refs):
            span = block_at(lax.div(partner("row", mask), 2), chunk)
            term = lax.dot_general(
                x_ref[...], d_ref[at : at + tall, span], ROWS_BY_ROWS, preferred_element_type=F32
            )
            product = term if product is None else product + term
        target[:, at : at + tall] = product.astype(target.dtype)
    if tasks:
        out_ref, flat = refs
        each = out_ref.shape[2]
        for at in range(tasks):
            out_ref[at] = flat[:, at * each : (at + 1) * each]
    elif len(refs) == 2:
        refs[1][...] = gram_pieces(refs[0][...])


def images(held, blocks, masks, partial=None, last=False, tasks=0):
    rows, cols = held.shape
    rank, chunk = blocks[0].shape
    scratch = ()
    if tasks:
        shapes = [shape_of((tasks, rank, rows // tasks), BF16)]
        scratch = [pltpu.VMEM((rank, rows), BF16)]
    elif last:
        shapes = [shape_of((rank, rows), BF16), shape_of((rank, LANES), BF16)]
    else:
        shapes = [shape_of((rank, rows), F32)]
    return call(
        functools.partial(images_kernel, masks, tall_of(rows, 512, 896, 256, 128), partial is not None, tasks),
        "images",
        [*blocks] + ([] if partial is None else [partial]),
        shapes,
        scratch,
        held=held,
        flops=2 * rows * chunk * 384 * len(masks),
    )


def join_kernel(first, *refs):
    in_refs, out_ref = refs[first : first + 2], refs[-1]
    if len(out_ref.shape) == 2:
        out_ref[...] = jnp.concatenate([ref[...] for ref in in_refs], axis=1)
    else:
        for at, ref in enumerate(in_refs):
            out_ref[at * ref.shape[0] : (at + 1) * ref.shape[0]] = ref[...]


def join(one, other, held=None, axis=0, after=()):
    shape = list(one.shape)
    shape[axis] *= 2
    kernel = functools.partial(join_kernel, 0 if held is None else 1)
    return call(kernel, "join", [one, other], [shape_of(tuple(shape), one.dtype)], held=held, idle=after)[0]


def pack_kernel(masks, _, *refs):
    *in_refs, out_ref = refs
    chunk = in_refs[0].shape[1]
    for mask, in_ref in zip(masks, in_refs):
        out_ref[0, :, block_at(lax.div(partner("row", mask), 2), chunk)] = in_ref[...]


def left_kernel(groups, *refs):
    in_refs, (gram_ref, panel_ref, whole) = refs[: len(groups)], refs[-3:]
    tasks, rank, each = in_refs[0].shape[-3:]
    for masks, in_ref in zip(groups, in_refs):
        for place, mask in enumerate(masks):
            down = block_at(partner("task", mask), rank)
            for at in range(tasks):
                whole[down, at * each : (at + 1) * each] = in_ref[place, at]
            panel_ref[down, :] = in_ref[place, partner("task", 0)]
    gram_ref[...] = lax.dot_general(whole[...], whole[...], ROWS_BY_ROWS, preferred_element_type=F32)


def left(blocks, groups, after):
    _, tasks, rank, each = blocks[0].shape
    size = tasks * rank
    return call(
        functools.partial(left_kernel, groups),
        "left",
        blocks,
        [shape_of((size, size), F32), shape_of((size, each), BF16)],
        [pltpu.VMEM((size, tasks * each), BF16)],
        idle=[after],
    )


def add_kernel(one_ref, other_ref, *refs):
    refs[-1][...] = one_ref[...] + other_ref[...]


def add(one, other, *after):
    return call(add_kernel, "add", [one, other], [shape_of(one.shape, F32)], idle=after, flops=10**6)[0]


def root_begin(gram):
    return gram / jnp.sqrt(jnp.sum(gram * gram)), eye_of(gram.shape[0]).astype(F32)


def root_steps(state, count):
    identity = eye_of(state[0].shape[0]).astype(F32)

    def step(_, state):
        upper, lower = state
        middle = 0.5 * (3.0 * identity - square(lower, upper))
        return square(upper, middle), square(middle, lower)

    return lax.fori_loop(0, count, step, state)


def root_end(state, gram):
    return state[1] / jnp.sqrt(jnp.sqrt(jnp.sum(gram * gram)))


def right_first_kernel(groups, *refs):
    in_refs, (wide_ref, lower_ref, gram_ref) = refs[: len(groups)], refs[-3:]
    rank = in_refs[0].shape[1]
    for masks, in_ref in zip(groups, in_refs):
        for place, mask in enumerate(masks):
            wide_ref[block_at(partner("task", mask), rank), :] = in_ref[place]
    wide = wide_ref[...]
    raw = lax.dot_general(wide, wide, ROWS_BY_ROWS, preferred_element_type=F32)
    spans = [slice(task * rank, (task + 1) * rank) for task in range(wide.shape[0] // rank)]
    lower_ref[...] = jnp.zeros_like(lower_ref)
    for span, inverse in zip(spans, lower_inverse([raw[span, span] for span in spans])):
        lower_ref[span, span] = inverse
    lower = lower_ref[...]
    gram_ref[...] = square(square(lower, raw), lower.T)


def right_second_kernel(gram_ref, upper_ref, lower_ref):
    upper_ref[...], lower_ref[...] = root_steps(root_begin(gram_ref[...]), ROOT_STEPS // 2)


def right_third_kernel(gram_ref, upper_ref, lower_ref, change_ref, out_ref):
    state = root_steps((upper_ref[...], lower_ref[...]), ROOT_STEPS - ROOT_STEPS // 2)
    out_ref[...] = square(root_end(state, gram_ref[...]).T, change_ref[...])


def finish_kernel(one_ref, other_ref, panel_ref, wide_ref, lower_ref, right_ref, out_ref, side):
    size = lower_ref.shape[0]

    @pl.when(pl.program_id(0) == 0)
    def _():
        lower = lower_ref[...]
        gram = square(square(lower, one_ref[...] + other_ref[...]), lower.T)
        diagonal = jnp.where(eye_of(size), gram, 0.0)
        down = jnp.sqrt(jnp.sum(diagonal, axis=1, keepdims=True))
        across = jnp.sqrt(jnp.sum(diagonal, axis=0, keepdims=True))
        normed = gram / (down * across)
        mixing = root_end(root_steps(root_begin(normed), ROOT_STEPS), normed) / down * across
        mixed = square(square(lower.T, mixing), right_ref[...])
        panel = panel_ref[...].T
        product = jnp.dot(
            jnp.concatenate([panel, panel], axis=1),
            jnp.concatenate(split_two(mixed), axis=0),
            preferred_element_type=F32,
        )
        side[...] = jnp.concatenate(split_two(product), axis=1)

    wide = wide_ref[...]
    out_ref[...] = jnp.dot(
        side[...], jnp.concatenate([wide, wide], axis=0), preferred_element_type=F32
    ).astype(BF16)


def finish(one, other, panel, wide, lower, right_side):
    size, rows = panel.shape
    cols = wide.shape[1]
    across = 512

    def whole(array):
        return pl.BlockSpec(array.shape, lambda at: (0, 0))

    return pl.pallas_call(
        finish_kernel,
        out_shape=shape_of((rows, cols), BF16),
        grid=(cols // across,),
        in_specs=[
            whole(one),
            whole(other),
            whole(panel),
            pl.BlockSpec((size, across), lambda at: (0, at)),
            whole(lower),
            whole(right_side),
        ],
        out_specs=pl.BlockSpec((rows, across), lambda at: (0, at)),
        scratch_shapes=[pltpu.VMEM((rows, 2 * size), BF16)],
        compiler_params=pltpu.CompilerParams(vmem_limit_bytes=VMEM_BYTES),
        name="finish",
    )(one, other, panel, wide, lower, right_side)


def send(piece, axis, mask, count):
    return lax.ppermute(piece, axis, [(at, at ^ mask) for at in range(count)])


def gather(piece, axis, count, joining):
    masks, groups, blocks, block = [0], [(0,)], [piece], piece
    bit = count // 2
    while bit:
        received = send(block, axis, bit, count)
        groups.append(tuple(mask ^ bit for mask in masks))
        blocks.append(received)
        masks = masks + [mask ^ bit for mask in masks]
        bit //= 2
        if bit:
            block = joining(block, received)
    return groups, blocks


def local(tasks, parts, task_delta, start_block):
    masks = tuple(range(0, parts, 2))
    nearest, farther = masks[1], masks[2:]
    count = len(masks)
    order = (*reversed(masks[1:]), 0)
    *pieces, keep = sweep(
        pltpu.with_memory_space_constraint(task_delta[0], pltpu.HBM), start_block[0].T, order, parts
    )
    held = pltpu.with_memory_space_constraint(task_delta[0], pltpu.VMEM)
    for step in range(ITERS):
        last = step == ITERS - 1
        if step:
            pieces, after = [], []
            for mask in order:
                pieces.append(backs(held, panel, gram, mask, count, *after))
                after = pieces[-1:]
            *pieces, keep = pieces
        received = {mask: send(piece, "row", mask, parts) for mask, piece in zip(order, pieces)}
        beside = held if step else None
        sums = combine(beside, [keep, *[received[mask] for mask in masks[1:]]])
        block = settle(beside, sums, send(sums, "row", 1, parts))
        blocks = {mask: send(block, "row", mask, parts) for mask in order[:-1]}
        blocks[0] = block
        (partial,) = images(held, [block], (0,))
        (partial,) = images(held, [blocks[nearest]], (nearest,), partial)
        rest = [blocks[mask] for mask in farther]
        if last:
            (own,) = call(
                functools.partial(pack_kernel, masks),
                "pack",
                [blocks[mask] for mask in masks],
                [shape_of((1, block.shape[0], held.shape[1]), BF16)],
                held=held,
            )
            (panel,) = images(held, rest, farther, partial, tasks=tasks)
        else:
            panel, gram = images(held, rest, farther, partial, last=True)
    task_groups, bases = gather(own, "task", tasks, lambda one, other: join(one, other, after=[panel]))
    size = tasks * start_block.shape[2]
    square_shape = shape_of((size, size), F32)
    wide, lower, right_gram = call(
        functools.partial(right_first_kernel, task_groups),
        "right_first",
        bases,
        [shape_of((size, held.shape[1]), BF16), square_shape, square_shape],
    )
    state = call(right_second_kernel, "right_second", [right_gram], [square_shape] * 2)
    _, panels = gather(panel[None], "task", tasks, lambda one, other: join(one, other, after=[lower]))
    gram, panel = left(panels, task_groups, state[0])
    right_side = call(right_third_kernel, "right_third", [right_gram, *state, lower], [square_shape])[0]
    bit, after = parts // 2, [right_side]
    while bit > 1:
        gram, after = add(gram, send(gram, "row", bit, parts), *after), []
        bit //= 2
    return finish(gram, send(gram, "row", 1, parts), panel, wide, lower, right_side)


def solution(mesh):
    tasks, parts = mesh.shape["task"], mesh.shape["row"]
    placed = (P("task", "row", None), P("task", None, None))
    return jax.shard_map(
        functools.partial(local, tasks, parts),
        mesh=mesh,
        in_specs=placed,
        out_specs=P(("row", "task"), None),
        check_vma=False,
    )
```

```python
import functools

import jax
import jax.numpy as jnp
from jax import lax
from jax.experimental import pallas as pl
from jax.experimental.pallas import tpu as pltpu
from jax.sharding import PartitionSpec as P

ITERS = 4
ROOT_STEPS = 12
LANES = 128
TILE = 8
F32 = jnp.float32
BF16 = jnp.bfloat16
ROWS_BY_ROWS = (((1,), (1,)), ((), ()))
VMEM_BYTES = 16 * 1024 * 1024
IN_VMEM = pl.BlockSpec(memory_space=pltpu.VMEM)
ANYWHERE = pl.BlockSpec(memory_space=pl.ANY)


def shape_of(shape, kind):
    return jax.ShapeDtypeStruct(shape, kind)


def call(kernel, name, operands, shapes, scratch=(), held=None, idle=(), flops=10**8):
    operands = [*operands, *idle]
    specs = [IN_VMEM] * (len(operands) - len(idle)) + [ANYWHERE] * len(idle)
    if held is not None:
        operands, specs = [held, *operands], [IN_VMEM, *specs]
    return pl.pallas_call(
        kernel,
        out_shape=tuple(shapes),
        in_specs=specs,
        out_specs=(IN_VMEM,) * len(shapes),
        scratch_shapes=list(scratch),
        cost_estimate=pl.CostEstimate(flops=flops, bytes_accessed=10**6, transcendentals=0),
        compiler_params=pltpu.CompilerParams(vmem_limit_bytes=VMEM_BYTES),
        name=name,
    )(*operands)


def split_two(value):
    high = value.astype(BF16)
    return high, (value - high.astype(F32)).astype(BF16)


def split_three(value):
    high = value.astype(BF16)
    rest = value - high.astype(F32)
    middle = rest.astype(BF16)
    return high, middle, (rest - middle.astype(F32)).astype(BF16)


def spread(value, order, axis):
    pieces = split_three(value)
    return jnp.concatenate([pieces[at] for at in order], axis=axis)


def square(left, right):
    return jnp.dot(
        spread(left, (0, 0, 1, 0, 2, 1), 1), spread(right, (0, 1, 0, 2, 0, 1), 0), preferred_element_type=F32
    )


def eye_of(size):
    return lax.broadcasted_iota(jnp.int32, (size, size), 0) == lax.broadcasted_iota(jnp.int32, (size, size), 1)


def tree_sum(values):
    while len(values) > 1:
        values = [values[at] + values[at + 1] for at in range(0, len(values), 2)]
    return values[0]


def lower_inverse(grams):
    size = grams[0].shape[0]
    tiles = size // TILE
    rows = lax.broadcasted_iota(jnp.int32, (TILE, LANES), 0)
    lanes = lax.broadcasted_iota(jnp.int32, (TILE, LANES), 1)
    columns, inverses, scales = [], [], []
    for gram in grams:
        wide = [jnp.broadcast_to(gram[:, at : at + 1], (size, LANES)) for at in range(size)]
        columns.append([[one[TILE * tile : TILE * (tile + 1)] for tile in range(tiles)] for one in wide])
        inverses.append([(rows + TILE * tile == lanes).astype(F32) for tile in range(tiles)])
        scales.append([jnp.zeros((TILE, LANES), F32) for _ in range(tiles)])
    for step in range(size):
        top, place = divmod(step, TILE)
        for cols, inverse, scale in zip(columns, inverses, scales):
            pivot = cols[step][top][place : place + 1]
            reciprocal = 1.0 / pivot
            ratio = [None] * top + [cols[step][tile] * reciprocal for tile in range(top, tiles)]
            for later in range(step + 1, size):
                first, inner = divmod(later, TILE)
                factor = ratio[first][inner : inner + 1]
                for tile in range(first, tiles):
                    cols[later][tile] = cols[later][tile] - cols[step][tile] * factor
            own = inverse[top][place : place + 1]
            for tile in range(top, tiles):
                factor = jnp.where(rows > place, ratio[tile], 0.0) if tile == top else ratio[tile]
                inverse[tile] = inverse[tile] - factor * own
            scale[top] = jnp.where(rows == place, lax.rsqrt(pivot), scale[top])
    return [
        jnp.concatenate([one * down for one, down in zip(inverse, scale)], axis=0)[:, :size]
        for inverse, scale in zip(inverses, scales)
    ]


def gram_pieces(images):
    return with_pieces(lax.dot_general(images, images, ROWS_BY_ROWS, preferred_element_type=F32))


def tall_of(rows, *sizes):
    return next(size for size in (*sizes, rows) if rows % size == 0)


def partner(axis, mask):
    return lax.bitwise_xor(lax.axis_index(axis).astype(jnp.int32), jnp.int32(mask))


def block_at(index, size):
    return pl.ds(pl.multiple_of(index * size, size), size)


def first_kernel(tall, d_ref, x_ref, out_ref, gram_ref, wide):
    wide[...] = x_ref[...].astype(BF16)
    for at in range(0, d_ref.shape[0], tall):
        product = lax.dot_general(wide[...], d_ref[at : at + tall, :], ROWS_BY_ROWS, preferred_element_type=F32)
        out_ref[:, at : at + tall] = product.astype(BF16)
    gram_ref[...] = gram_pieces(out_ref[...])


def first(held, start):
    rows, cols = held.shape
    rank = start.shape[0]
    return call(
        functools.partial(first_kernel, tall_of(rows, 512, 896, 256, 128)),
        "first",
        [start],
        [shape_of((rank, rows), BF16), shape_of((rank, LANES), BF16)],
        [pltpu.VMEM((rank, cols), BF16)],
        held=held,
        flops=2 * rows * cols * 384,
    )


def with_pieces(gram):
    rank = gram.shape[0]
    return jnp.concatenate([*split_three(gram), jnp.zeros((rank, LANES - 3 * rank), BF16)], axis=1)


def from_pieces(pieces):
    rank = pieces.shape[0]
    pieces = pieces.astype(F32)
    return pieces[:, :rank] + pieces[:, rank : 2 * rank] + pieces[:, 2 * rank : 3 * rank]


def backs_kernel(mask, d_ref, images_ref, gram_ref, *refs):
    out_ref = refs[-1]
    chunk = out_ref.shape[1] - LANES
    across = tall_of(chunk, 512)
    out_ref[:, :LANES] = gram_ref[...].astype(out_ref.dtype)
    for at in range(0, chunk, across):
        span = block_at(lax.div(partner("row", mask), 2) * (chunk // across) + at // across, across)
        out_ref[:, LANES + at : LANES + at + across] = jnp.dot(
            images_ref[...], d_ref[:, span], preferred_element_type=F32
        ).astype(out_ref.dtype)


def backs(held, panel, gram, mask, count, *after):
    rows, cols = held.shape
    rank = panel.shape[0]
    return call(
        functools.partial(backs_kernel, mask),
        "backs",
        [panel, gram],
        [shape_of((rank, LANES + cols // count), BF16 if mask else F32)],
        held=held,
        idle=after,
        flops=10**6,
    )[0]


def combine_kernel(_, *refs):
    *in_refs, out_ref = refs
    gram = tree_sum([from_pieces(ref[:, :LANES]) for ref in in_refs])
    out_ref[:, :LANES] = with_pieces(gram)
    out_ref[:, LANES:] = tree_sum([ref[:, LANES:].astype(F32) for ref in in_refs]).astype(BF16)


def settle_kernel(_, one_ref, other_ref, out_ref):
    rank = one_ref.shape[0]
    gram = from_pieces(one_ref[:, :LANES]) + from_pieces(other_ref[:, :LANES])
    total = one_ref[:, LANES:].astype(F32) + other_ref[:, LANES:].astype(F32)
    out_ref[...] = square(lower_inverse([gram])[0], total).astype(BF16)


def combine(held, pieces):
    return call(combine_kernel, "combine", pieces, [shape_of(pieces[0].shape, BF16)], held=held)[0]


def settle(held, one, other):
    rank, wide = one.shape
    return call(settle_kernel, "settle", [one, other], [shape_of((rank, wide - LANES), BF16)], held=held)[0]


def images_kernel(masks, tall, partial, tasks, d_ref, *refs):
    x_refs, refs = refs[: len(masks)], refs[len(masks) :]
    if partial:
        sum_ref, refs = refs[0], refs[1:]
    target = refs[1] if tasks else refs[0]
    chunk = x_refs[0].shape[1]
    for at in range(0, d_ref.shape[0], tall):
        product = sum_ref[:, at : at + tall] if partial else None
        for mask, x_ref in zip(masks, x_refs):
            span = block_at(lax.div(partner("row", mask), 2), chunk)
            term = lax.dot_general(
                x_ref[...], d_ref[at : at + tall, span], ROWS_BY_ROWS, preferred_element_type=F32
            )
            product = term if product is None else product + term
        target[:, at : at + tall] = product.astype(target.dtype)
    if tasks:
        out_ref, flat = refs
        each = out_ref.shape[2]
        for at in range(tasks):
            out_ref[at] = flat[:, at * each : (at + 1) * each]
    elif len(refs) == 2:
        refs[1][...] = gram_pieces(refs[0][...])


def images(held, blocks, masks, partial=None, last=False, tasks=0):
    rows, cols = held.shape
    rank, chunk = blocks[0].shape
    scratch = ()
    if tasks:
        shapes = [shape_of((tasks, rank, rows // tasks), BF16)]
        scratch = [pltpu.VMEM((rank, rows), BF16)]
    elif last:
        shapes = [shape_of((rank, rows), BF16), shape_of((rank, LANES), BF16)]
    else:
        shapes = [shape_of((rank, rows), F32)]
    return call(
        functools.partial(images_kernel, masks, tall_of(rows, 512, 896, 256, 128), partial is not None, tasks),
        "images",
        [*blocks] + ([] if partial is None else [partial]),
        shapes,
        scratch,
        held=held,
        flops=2 * rows * chunk * 384 * len(masks),
    )


def join_kernel(first, *refs):
    in_refs, out_ref = refs[first : first + 2], refs[-1]
    if len(out_ref.shape) == 2:
        out_ref[...] = jnp.concatenate([ref[...] for ref in in_refs], axis=1)
    else:
        for at, ref in enumerate(in_refs):
            out_ref[at * ref.shape[0] : (at + 1) * ref.shape[0]] = ref[...]


def join(one, other, held=None, axis=0, after=()):
    shape = list(one.shape)
    shape[axis] *= 2
    kernel = functools.partial(join_kernel, 0 if held is None else 1)
    return call(kernel, "join", [one, other], [shape_of(tuple(shape), one.dtype)], held=held, idle=after)[0]


def pack_kernel(masks, _, *refs):
    *in_refs, out_ref = refs
    chunk = in_refs[0].shape[1]
    for mask, in_ref in zip(masks, in_refs):
        out_ref[0, :, block_at(lax.div(partner("row", mask), 2), chunk)] = in_ref[...]


def left_kernel(groups, *refs):
    in_refs, (gram_ref, panel_ref, whole) = refs[: len(groups)], refs[-3:]
    tasks, rank, each = in_refs[0].shape[-3:]
    for masks, in_ref in zip(groups, in_refs):
        for place, mask in enumerate(masks):
            down = block_at(partner("task", mask), rank)
            for at in range(tasks):
                whole[down, at * each : (at + 1) * each] = in_ref[place, at]
            panel_ref[down, :] = in_ref[place, partner("task", 0)]
    gram_ref[...] = lax.dot_general(whole[...], whole[...], ROWS_BY_ROWS, preferred_element_type=F32)


def left(blocks, groups, after):
    _, tasks, rank, each = blocks[0].shape
    size = tasks * rank
    return call(
        functools.partial(left_kernel, groups),
        "left",
        blocks,
        [shape_of((size, size), F32), shape_of((size, each), BF16)],
        [pltpu.VMEM((size, tasks * each), BF16)],
        idle=[after],
    )


def add_kernel(one_ref, other_ref, *refs):
    refs[-1][...] = one_ref[...] + other_ref[...]


def add(one, other, *after):
    return call(add_kernel, "add", [one, other], [shape_of(one.shape, F32)], idle=after, flops=10**6)[0]


def root_begin(gram):
    return gram / jnp.sqrt(jnp.sum(gram * gram)), eye_of(gram.shape[0]).astype(F32)


def root_steps(state, count):
    identity = eye_of(state[0].shape[0]).astype(F32)

    def step(_, state):
        upper, lower = state
        middle = 0.5 * (3.0 * identity - square(lower, upper))
        both = square(jnp.concatenate([upper, lower], axis=0), middle)
        return both[: identity.shape[0]], both[identity.shape[0] :]

    return lax.fori_loop(0, count, step, state)


def root_end(state, gram):
    return state[1] / jnp.sqrt(jnp.sqrt(jnp.sum(gram * gram)))


def right_first_kernel(groups, *refs):
    in_refs, (wide_ref, lower_ref, gram_ref) = refs[: len(groups)], refs[-3:]
    rank = in_refs[0].shape[1]
    for masks, in_ref in zip(groups, in_refs):
        for place, mask in enumerate(masks):
            wide_ref[block_at(partner("task", mask), rank), :] = in_ref[place]
    wide = wide_ref[...]
    raw = lax.dot_general(wide, wide, ROWS_BY_ROWS, preferred_element_type=F32)
    spans = [slice(task * rank, (task + 1) * rank) for task in range(wide.shape[0] // rank)]
    lower_ref[...] = jnp.zeros_like(lower_ref)
    for span, inverse in zip(spans, lower_inverse([raw[span, span] for span in spans])):
        lower_ref[span, span] = inverse
    lower = lower_ref[...]
    gram_ref[...] = square(square(lower, raw), lower.T)


def right_second_kernel(gram_ref, upper_ref, lower_ref):
    upper_ref[...], lower_ref[...] = root_steps(root_begin(gram_ref[...]), ROOT_STEPS // 2)


def right_third_kernel(gram_ref, upper_ref, lower_ref, change_ref, out_ref):
    state = root_steps((upper_ref[...], lower_ref[...]), ROOT_STEPS - ROOT_STEPS // 2)
    out_ref[...] = square(root_end(state, gram_ref[...]).T, change_ref[...])


def finish_kernel(one_ref, other_ref, panel_ref, wide_ref, lower_ref, right_ref, out_ref, side):
    size = lower_ref.shape[0]

    @pl.when(pl.program_id(0) == 0)
    def _():
        lower = lower_ref[...]
        gram = square(square(lower, one_ref[...] + other_ref[...]), lower.T)
        diagonal = jnp.where(eye_of(size), gram, 0.0)
        down = jnp.sqrt(jnp.sum(diagonal, axis=1, keepdims=True))
        across = jnp.sqrt(jnp.sum(diagonal, axis=0, keepdims=True))
        normed = gram / (down * across)
        mixing = root_end(root_steps(root_begin(normed), ROOT_STEPS), normed) / down * across
        mixed = square(square(lower.T, mixing), right_ref[...])
        panel = panel_ref[...].T
        product = jnp.dot(
            jnp.concatenate([panel, panel], axis=1),
            jnp.concatenate(split_two(mixed), axis=0),
            preferred_element_type=F32,
        )
        side[...] = jnp.concatenate(split_two(product), axis=1)

    wide = wide_ref[...]
    out_ref[...] = jnp.dot(
        side[...], jnp.concatenate([wide, wide], axis=0), preferred_element_type=F32
    ).astype(BF16)


def finish(one, other, panel, wide, lower, right_side):
    size, rows = panel.shape
    cols = wide.shape[1]
    across = 512

    def whole(array):
        return pl.BlockSpec(array.shape, lambda at: (0, 0))

    return pl.pallas_call(
        finish_kernel,
        out_shape=shape_of((rows, cols), BF16),
        grid=(cols // across,),
        in_specs=[
            whole(one),
            whole(other),
            whole(panel),
            pl.BlockSpec((size, across), lambda at: (0, at)),
            whole(lower),
            whole(right_side),
        ],
        out_specs=pl.BlockSpec((rows, across), lambda at: (0, at)),
        scratch_shapes=[pltpu.VMEM((rows, 2 * size), BF16)],
        compiler_params=pltpu.CompilerParams(vmem_limit_bytes=VMEM_BYTES),
        name="finish",
    )(one, other, panel, wide, lower, right_side)


def send(piece, axis, mask, count):
    return lax.ppermute(piece, axis, [(at, at ^ mask) for at in range(count)])


def gather(piece, axis, count, joining):
    masks, groups, blocks, block = [0], [(0,)], [piece], piece
    bit = count // 2
    while bit:
        received = send(block, axis, bit, count)
        groups.append(tuple(mask ^ bit for mask in masks))
        blocks.append(received)
        masks = masks + [mask ^ bit for mask in masks]
        bit //= 2
        if bit:
            block = joining(block, received)
    return groups, blocks


def local(tasks, parts, task_delta, start_block):
    masks = tuple(range(0, parts, 2))
    nearest, farther = masks[1], masks[2:]
    count = len(masks)
    order = (*reversed(masks[1:]), 0)
    held = pltpu.with_memory_space_constraint(task_delta[0], pltpu.VMEM)
    panel, gram = first(held, start_block[0].T)
    for step in range(ITERS):
        last = step == ITERS - 1
        received, after = {}, []
        for mask in order[:-1]:
            piece = backs(held, panel, gram, mask, count, *after)
            received[mask] = send(piece, "row", mask, parts)
            after = [piece]
        keep = backs(held, panel, gram, 0, count, *after, received[order[0]])
        sums = combine(held, [keep, *[received[mask] for mask in masks[1:]]])
        block = settle(held, sums, send(sums, "row", 1, parts))
        blocks = {mask: send(block, "row", mask, parts) for mask in order[:-1]}
        blocks[0] = block
        (partial,) = images(held, [block], (0,))
        (partial,) = images(held, [blocks[nearest]], (nearest,), partial)
        rest = [blocks[mask] for mask in farther]
        if last:
            (own,) = call(
                functools.partial(pack_kernel, masks),
                "pack",
                [blocks[mask] for mask in masks],
                [shape_of((1, block.shape[0], held.shape[1]), BF16)],
                held=held,
            )
            (panel,) = images(held, rest, farther, partial, tasks=tasks)
        else:
            panel, gram = images(held, rest, farther, partial, last=True)
    task_groups, bases = gather(own, "task", tasks, lambda one, other: join(one, other, after=[panel]))
    size = tasks * start_block.shape[2]
    square_shape = shape_of((size, size), F32)
    wide, lower, right_gram = call(
        functools.partial(right_first_kernel, task_groups),
        "right_first",
        bases,
        [shape_of((size, held.shape[1]), BF16), square_shape, square_shape],
    )
    state = call(right_second_kernel, "right_second", [right_gram], [square_shape] * 2)
    right_side = call(right_third_kernel, "right_third", [right_gram, *state, lower], [square_shape])[0]
    _, panels = gather(panel[None], "task", tasks, lambda one, other: join(one, other, after=[state[0]]))
    gram, panel = left(panels, task_groups, right_side)
    bit = parts // 2
    while bit > 1:
        gram = add(gram, send(gram, "row", bit, parts))
        bit //= 2
    return finish(gram, send(gram, "row", 1, parts), panel, wide, lower, right_side)


def solution(mesh):
    tasks, parts = mesh.shape["task"], mesh.shape["row"]
    placed = (P("task", "row", None), P("task", None, None))
    return jax.shard_map(
        functools.partial(local, tasks, parts),
        mesh=mesh,
        in_specs=placed,
        out_specs=P(("row", "task"), None),
        check_vma=False,
    )
```

```python
import functools

import jax
import jax.numpy as jnp
from jax import lax
from jax.experimental import pallas as pl
from jax.experimental.pallas import tpu as pltpu
from jax.sharding import PartitionSpec as P

ITERS = 4
ROOT_STEPS = 12
LANES = 128
TILE = 8
F32 = jnp.float32
BF16 = jnp.bfloat16
ROWS_BY_ROWS = (((1,), (1,)), ((), ()))
VMEM_BYTES = 16 * 1024 * 1024
IN_VMEM = pl.BlockSpec(memory_space=pltpu.VMEM)
ANYWHERE = pl.BlockSpec(memory_space=pl.ANY)


def shape_of(shape, kind):
    return jax.ShapeDtypeStruct(shape, kind)


def call(kernel, name, operands, shapes, scratch=(), held=None, idle=(), flops=10**8):
    operands = [*operands, *idle]
    specs = [IN_VMEM] * (len(operands) - len(idle)) + [ANYWHERE] * len(idle)
    if held is not None:
        operands, specs = [held, *operands], [IN_VMEM, *specs]
    return pl.pallas_call(
        kernel,
        out_shape=tuple(shapes),
        in_specs=specs,
        out_specs=(IN_VMEM,) * len(shapes),
        scratch_shapes=list(scratch),
        cost_estimate=pl.CostEstimate(flops=flops, bytes_accessed=10**6, transcendentals=0),
        compiler_params=pltpu.CompilerParams(vmem_limit_bytes=VMEM_BYTES),
        name=name,
    )(*operands)


def split_two(value):
    high = value.astype(BF16)
    return high, (value - high.astype(F32)).astype(BF16)


def split_three(value):
    high = value.astype(BF16)
    rest = value - high.astype(F32)
    middle = rest.astype(BF16)
    return high, middle, (rest - middle.astype(F32)).astype(BF16)


def spread(value, order, axis):
    pieces = split_three(value)
    return jnp.concatenate([pieces[at] for at in order], axis=axis)


def square(left, right):
    return jnp.dot(
        spread(left, (0, 0, 1, 0, 2, 1), 1), spread(right, (0, 1, 0, 2, 0, 1), 0), preferred_element_type=F32
    )


def eye_of(size):
    return lax.broadcasted_iota(jnp.int32, (size, size), 0) == lax.broadcasted_iota(jnp.int32, (size, size), 1)


def tree_sum(values):
    while len(values) > 1:
        values = [values[at] + values[at + 1] for at in range(0, len(values), 2)]
    return values[0]


def lower_inverse(grams):
    size = grams[0].shape[0]
    tiles = size // TILE
    rows = lax.broadcasted_iota(jnp.int32, (TILE, LANES), 0)
    lanes = lax.broadcasted_iota(jnp.int32, (TILE, LANES), 1)
    columns, inverses, scales = [], [], []
    for gram in grams:
        wide = [jnp.broadcast_to(gram[:, at : at + 1], (size, LANES)) for at in range(size)]
        columns.append([[one[TILE * tile : TILE * (tile + 1)] for tile in range(tiles)] for one in wide])
        inverses.append([(rows + TILE * tile == lanes).astype(F32) for tile in range(tiles)])
        scales.append([jnp.zeros((TILE, LANES), F32) for _ in range(tiles)])
    for step in range(size):
        top, place = divmod(step, TILE)
        for cols, inverse, scale in zip(columns, inverses, scales):
            pivot = cols[step][top][place : place + 1]
            reciprocal = 1.0 / pivot
            ratio = [None] * top + [cols[step][tile] * reciprocal for tile in range(top, tiles)]
            for later in range(step + 1, size):
                first, inner = divmod(later, TILE)
                factor = ratio[first][inner : inner + 1]
                for tile in range(first, tiles):
                    cols[later][tile] = cols[later][tile] - cols[step][tile] * factor
            own = inverse[top][place : place + 1]
            for tile in range(top, tiles):
                factor = jnp.where(rows > place, ratio[tile], 0.0) if tile == top else ratio[tile]
                inverse[tile] = inverse[tile] - factor * own
            scale[top] = jnp.where(rows == place, lax.rsqrt(pivot), scale[top])
    return [
        jnp.concatenate([one * down for one, down in zip(inverse, scale)], axis=0)[:, :size]
        for inverse, scale in zip(inverses, scales)
    ]


def gram_pieces(images):
    return with_pieces(lax.dot_general(images, images, ROWS_BY_ROWS, preferred_element_type=F32))


def tall_of(rows, *sizes):
    return next(size for size in (*sizes, rows) if rows % size == 0)


def partner(axis, mask):
    return lax.bitwise_xor(lax.axis_index(axis).astype(jnp.int32), jnp.int32(mask))


def block_at(index, size):
    return pl.ds(pl.multiple_of(index * size, size), size)


def first_kernel(tall, d_ref, x_ref, out_ref, gram_ref, wide):
    wide[...] = x_ref[...].astype(BF16)
    for at in range(0, d_ref.shape[0], tall):
        product = lax.dot_general(d_ref[at : at + tall, :], wide[...], ROWS_BY_ROWS, preferred_element_type=F32)
        out_ref[:, at : at + tall] = product.T.astype(BF16)
    gram_ref[...] = gram_pieces(out_ref[...])


def first(held, start):
    rows, cols = held.shape
    rank = start.shape[0]
    return call(
        functools.partial(first_kernel, tall_of(rows, 512, 896, 256, 128)),
        "first",
        [start],
        [shape_of((rank, rows), BF16), shape_of((rank, LANES), BF16)],
        [pltpu.VMEM((rank, cols), BF16)],
        held=held,
        flops=2 * rows * cols * 384,
    )


def with_pieces(gram):
    rank = gram.shape[0]
    return jnp.concatenate([*split_three(gram), jnp.zeros((rank, LANES - 3 * rank), BF16)], axis=1)


def from_pieces(pieces):
    rank = pieces.shape[0]
    pieces = pieces.astype(F32)
    return pieces[:, :rank] + pieces[:, rank : 2 * rank] + pieces[:, 2 * rank : 3 * rank]


def backs_kernel(mask, d_ref, images_ref, gram_ref, *refs):
    out_ref = refs[-1]
    chunk = out_ref.shape[1] - LANES
    across = tall_of(chunk, 512)
    out_ref[:, :LANES] = gram_ref[...].astype(out_ref.dtype)
    for at in range(0, chunk, across):
        span = block_at(lax.div(partner("row", mask), 2) * (chunk // across) + at // across, across)
        out_ref[:, LANES + at : LANES + at + across] = jnp.dot(
            images_ref[...], d_ref[:, span], preferred_element_type=F32
        ).astype(out_ref.dtype)


def backs(held, panel, gram, mask, count, *after):
    rows, cols = held.shape
    rank = panel.shape[0]
    return call(
        functools.partial(backs_kernel, mask),
        "backs",
        [panel, gram],
        [shape_of((rank, LANES + cols // count), BF16 if mask else F32)],
        held=held,
        idle=after,
        flops=10**6,
    )[0]


def combine_kernel(_, *refs):
    *in_refs, out_ref = refs
    gram = tree_sum([from_pieces(ref[:, :LANES]) for ref in in_refs])
    out_ref[:, :LANES] = with_pieces(gram)
    out_ref[:, LANES:] = tree_sum([ref[:, LANES:].astype(F32) for ref in in_refs]).astype(BF16)


def settle_kernel(_, one_ref, other_ref, out_ref):
    rank = one_ref.shape[0]
    gram = from_pieces(one_ref[:, :LANES]) + from_pieces(other_ref[:, :LANES])
    total = one_ref[:, LANES:].astype(F32) + other_ref[:, LANES:].astype(F32)
    out_ref[...] = square(lower_inverse([gram])[0], total).astype(BF16)


def combine(held, pieces):
    return call(combine_kernel, "combine", pieces, [shape_of(pieces[0].shape, BF16)], held=held)[0]


def settle(held, one, other):
    rank, wide = one.shape
    return call(settle_kernel, "settle", [one, other], [shape_of((rank, wide - LANES), BF16)], held=held)[0]


def images_kernel(masks, tall, partial, tasks, d_ref, *refs):
    x_refs, refs = refs[: len(masks)], refs[len(masks) :]
    if partial:
        sum_ref, refs = refs[0], refs[1:]
    target = refs[1] if tasks else refs[0]
    chunk = x_refs[0].shape[1]
    for at in range(0, d_ref.shape[0], tall):
        product = sum_ref[:, at : at + tall] if partial else None
        for mask, x_ref in zip(masks, x_refs):
            span = block_at(lax.div(partner("row", mask), 2), chunk)
            term = lax.dot_general(
                d_ref[at : at + tall, span], x_ref[...], ROWS_BY_ROWS, preferred_element_type=F32
            ).T
            product = term if product is None else product + term
        target[:, at : at + tall] = product.astype(target.dtype)
    if tasks:
        out_ref, flat = refs
        each = out_ref.shape[2]
        for at in range(tasks):
            out_ref[at] = flat[:, at * each : (at + 1) * each]
    elif len(refs) == 2:
        refs[1][...] = gram_pieces(refs[0][...])


def images(held, blocks, masks, partial=None, last=False, tasks=0):
    rows, cols = held.shape
    rank, chunk = blocks[0].shape
    scratch = ()
    if tasks:
        shapes = [shape_of((tasks, rank, rows // tasks), BF16)]
        scratch = [pltpu.VMEM((rank, rows), BF16)]
    elif last:
        shapes = [shape_of((rank, rows), BF16), shape_of((rank, LANES), BF16)]
    else:
        shapes = [shape_of((rank, rows), F32)]
    return call(
        functools.partial(images_kernel, masks, tall_of(rows, 896, 512, 256, 128), partial is not None, tasks),
        "images",
        [*blocks] + ([] if partial is None else [partial]),
        shapes,
        scratch,
        held=held,
        flops=2 * rows * chunk * 384 * len(masks),
    )


def join_kernel(first, *refs):
    in_refs, out_ref = refs[first : first + 2], refs[-1]
    if len(out_ref.shape) == 2:
        out_ref[...] = jnp.concatenate([ref[...] for ref in in_refs], axis=1)
    else:
        for at, ref in enumerate(in_refs):
            out_ref[at * ref.shape[0] : (at + 1) * ref.shape[0]] = ref[...]


def join(one, other, held=None, axis=0, after=()):
    shape = list(one.shape)
    shape[axis] *= 2
    kernel = functools.partial(join_kernel, 0 if held is None else 1)
    return call(kernel, "join", [one, other], [shape_of(tuple(shape), one.dtype)], held=held, idle=after)[0]


def pack_kernel(masks, _, *refs):
    *in_refs, out_ref = refs
    chunk = in_refs[0].shape[1]
    for mask, in_ref in zip(masks, in_refs):
        out_ref[0, :, block_at(lax.div(partner("row", mask), 2), chunk)] = in_ref[...]


def left_kernel(groups, *refs):
    in_refs, (gram_ref, panel_ref, whole) = refs[: len(groups)], refs[-3:]
    tasks, rank, each = in_refs[0].shape[-3:]
    for masks, in_ref in zip(groups, in_refs):
        for place, mask in enumerate(masks):
            down = block_at(partner("task", mask), rank)
            for at in range(tasks):
                whole[down, at * each : (at + 1) * each] = in_ref[place, at]
            panel_ref[down, :] = in_ref[place, partner("task", 0)]
    gram_ref[...] = lax.dot_general(whole[...], whole[...], ROWS_BY_ROWS, preferred_element_type=F32)


def left(blocks, groups, after):
    _, tasks, rank, each = blocks[0].shape
    size = tasks * rank
    return call(
        functools.partial(left_kernel, groups),
        "left",
        blocks,
        [shape_of((size, size), F32), shape_of((size, each), BF16)],
        [pltpu.VMEM((size, tasks * each), BF16)],
        idle=[after],
    )


def add_kernel(one_ref, other_ref, *refs):
    refs[-1][...] = one_ref[...] + other_ref[...]


def add(one, other, *after):
    return call(add_kernel, "add", [one, other], [shape_of(one.shape, F32)], idle=after, flops=10**6)[0]


def root_begin(gram):
    return gram / jnp.sqrt(jnp.sum(gram * gram)), eye_of(gram.shape[0]).astype(F32)


def root_steps(state, count):
    identity = eye_of(state[0].shape[0]).astype(F32)

    def step(_, state):
        upper, lower = state
        middle = 0.5 * (3.0 * identity - square(lower, upper))
        both = square(middle, jnp.concatenate([upper, lower], axis=1))
        return both[:, : identity.shape[0]], both[:, identity.shape[0] :]

    return lax.fori_loop(0, count, step, state)


def root_end(state, gram):
    return state[1] / jnp.sqrt(jnp.sqrt(jnp.sum(gram * gram)))


def right_first_kernel(groups, *refs):
    in_refs, (wide_ref, lower_ref, gram_ref) = refs[: len(groups)], refs[-3:]
    rank = in_refs[0].shape[1]
    for masks, in_ref in zip(groups, in_refs):
        for place, mask in enumerate(masks):
            wide_ref[block_at(partner("task", mask), rank), :] = in_ref[place]
    wide = wide_ref[...]
    raw = lax.dot_general(wide, wide, ROWS_BY_ROWS, preferred_element_type=F32)
    spans = [slice(task * rank, (task + 1) * rank) for task in range(wide.shape[0] // rank)]
    lower_ref[...] = jnp.zeros_like(lower_ref)
    for span, inverse in zip(spans, lower_inverse([raw[span, span] for span in spans])):
        lower_ref[span, span] = inverse
    lower = lower_ref[...]
    gram_ref[...] = square(square(lower, raw), lower.T)


def right_begin_kernel(count, gram_ref, upper_ref, lower_ref):
    upper_ref[...], lower_ref[...] = root_steps(root_begin(gram_ref[...]), count)


def right_steps_kernel(count, upper_in, lower_in, upper_ref, lower_ref):
    upper_ref[...], lower_ref[...] = root_steps((upper_in[...], lower_in[...]), count)


def right_end_kernel(count, gram_ref, upper_ref, lower_ref, change_ref, *refs):
    state = root_steps((upper_ref[...], lower_ref[...]), count)
    refs[-1][...] = square(root_end(state, gram_ref[...]).T, change_ref[...])


def finish_kernel(one_ref, other_ref, panel_ref, wide_ref, lower_ref, right_ref, out_ref, side):
    size = lower_ref.shape[0]

    @pl.when(pl.program_id(0) == 0)
    def _():
        lower = lower_ref[...]
        gram = square(square(lower, one_ref[...] + other_ref[...]), lower.T)
        diagonal = jnp.where(eye_of(size), gram, 0.0)
        down = jnp.sqrt(jnp.sum(diagonal, axis=1, keepdims=True))
        across = jnp.sqrt(jnp.sum(diagonal, axis=0, keepdims=True))
        normed = gram / (down * across)
        mixing = root_end(root_steps(root_begin(normed), ROOT_STEPS), normed) / down * across
        mixed = square(square(lower.T, mixing), right_ref[...])
        panel = panel_ref[...].T
        product = jnp.dot(
            jnp.concatenate([panel, panel], axis=1),
            jnp.concatenate(split_two(mixed), axis=0),
            preferred_element_type=F32,
        )
        side[...] = jnp.concatenate(split_two(product), axis=1)

    wide = wide_ref[...]
    out_ref[...] = jnp.dot(
        side[...], jnp.concatenate([wide, wide], axis=0), preferred_element_type=F32
    ).astype(BF16)


def finish(one, other, panel, wide, lower, right_side):
    size, rows = panel.shape
    cols = wide.shape[1]
    across = 512

    def whole(array):
        return pl.BlockSpec(array.shape, lambda at: (0, 0))

    return pl.pallas_call(
        finish_kernel,
        out_shape=shape_of((rows, cols), BF16),
        grid=(cols // across,),
        in_specs=[
            whole(one),
            whole(other),
            whole(panel),
            pl.BlockSpec((size, across), lambda at: (0, at)),
            whole(lower),
            whole(right_side),
        ],
        out_specs=pl.BlockSpec((rows, across), lambda at: (0, at)),
        scratch_shapes=[pltpu.VMEM((rows, 2 * size), BF16)],
        compiler_params=pltpu.CompilerParams(vmem_limit_bytes=VMEM_BYTES),
        name="finish",
    )(one, other, panel, wide, lower, right_side)


def send(piece, axis, mask, count):
    return lax.ppermute(piece, axis, [(at, at ^ mask) for at in range(count)])


def gather(piece, axis, count, joining):
    masks, groups, blocks, block = [0], [(0,)], [piece], piece
    bit = count // 2
    while bit:
        received = send(block, axis, bit, count)
        groups.append(tuple(mask ^ bit for mask in masks))
        blocks.append(received)
        masks = masks + [mask ^ bit for mask in masks]
        bit //= 2
        if bit:
            block = joining(block, received)
    return groups, blocks


def local(tasks, parts, task_delta, start_block):
    masks = tuple(range(0, parts, 2))
    nearest, farther = masks[1], masks[2:]
    count = len(masks)
    order = (*reversed(masks[1:]), 0)
    held = pltpu.with_memory_space_constraint(task_delta[0], pltpu.VMEM)
    panel, gram = first(held, start_block[0].T)
    for step in range(ITERS):
        last = step == ITERS - 1
        received, after = {}, []
        for mask in order[:-1]:
            piece = backs(held, panel, gram, mask, count, *after)
            received[mask] = send(piece, "row", mask, parts)
            after = [piece]
        keep = backs(held, panel, gram, 0, count, *after, received[order[0]])
        sums = combine(held, [keep, *[received[mask] for mask in masks[1:]]])
        block = settle(held, sums, send(sums, "row", 1, parts))
        blocks = {mask: send(block, "row", mask, parts) for mask in order[:-1]}
        blocks[0] = block
        (partial,) = images(held, [block], (0,))
        (partial,) = images(held, [blocks[nearest]], (nearest,), partial)
        rest = [blocks[mask] for mask in farther]
        if last:
            (own,) = call(
                functools.partial(pack_kernel, masks),
                "pack",
                [blocks[mask] for mask in masks],
                [shape_of((1, block.shape[0], held.shape[1]), BF16)],
                held=held,
            )
            (panel,) = images(held, rest, farther, partial, tasks=tasks)
        else:
            panel, gram = images(held, rest, farther, partial, last=True)
    task_groups, bases = gather(own, "task", tasks, lambda one, other: join(one, other, after=[panel]))
    size = tasks * start_block.shape[2]
    square_shape = shape_of((size, size), F32)
    wide, lower, right_gram = call(
        functools.partial(right_first_kernel, task_groups),
        "right_first",
        bases,
        [shape_of((size, held.shape[1]), BF16), square_shape, square_shape],
    )
    begin, middle = ROOT_STEPS // 2, ROOT_STEPS // 6
    state = call(functools.partial(right_begin_kernel, begin), "right_begin", [right_gram], [square_shape] * 2)
    _, panels = gather(panel[None], "task", tasks, lambda one, other: join(one, other, after=[state[0]]))
    state = call(functools.partial(right_steps_kernel, middle), "right_steps", state, [square_shape] * 2)
    gram, panel = left(panels, task_groups, state[0])
    bit = parts // 2
    other = send(gram, "row", bit, parts)
    (right_side,) = call(
        functools.partial(right_end_kernel, ROOT_STEPS - begin - middle),
        "right_end",
        [right_gram, *state, lower],
        [square_shape],
        idle=[gram],
    )
    after = [right_side]
    while bit > 1:
        gram, after = add(gram, other, *after), []
        bit //= 2
        other = send(gram, "row", bit, parts)
    return finish(gram, other, panel, wide, lower, right_side)


def solution(mesh):
    tasks, parts = mesh.shape["task"], mesh.shape["row"]
    placed = (P("task", "row", None), P("task", None, None))
    return jax.shard_map(
        functools.partial(local, tasks, parts),
        mesh=mesh,
        in_specs=placed,
        out_specs=P(("row", "task"), None),
        check_vma=False,
    )
```

```python
import functools

import jax
import jax.numpy as jnp
from jax import lax
from jax.experimental import pallas as pl
from jax.experimental.pallas import tpu as pltpu
from jax.sharding import PartitionSpec as P

ITERS = 4
ROOT_STEPS = 12
LANES = 128
TILE = 8
F32 = jnp.float32
BF16 = jnp.bfloat16
ROWS_BY_ROWS = (((1,), (1,)), ((), ()))
VMEM_BYTES = 16 * 1024 * 1024
IN_VMEM = pl.BlockSpec(memory_space=pltpu.VMEM)
ANYWHERE = pl.BlockSpec(memory_space=pl.ANY)


def shape_of(shape, kind):
    return jax.ShapeDtypeStruct(shape, kind)


def call(kernel, name, operands, shapes, scratch=(), held=None, idle=(), flops=10**8):
    operands = [*operands, *idle]
    specs = [IN_VMEM] * (len(operands) - len(idle)) + [ANYWHERE] * len(idle)
    if held is not None:
        operands, specs = [held, *operands], [IN_VMEM, *specs]
    return pl.pallas_call(
        kernel,
        out_shape=tuple(shapes),
        in_specs=specs,
        out_specs=(IN_VMEM,) * len(shapes),
        scratch_shapes=list(scratch),
        cost_estimate=pl.CostEstimate(flops=flops, bytes_accessed=10**6, transcendentals=0),
        compiler_params=pltpu.CompilerParams(vmem_limit_bytes=VMEM_BYTES),
        name=name,
    )(*operands)


def split_two(value):
    high = value.astype(BF16)
    return high, (value - high.astype(F32)).astype(BF16)


def split_three(value):
    high = value.astype(BF16)
    rest = value - high.astype(F32)
    middle = rest.astype(BF16)
    return high, middle, (rest - middle.astype(F32)).astype(BF16)


def spread(value, order, axis):
    pieces = split_three(value)
    return jnp.concatenate([pieces[at] for at in order], axis=axis)


def square(left, right):
    return jnp.dot(
        spread(left, (0, 0, 1, 0, 2, 1), 1), spread(right, (0, 1, 0, 2, 0, 1), 0), preferred_element_type=F32
    )


def eye_of(size):
    return lax.broadcasted_iota(jnp.int32, (size, size), 0) == lax.broadcasted_iota(jnp.int32, (size, size), 1)


def tree_sum(values):
    while len(values) > 1:
        values = [values[at] + values[at + 1] for at in range(0, len(values), 2)]
    return values[0]


def lower_inverse(grams):
    size = grams[0].shape[0]
    tiles = size // TILE
    rows = lax.broadcasted_iota(jnp.int32, (TILE, LANES), 0)
    lanes = lax.broadcasted_iota(jnp.int32, (TILE, LANES), 1)
    columns, inverses, scales = [], [], []
    for gram in grams:
        wide = [jnp.broadcast_to(gram[:, at : at + 1], (size, LANES)) for at in range(size)]
        columns.append([[one[TILE * tile : TILE * (tile + 1)] for tile in range(tiles)] for one in wide])
        inverses.append([(rows + TILE * tile == lanes).astype(F32) for tile in range(tiles)])
        scales.append([jnp.zeros((TILE, LANES), F32) for _ in range(tiles)])
    for step in range(size):
        top, place = divmod(step, TILE)
        for cols, inverse, scale in zip(columns, inverses, scales):
            pivot = cols[step][top][place : place + 1]
            reciprocal = 1.0 / pivot
            ratio = [None] * top + [cols[step][tile] * reciprocal for tile in range(top, tiles)]
            for later in range(step + 1, size):
                first, inner = divmod(later, TILE)
                factor = ratio[first][inner : inner + 1]
                for tile in range(first, tiles):
                    cols[later][tile] = cols[later][tile] - cols[step][tile] * factor
            own = inverse[top][place : place + 1]
            for tile in range(top, tiles):
                factor = jnp.where(rows > place, ratio[tile], 0.0) if tile == top else ratio[tile]
                inverse[tile] = inverse[tile] - factor * own
            scale[top] = jnp.where(rows == place, lax.rsqrt(pivot), scale[top])
    return [
        jnp.concatenate([one * down for one, down in zip(inverse, scale)], axis=0)[:, :size]
        for inverse, scale in zip(inverses, scales)
    ]


def gram_pieces(images):
    return with_pieces(lax.dot_general(images, images, ROWS_BY_ROWS, preferred_element_type=F32))


def tall_of(rows, *sizes):
    return next(size for size in (*sizes, rows) if rows % size == 0)


def partner(axis, mask):
    return lax.bitwise_xor(lax.axis_index(axis).astype(jnp.int32), jnp.int32(mask))


def block_at(index, size):
    return pl.ds(pl.multiple_of(index * size, size), size)


def first_kernel(tall, d_ref, x_ref, out_ref, gram_ref, wide):
    wide[...] = x_ref[...].astype(BF16)

    def body(at, carry):
        rows = block_at(at, tall)
        product = lax.dot_general(d_ref[rows, :], wide[...], ROWS_BY_ROWS, preferred_element_type=F32)
        out_ref[:, rows] = product.T.astype(BF16)
        return carry

    lax.fori_loop(0, d_ref.shape[0] // tall, body, 0)
    gram_ref[...] = gram_pieces(out_ref[...])


def first(held, start):
    rows, cols = held.shape
    rank = start.shape[0]
    return call(
        functools.partial(first_kernel, tall_of(rows, 896, 512, 256, 128)),
        "first",
        [start],
        [shape_of((rank, rows), BF16), shape_of((rank, LANES), BF16)],
        [pltpu.VMEM((rank, cols), BF16)],
        held=held,
        flops=2 * rows * cols * 384,
    )


def with_pieces(gram):
    rank = gram.shape[0]
    return jnp.concatenate([*split_three(gram), jnp.zeros((rank, LANES - 3 * rank), BF16)], axis=1)


def from_pieces(pieces):
    rank = pieces.shape[0]
    pieces = pieces.astype(F32)
    return pieces[:, :rank] + pieces[:, rank : 2 * rank] + pieces[:, 2 * rank : 3 * rank]


def backs_kernel(mask, d_ref, images_ref, gram_ref, *refs):
    out_ref = refs[-1]
    chunk = out_ref.shape[1] - LANES
    across = tall_of(chunk, 512)
    out_ref[:, :LANES] = gram_ref[...].astype(out_ref.dtype)
    for at in range(0, chunk, across):
        span = block_at(lax.div(partner("row", mask), 2) * (chunk // across) + at // across, across)
        out_ref[:, LANES + at : LANES + at + across] = jnp.dot(
            images_ref[...], d_ref[:, span], preferred_element_type=F32
        ).astype(out_ref.dtype)


def backs(held, panel, gram, mask, count, *after):
    rows, cols = held.shape
    rank = panel.shape[0]
    return call(
        functools.partial(backs_kernel, mask),
        "backs",
        [panel, gram],
        [shape_of((rank, LANES + cols // count), BF16 if mask else F32)],
        held=held,
        idle=after,
        flops=10**6,
    )[0]


def combine_kernel(_, *refs):
    *in_refs, out_ref = refs
    gram = tree_sum([from_pieces(ref[:, :LANES]) for ref in in_refs])
    out_ref[:, :LANES] = with_pieces(gram)
    out_ref[:, LANES:] = tree_sum([ref[:, LANES:].astype(F32) for ref in in_refs]).astype(BF16)


def settle_kernel(_, one_ref, other_ref, out_ref):
    rank = one_ref.shape[0]
    gram = from_pieces(one_ref[:, :LANES]) + from_pieces(other_ref[:, :LANES])
    total = one_ref[:, LANES:].astype(F32) + other_ref[:, LANES:].astype(F32)
    out_ref[...] = square(lower_inverse([gram])[0], total).astype(BF16)


def combine(held, pieces):
    return call(combine_kernel, "combine", pieces, [shape_of(pieces[0].shape, BF16)], held=held)[0]


def settle(held, one, other):
    rank, wide = one.shape
    return call(settle_kernel, "settle", [one, other], [shape_of((rank, wide - LANES), BF16)], held=held)[0]


def images_kernel(masks, tall, partial, tasks, d_ref, *refs):
    x_refs, refs = refs[: len(masks)], refs[len(masks) :]
    if partial:
        sum_ref, refs = refs[0], refs[1:]
    target = refs[1] if tasks else refs[0]
    chunk = x_refs[0].shape[1]

    def body(at, carry):
        rows = block_at(at, tall)
        product = None
        for mask, x_ref in zip(masks, x_refs):
            span = block_at(lax.div(partner("row", mask), 2), chunk)
            term = lax.dot_general(d_ref[rows, span], x_ref[...], ROWS_BY_ROWS, preferred_element_type=F32)
            product = term if product is None else product + term
        product = product.T
        if partial:
            product = product + sum_ref[:, rows]
        target[:, rows] = product.astype(target.dtype)
        return carry

    lax.fori_loop(0, d_ref.shape[0] // tall, body, 0)
    if tasks:
        out_ref, flat = refs
        each = out_ref.shape[2]
        for at in range(tasks):
            out_ref[at] = flat[:, at * each : (at + 1) * each]
    elif len(refs) == 2:
        refs[1][...] = gram_pieces(refs[0][...])


def images(held, blocks, masks, partial=None, last=False, tasks=0):
    rows, cols = held.shape
    rank, chunk = blocks[0].shape
    scratch = ()
    if tasks:
        shapes = [shape_of((tasks, rank, rows // tasks), BF16)]
        scratch = [pltpu.VMEM((rank, rows), BF16)]
    elif last:
        shapes = [shape_of((rank, rows), BF16), shape_of((rank, LANES), BF16)]
    else:
        shapes = [shape_of((rank, rows), F32)]
    return call(
        functools.partial(images_kernel, masks, tall_of(rows, 896, 512, 256, 128), partial is not None, tasks),
        "images",
        [*blocks] + ([] if partial is None else [partial]),
        shapes,
        scratch,
        held=held,
        flops=2 * rows * chunk * 384 * len(masks),
    )


def join_kernel(first, *refs):
    in_refs, out_ref = refs[first : first + 2], refs[-1]
    if len(out_ref.shape) == 2:
        out_ref[...] = jnp.concatenate([ref[...] for ref in in_refs], axis=1)
    else:
        for at, ref in enumerate(in_refs):
            out_ref[at * ref.shape[0] : (at + 1) * ref.shape[0]] = ref[...]


def join(one, other, held=None, axis=0, after=()):
    shape = list(one.shape)
    shape[axis] *= 2
    kernel = functools.partial(join_kernel, 0 if held is None else 1)
    return call(kernel, "join", [one, other], [shape_of(tuple(shape), one.dtype)], held=held, idle=after)[0]


def pack_kernel(masks, _, *refs):
    *in_refs, out_ref = refs
    chunk = in_refs[0].shape[1]
    for mask, in_ref in zip(masks, in_refs):
        out_ref[0, :, block_at(lax.div(partner("row", mask), 2), chunk)] = in_ref[...]


def left_kernel(groups, *refs):
    in_refs, (gram_ref, panel_ref, whole) = refs[: len(groups)], refs[-3:]
    tasks, rank, each = in_refs[0].shape[-3:]
    for masks, in_ref in zip(groups, in_refs):
        for place, mask in enumerate(masks):
            down = block_at(partner("task", mask), rank)
            for at in range(tasks):
                whole[down, at * each : (at + 1) * each] = in_ref[place, at]
            panel_ref[down, :] = in_ref[place, partner("task", 0)]
    gram_ref[...] = lax.dot_general(whole[...], whole[...], ROWS_BY_ROWS, preferred_element_type=F32)


def left(blocks, groups, after):
    _, tasks, rank, each = blocks[0].shape
    size = tasks * rank
    return call(
        functools.partial(left_kernel, groups),
        "left",
        blocks,
        [shape_of((size, size), F32), shape_of((size, each), BF16)],
        [pltpu.VMEM((size, tasks * each), BF16)],
        idle=[after],
    )


def add_kernel(one_ref, other_ref, *refs):
    refs[-1][...] = one_ref[...] + other_ref[...]


def add(one, other, *after):
    return call(add_kernel, "add", [one, other], [shape_of(one.shape, F32)], idle=after, flops=10**6)[0]


def root_begin(gram):
    return gram / jnp.sqrt(jnp.sum(gram * gram)), eye_of(gram.shape[0]).astype(F32)


def root_steps(state, count):
    identity = eye_of(state[0].shape[0]).astype(F32)

    def step(_, state):
        upper, lower = state
        middle = 0.5 * (3.0 * identity - square(lower, upper))
        both = square(middle, jnp.concatenate([upper, lower], axis=1))
        return both[:, : identity.shape[0]], both[:, identity.shape[0] :]

    return lax.fori_loop(0, count, step, state)


def root_end(state, gram):
    return state[1] / jnp.sqrt(jnp.sqrt(jnp.sum(gram * gram)))


def right_first_kernel(groups, *refs):
    in_refs, (wide_ref, lower_ref, gram_ref) = refs[: len(groups)], refs[-3:]
    rank = in_refs[0].shape[1]
    for masks, in_ref in zip(groups, in_refs):
        for place, mask in enumerate(masks):
            wide_ref[block_at(partner("task", mask), rank), :] = in_ref[place]
    wide = wide_ref[...]
    raw = lax.dot_general(wide, wide, ROWS_BY_ROWS, preferred_element_type=F32)
    spans = [slice(task * rank, (task + 1) * rank) for task in range(wide.shape[0] // rank)]
    lower_ref[...] = jnp.zeros_like(lower_ref)
    for span, inverse in zip(spans, lower_inverse([raw[span, span] for span in spans])):
        lower_ref[span, span] = inverse
    lower = lower_ref[...]
    gram_ref[...] = square(square(lower, raw), lower.T)


def right_begin_kernel(count, gram_ref, upper_ref, lower_ref):
    upper_ref[...], lower_ref[...] = root_steps(root_begin(gram_ref[...]), count)


def right_steps_kernel(count, upper_in, lower_in, upper_ref, lower_ref):
    upper_ref[...], lower_ref[...] = root_steps((upper_in[...], lower_in[...]), count)


def right_end_kernel(count, gram_ref, upper_ref, lower_ref, change_ref, *refs):
    state = root_steps((upper_ref[...], lower_ref[...]), count)
    refs[-1][...] = square(root_end(state, gram_ref[...]).T, change_ref[...])


def finish_kernel(one_ref, other_ref, panel_ref, wide_ref, lower_ref, right_ref, out_ref, side):
    size = lower_ref.shape[0]

    @pl.when(pl.program_id(0) == 0)
    def _():
        lower = lower_ref[...]
        gram = square(square(lower, one_ref[...] + other_ref[...]), lower.T)
        diagonal = jnp.where(eye_of(size), gram, 0.0)
        down = jnp.sqrt(jnp.sum(diagonal, axis=1, keepdims=True))
        across = jnp.sqrt(jnp.sum(diagonal, axis=0, keepdims=True))
        normed = gram / (down * across)
        mixing = root_end(root_steps(root_begin(normed), ROOT_STEPS), normed) / down * across
        mixed = square(square(lower.T, mixing), right_ref[...])
        panel = panel_ref[...].T
        product = jnp.dot(
            jnp.concatenate([panel, panel], axis=1),
            jnp.concatenate(split_two(mixed), axis=0),
            preferred_element_type=F32,
        )
        side[...] = jnp.concatenate(split_two(product), axis=1)

    wide = wide_ref[...]
    out_ref[...] = jnp.dot(
        side[...], jnp.concatenate([wide, wide], axis=0), preferred_element_type=F32
    ).astype(BF16)


def finish(one, other, panel, wide, lower, right_side):
    size, rows = panel.shape
    cols = wide.shape[1]
    across = 512

    def whole(array):
        return pl.BlockSpec(array.shape, lambda at: (0, 0))

    return pl.pallas_call(
        finish_kernel,
        out_shape=shape_of((rows, cols), BF16),
        grid=(cols // across,),
        in_specs=[
            whole(one),
            whole(other),
            whole(panel),
            pl.BlockSpec((size, across), lambda at: (0, at)),
            whole(lower),
            whole(right_side),
        ],
        out_specs=pl.BlockSpec((rows, across), lambda at: (0, at)),
        scratch_shapes=[pltpu.VMEM((rows, 2 * size), BF16)],
        compiler_params=pltpu.CompilerParams(vmem_limit_bytes=VMEM_BYTES),
        name="finish",
    )(one, other, panel, wide, lower, right_side)


def send(piece, axis, mask, count):
    return lax.ppermute(piece, axis, [(at, at ^ mask) for at in range(count)])


def gather(piece, axis, count, joining):
    masks, groups, blocks, block = [0], [(0,)], [piece], piece
    bit = count // 2
    while bit:
        received = send(block, axis, bit, count)
        groups.append(tuple(mask ^ bit for mask in masks))
        blocks.append(received)
        masks = masks + [mask ^ bit for mask in masks]
        bit //= 2
        if bit:
            block = joining(block, received)
    return groups, blocks


def local(tasks, parts, task_delta, start_block):
    masks = tuple(range(0, parts, 2))
    nearest, farther = masks[1], masks[2:]
    count = len(masks)
    order = (*reversed(masks[1:]), 0)
    held = pltpu.with_memory_space_constraint(task_delta[0], pltpu.VMEM)
    panel, gram = first(held, start_block[0].T)
    for step in range(ITERS):
        last = step == ITERS - 1
        received, after = {}, []
        for mask in order[:-1]:
            piece = backs(held, panel, gram, mask, count, *after)
            received[mask] = send(piece, "row", mask, parts)
            after = [piece]
        keep = backs(held, panel, gram, 0, count, *after, received[order[0]])
        sums = combine(held, [keep, *[received[mask] for mask in masks[1:]]])
        block = settle(held, sums, send(sums, "row", 1, parts))
        blocks = {mask: send(block, "row", mask, parts) for mask in order[:-1]}
        blocks[0] = block
        (partial,) = images(held, [block], (0,))
        (partial,) = images(held, [blocks[nearest]], (nearest,), partial)
        rest = [blocks[mask] for mask in farther]
        if last:
            (own,) = call(
                functools.partial(pack_kernel, masks),
                "pack",
                [blocks[mask] for mask in masks],
                [shape_of((1, block.shape[0], held.shape[1]), BF16)],
                held=held,
            )
            (panel,) = images(held, rest, farther, partial, tasks=tasks)
        else:
            panel, gram = images(held, rest, farther, partial, last=True)
    task_groups, bases = gather(own, "task", tasks, lambda one, other: join(one, other, after=[panel]))
    size = tasks * start_block.shape[2]
    square_shape = shape_of((size, size), F32)
    wide, lower, right_gram = call(
        functools.partial(right_first_kernel, task_groups),
        "right_first",
        bases,
        [shape_of((size, held.shape[1]), BF16), square_shape, square_shape],
    )
    begin, middle = ROOT_STEPS // 2, ROOT_STEPS // 6
    state = call(functools.partial(right_begin_kernel, begin), "right_begin", [right_gram], [square_shape] * 2)
    _, panels = gather(panel[None], "task", tasks, lambda one, other: join(one, other, after=[state[0]]))
    state = call(functools.partial(right_steps_kernel, middle), "right_steps", state, [square_shape] * 2)
    gram, panel = left(panels, task_groups, state[0])
    bit = parts // 2
    other = send(gram, "row", bit, parts)
    (right_side,) = call(
        functools.partial(right_end_kernel, ROOT_STEPS - begin - middle),
        "right_end",
        [right_gram, *state, lower],
        [square_shape],
        idle=[gram],
    )
    after = [right_side]
    while bit > 1:
        gram, after = add(gram, other, *after), []
        bit //= 2
        other = send(gram, "row", bit, parts)
    return finish(gram, other, panel, wide, lower, right_side)


def solution(mesh):
    tasks, parts = mesh.shape["task"], mesh.shape["row"]
    placed = (P("task", "row", None), P("task", None, None))
    return jax.shard_map(
        functools.partial(local, tasks, parts),
        mesh=mesh,
        in_specs=placed,
        out_specs=P(("row", "task"), None),
        check_vma=False,
    )
```

```python
import functools

import jax
import jax.numpy as jnp
from jax import lax
from jax.experimental import pallas as pl
from jax.experimental.pallas import tpu as pltpu
from jax.sharding import PartitionSpec as P

ITERS = 4
ROOT_STEPS = 12
LANES = 128
TILE = 8
F32 = jnp.float32
BF16 = jnp.bfloat16
ROWS_BY_ROWS = (((1,), (1,)), ((), ()))
VMEM_BYTES = 16 * 1024 * 1024
IN_VMEM = pl.BlockSpec(memory_space=pltpu.VMEM)
ANYWHERE = pl.BlockSpec(memory_space=pl.ANY)


def shape_of(shape, kind):
    return jax.ShapeDtypeStruct(shape, kind)


def call(kernel, name, operands, shapes, scratch=(), held=None, idle=(), flops=10**8):
    operands = [*operands, *idle]
    specs = [IN_VMEM] * (len(operands) - len(idle)) + [ANYWHERE] * len(idle)
    if held is not None:
        operands, specs = [held, *operands], [IN_VMEM, *specs]
    return pl.pallas_call(
        kernel,
        out_shape=tuple(shapes),
        in_specs=specs,
        out_specs=(IN_VMEM,) * len(shapes),
        scratch_shapes=list(scratch),
        cost_estimate=pl.CostEstimate(flops=flops, bytes_accessed=10**6, transcendentals=0),
        compiler_params=pltpu.CompilerParams(vmem_limit_bytes=VMEM_BYTES),
        name=name,
    )(*operands)


def split_two(value):
    high = value.astype(BF16)
    return high, (value - high.astype(F32)).astype(BF16)


def split_three(value):
    high = value.astype(BF16)
    rest = value - high.astype(F32)
    middle = rest.astype(BF16)
    return high, middle, (rest - middle.astype(F32)).astype(BF16)


def spread(value, order, axis):
    pieces = split_three(value)
    return jnp.concatenate([pieces[at] for at in order], axis=axis)


def square(left, right):
    return jnp.dot(
        spread(left, (0, 0, 1, 0, 2, 1), 1), spread(right, (0, 1, 0, 2, 0, 1), 0), preferred_element_type=F32
    )


def eye_of(size):
    return lax.broadcasted_iota(jnp.int32, (size, size), 0) == lax.broadcasted_iota(jnp.int32, (size, size), 1)


def tree_sum(values):
    while len(values) > 1:
        values = [values[at] + values[at + 1] for at in range(0, len(values), 2)]
    return values[0]


def lower_inverse(grams):
    size = grams[0].shape[0]
    tiles = size // TILE
    rows = lax.broadcasted_iota(jnp.int32, (TILE, LANES), 0)
    lanes = lax.broadcasted_iota(jnp.int32, (TILE, LANES), 1)
    columns, inverses, scales = [], [], []
    for gram in grams:
        wide = [jnp.broadcast_to(gram[:, at : at + 1], (size, LANES)) for at in range(size)]
        columns.append([[one[TILE * tile : TILE * (tile + 1)] for tile in range(tiles)] for one in wide])
        inverses.append([(rows + TILE * tile == lanes).astype(F32) for tile in range(tiles)])
        scales.append([jnp.zeros((TILE, LANES), F32) for _ in range(tiles)])
    for step in range(size):
        top, place = divmod(step, TILE)
        for cols, inverse, scale in zip(columns, inverses, scales):
            pivot = cols[step][top][place : place + 1]
            reciprocal = 1.0 / pivot
            ratio = [None] * top + [cols[step][tile] * reciprocal for tile in range(top, tiles)]
            for later in range(step + 1, size):
                first, inner = divmod(later, TILE)
                factor = ratio[first][inner : inner + 1]
                for tile in range(first, tiles):
                    cols[later][tile] = cols[later][tile] - cols[step][tile] * factor
            own = inverse[top][place : place + 1]
            for tile in range(top, tiles):
                factor = jnp.where(rows > place, ratio[tile], 0.0) if tile == top else ratio[tile]
                inverse[tile] = inverse[tile] - factor * own
            scale[top] = jnp.where(rows == place, lax.rsqrt(pivot), scale[top])
    return [
        jnp.concatenate([one * down for one, down in zip(inverse, scale)], axis=0)[:, :size]
        for inverse, scale in zip(inverses, scales)
    ]


def gram_pieces(images):
    return with_pieces(lax.dot_general(images, images, ROWS_BY_ROWS, preferred_element_type=F32))


def tall_of(rows, *sizes):
    return next(size for size in (*sizes, rows) if rows % size == 0)


def partner(axis, mask):
    return lax.bitwise_xor(lax.axis_index(axis).astype(jnp.int32), jnp.int32(mask))


def block_at(index, size):
    return pl.ds(pl.multiple_of(index * size, size), size)


def first_kernel(tall, d_ref, x_ref, out_ref, gram_ref, wide):
    wide[...] = x_ref[...].astype(BF16)

    def body(at, carry):
        rows = block_at(at, tall)
        product = lax.dot_general(d_ref[rows, :], wide[...], ROWS_BY_ROWS, preferred_element_type=F32)
        out_ref[:, rows] = product.T.astype(BF16)
        return carry

    lax.fori_loop(0, d_ref.shape[0] // tall, body, 0)
    gram_ref[...] = gram_pieces(out_ref[...])


def first(held, start):
    rows, cols = held.shape
    rank = start.shape[0]
    return call(
        functools.partial(first_kernel, tall_of(rows, 896, 512, 256, 128)),
        "first",
        [start],
        [shape_of((rank, rows), BF16), shape_of((rank, LANES), BF16)],
        [pltpu.VMEM((rank, cols), BF16)],
        held=held,
        flops=2 * rows * cols * 384,
    )


def with_pieces(gram):
    rank = gram.shape[0]
    return jnp.concatenate([*split_three(gram), jnp.zeros((rank, LANES - 3 * rank), BF16)], axis=1)


def from_pieces(pieces):
    rank = pieces.shape[0]
    pieces = pieces.astype(F32)
    return pieces[:, :rank] + pieces[:, rank : 2 * rank] + pieces[:, 2 * rank : 3 * rank]


def backs_kernel(mask, d_ref, images_ref, gram_ref, *refs):
    out_ref = refs[-1]
    chunk = out_ref.shape[1] - LANES
    across = tall_of(chunk, 512)
    out_ref[:, :LANES] = gram_ref[...].astype(out_ref.dtype)
    for at in range(0, chunk, across):
        span = block_at(lax.div(partner("row", mask), 2) * (chunk // across) + at // across, across)
        out_ref[:, LANES + at : LANES + at + across] = jnp.dot(
            images_ref[...], d_ref[:, span], preferred_element_type=F32
        ).astype(out_ref.dtype)


def backs(held, panel, gram, mask, count, *after):
    rows, cols = held.shape
    rank = panel.shape[0]
    return call(
        functools.partial(backs_kernel, mask),
        "backs",
        [panel, gram],
        [shape_of((rank, LANES + cols // count), BF16 if mask else F32)],
        held=held,
        idle=after,
        flops=10**6,
    )[0]


def combine_kernel(_, *refs):
    *in_refs, out_ref = refs
    gram = tree_sum([from_pieces(ref[:, :LANES]) for ref in in_refs])
    out_ref[:, :LANES] = with_pieces(gram)
    out_ref[:, LANES:] = tree_sum([ref[:, LANES:].astype(F32) for ref in in_refs]).astype(BF16)


def settle_kernel(_, one_ref, other_ref, out_ref):
    rank = one_ref.shape[0]
    gram = from_pieces(one_ref[:, :LANES]) + from_pieces(other_ref[:, :LANES])
    total = one_ref[:, LANES:].astype(F32) + other_ref[:, LANES:].astype(F32)
    out_ref[...] = square(lower_inverse([gram])[0], total).astype(BF16)


def combine(held, pieces):
    return call(combine_kernel, "combine", pieces, [shape_of(pieces[0].shape, BF16)], held=held)[0]


def settle(held, one, other):
    rank, wide = one.shape
    return call(settle_kernel, "settle", [one, other], [shape_of((rank, wide - LANES), BF16)], held=held)[0]


def images_kernel(masks, tall, partial, tasks, d_ref, *refs):
    x_refs, refs = refs[: len(masks)], refs[len(masks) :]
    if partial:
        sum_ref, refs = refs[0], refs[1:]
    target = refs[1] if tasks else refs[0]
    chunk = x_refs[0].shape[1]

    def body(at, carry):
        rows = block_at(at, tall)
        product = None
        for mask, x_ref in zip(masks, x_refs):
            span = block_at(lax.div(partner("row", mask), 2), chunk)
            term = lax.dot_general(d_ref[rows, span], x_ref[...], ROWS_BY_ROWS, preferred_element_type=F32)
            product = term if product is None else product + term
        product = product.T
        if partial:
            product = product + sum_ref[:, rows]
        target[:, rows] = product.astype(target.dtype)
        return carry

    lax.fori_loop(0, d_ref.shape[0] // tall, body, 0)
    if tasks:
        out_ref, flat = refs
        each = out_ref.shape[2]
        for at in range(tasks):
            out_ref[at] = flat[:, at * each : (at + 1) * each]
    elif len(refs) == 2:
        refs[1][...] = gram_pieces(refs[0][...])


def images(held, blocks, masks, partial=None, last=False, tasks=0):
    rows, cols = held.shape
    rank, chunk = blocks[0].shape
    scratch = ()
    if tasks:
        shapes = [shape_of((tasks, rank, rows // tasks), BF16)]
        scratch = [pltpu.VMEM((rank, rows), BF16)]
    elif last:
        shapes = [shape_of((rank, rows), BF16), shape_of((rank, LANES), BF16)]
    else:
        shapes = [shape_of((rank, rows), F32)]
    return call(
        functools.partial(images_kernel, masks, tall_of(rows, 896, 512, 256, 128), partial is not None, tasks),
        "images",
        [*blocks] + ([] if partial is None else [partial]),
        shapes,
        scratch,
        held=held,
        flops=2 * rows * chunk * 384 * len(masks),
    )


def join_kernel(first, *refs):
    in_refs, out_ref = refs[first : first + 2], refs[-1]
    if len(out_ref.shape) == 2:
        out_ref[...] = jnp.concatenate([ref[...] for ref in in_refs], axis=1)
    else:
        for at, ref in enumerate(in_refs):
            out_ref[at * ref.shape[0] : (at + 1) * ref.shape[0]] = ref[...]


def join(one, other, held=None, axis=0, after=()):
    shape = list(one.shape)
    shape[axis] *= 2
    kernel = functools.partial(join_kernel, 0 if held is None else 1)
    return call(kernel, "join", [one, other], [shape_of(tuple(shape), one.dtype)], held=held, idle=after)[0]


def pack_kernel(masks, _, *refs):
    *in_refs, out_ref = refs
    chunk = in_refs[0].shape[1]
    for mask, in_ref in zip(masks, in_refs):
        out_ref[0, :, block_at(lax.div(partner("row", mask), 2), chunk)] = in_ref[...]


def left_kernel(groups, *refs):
    in_refs, (gram_ref, panel_ref, whole) = refs[: len(groups)], refs[-3:]
    tasks, rank, each = in_refs[0].shape[-3:]
    for masks, in_ref in zip(groups, in_refs):
        for place, mask in enumerate(masks):
            down = block_at(partner("task", mask), rank)
            for at in range(tasks):
                whole[down, at * each : (at + 1) * each] = in_ref[place, at]
            panel_ref[down, :] = in_ref[place, partner("task", 0)]
    gram_ref[...] = lax.dot_general(whole[...], whole[...], ROWS_BY_ROWS, preferred_element_type=F32)


def left(blocks, groups, after):
    _, tasks, rank, each = blocks[0].shape
    size = tasks * rank
    return call(
        functools.partial(left_kernel, groups),
        "left",
        blocks,
        [shape_of((size, size), F32), shape_of((size, each), BF16)],
        [pltpu.VMEM((size, tasks * each), BF16)],
        idle=[after],
    )


def add_kernel(one_ref, other_ref, *refs):
    refs[-1][...] = one_ref[...] + other_ref[...]


def add(one, other, *after):
    return call(add_kernel, "add", [one, other], [shape_of(one.shape, F32)], idle=after, flops=10**6)[0]


def root_begin(gram):
    return gram / jnp.sqrt(jnp.sum(gram * gram)), eye_of(gram.shape[0]).astype(F32)


def root_steps(state, count):
    identity = eye_of(state[0].shape[0]).astype(F32)

    def step(_, state):
        upper, lower = state
        middle = 0.5 * (3.0 * identity - square(lower, upper))
        both = square(middle, jnp.concatenate([upper, lower], axis=1))
        return both[:, : identity.shape[0]], both[:, identity.shape[0] :]

    return lax.fori_loop(0, count, step, state)


def root_end(state, gram):
    return state[1] / jnp.sqrt(jnp.sqrt(jnp.sum(gram * gram)))


def right_first_kernel(groups, *refs):
    in_refs, (wide_ref, lower_ref, gram_ref) = refs[: len(groups)], refs[-3:]
    rank = in_refs[0].shape[1]
    for masks, in_ref in zip(groups, in_refs):
        for place, mask in enumerate(masks):
            wide_ref[block_at(partner("task", mask), rank), :] = in_ref[place]
    wide = wide_ref[...]
    raw = lax.dot_general(wide, wide, ROWS_BY_ROWS, preferred_element_type=F32)
    spans = [slice(task * rank, (task + 1) * rank) for task in range(wide.shape[0] // rank)]
    lower_ref[...] = jnp.zeros_like(lower_ref)
    for span, inverse in zip(spans, lower_inverse([raw[span, span] for span in spans])):
        lower_ref[span, span] = inverse
    lower = lower_ref[...]
    gram_ref[...] = square(square(lower, raw), lower.T)


def right_begin_kernel(count, gram_ref, upper_ref, lower_ref):
    upper_ref[...], lower_ref[...] = root_steps(root_begin(gram_ref[...]), count)


def right_steps_kernel(count, upper_in, lower_in, upper_ref, lower_ref):
    upper_ref[...], lower_ref[...] = root_steps((upper_in[...], lower_in[...]), count)


def right_end_kernel(count, gram_ref, upper_ref, lower_ref, change_ref, *refs):
    state = root_steps((upper_ref[...], lower_ref[...]), count)
    refs[-1][...] = square(root_end(state, gram_ref[...]).T, change_ref[...])


def finish_kernel(across, one_ref, other_ref, panel_ref, wide_ref, lower_ref, right_ref, out_ref, made, sems):
    size, cols = wide_ref.shape
    lower = lower_ref[...]
    gram = square(square(lower, one_ref[...] + other_ref[...]), lower.T)
    diagonal = jnp.where(eye_of(size), gram, 0.0)
    down = jnp.sqrt(jnp.sum(diagonal, axis=1, keepdims=True))
    over = jnp.sqrt(jnp.sum(diagonal, axis=0, keepdims=True))
    normed = gram / (down * over)
    mixing = root_end(root_steps(root_begin(normed), ROOT_STEPS), normed) / down * over
    mixed = square(square(lower.T, mixing), right_ref[...])
    panel = panel_ref[...].T
    product = jnp.dot(
        jnp.concatenate([panel, panel], axis=1),
        jnp.concatenate(split_two(mixed), axis=0),
        preferred_element_type=F32,
    )
    side = jnp.concatenate(split_two(product), axis=1)
    copies = []
    for at in range(cols // across):
        span = slice(at * across, (at + 1) * across)
        wide = wide_ref[:, span]
        made[at] = jnp.dot(side, jnp.concatenate([wide, wide], axis=0), preferred_element_type=F32).astype(BF16)
        copies.append(pltpu.make_async_copy(made.at[at], out_ref.at[:, span], sems.at[at]))
        copies[-1].start()
    for copy in copies:
        copy.wait()


def finish(one, other, panel, wide, lower, right_side):
    size, rows = panel.shape
    cols = wide.shape[1]
    across = 512
    return pl.pallas_call(
        functools.partial(finish_kernel, across),
        out_shape=shape_of((rows, cols), BF16),
        in_specs=[IN_VMEM] * 6,
        out_specs=ANYWHERE,
        scratch_shapes=[
            pltpu.VMEM((cols // across, rows, across), BF16),
            pltpu.SemaphoreType.DMA((cols // across,)),
        ],
        compiler_params=pltpu.CompilerParams(vmem_limit_bytes=VMEM_BYTES),
        name="finish",
    )(one, other, panel, wide, lower, right_side)


def send(piece, axis, mask, count):
    return lax.ppermute(piece, axis, [(at, at ^ mask) for at in range(count)])


def gather(piece, axis, count, joining):
    masks, groups, blocks, block = [0], [(0,)], [piece], piece
    bit = count // 2
    while bit:
        received = send(block, axis, bit, count)
        groups.append(tuple(mask ^ bit for mask in masks))
        blocks.append(received)
        masks = masks + [mask ^ bit for mask in masks]
        bit //= 2
        if bit:
            block = joining(block, received)
    return groups, blocks


def local(tasks, parts, task_delta, start_block):
    masks = tuple(range(0, parts, 2))
    nearest, farther = masks[1], masks[2:]
    count = len(masks)
    order = (*reversed(masks[1:]), 0)
    held = pltpu.with_memory_space_constraint(task_delta[0], pltpu.VMEM)
    panel, gram = first(held, start_block[0].T)
    for step in range(ITERS):
        last = step == ITERS - 1
        received, after = {}, []
        for mask in order[:-1]:
            piece = backs(held, panel, gram, mask, count, *after)
            received[mask] = send(piece, "row", mask, parts)
            after = [piece]
        keep = backs(held, panel, gram, 0, count, *after, received[order[0]])
        sums = combine(held, [keep, *[received[mask] for mask in masks[1:]]])
        block = settle(held, sums, send(sums, "row", 1, parts))
        blocks = {mask: send(block, "row", mask, parts) for mask in order[:-1]}
        blocks[0] = block
        (partial,) = images(held, [block, blocks[nearest]], (0, nearest))
        rest = [blocks[mask] for mask in farther]
        if last:
            (own,) = call(
                functools.partial(pack_kernel, masks),
                "pack",
                [blocks[mask] for mask in masks],
                [shape_of((1, block.shape[0], held.shape[1]), BF16)],
                held=held,
            )
            (panel,) = images(held, rest, farther, partial, tasks=tasks)
        else:
            panel, gram = images(held, rest, farther, partial, last=True)
    task_groups, bases = gather(own, "task", tasks, lambda one, other: join(one, other, after=[panel]))
    size = tasks * start_block.shape[2]
    square_shape = shape_of((size, size), F32)
    wide, lower, right_gram = call(
        functools.partial(right_first_kernel, task_groups),
        "right_first",
        bases,
        [shape_of((size, held.shape[1]), BF16), square_shape, square_shape],
    )
    begin, middle = ROOT_STEPS // 2, ROOT_STEPS // 6
    state = call(functools.partial(right_begin_kernel, begin), "right_begin", [right_gram], [square_shape] * 2)
    _, panels = gather(panel[None], "task", tasks, lambda one, other: join(one, other, after=[state[0]]))
    state = call(functools.partial(right_steps_kernel, middle), "right_steps", state, [square_shape] * 2)
    gram, panel = left(panels, task_groups, state[0])
    bit = parts // 2
    other = send(gram, "row", bit, parts)
    (right_side,) = call(
        functools.partial(right_end_kernel, ROOT_STEPS - begin - middle),
        "right_end",
        [right_gram, *state, lower],
        [square_shape],
        idle=[gram],
    )
    after = [right_side]
    while bit > 1:
        gram, after = add(gram, other, *after), []
        bit //= 2
        other = send(gram, "row", bit, parts)
    return finish(gram, other, panel, wide, lower, right_side)


def solution(mesh):
    tasks, parts = mesh.shape["task"], mesh.shape["row"]
    placed = (P("task", "row", None), P("task", None, None))
    return jax.shard_map(
        functools.partial(local, tasks, parts),
        mesh=mesh,
        in_specs=placed,
        out_specs=P(("row", "task"), None),
        check_vma=False,
    )
```

```python
import functools

import jax
import jax.numpy as jnp
from jax import lax
from jax.experimental import pallas as pl
from jax.experimental.pallas import tpu as pltpu
from jax.sharding import PartitionSpec as P

ITERS = 4
ROOT_STEPS = 12
LANES = 128
TILE = 8
F32 = jnp.float32
BF16 = jnp.bfloat16
ROWS_BY_ROWS = (((1,), (1,)), ((), ()))
VMEM_BYTES = 16 * 1024 * 1024
IN_VMEM = pl.BlockSpec(memory_space=pltpu.VMEM)
ANYWHERE = pl.BlockSpec(memory_space=pl.ANY)


def shape_of(shape, kind):
    return jax.ShapeDtypeStruct(shape, kind)


def call(kernel, name, operands, shapes, scratch=(), held=None, idle=(), flops=10**8):
    operands = [*operands, *idle]
    specs = [IN_VMEM] * (len(operands) - len(idle)) + [ANYWHERE] * len(idle)
    if held is not None:
        operands, specs = [held, *operands], [IN_VMEM, *specs]
    return pl.pallas_call(
        kernel,
        out_shape=tuple(shapes),
        in_specs=specs,
        out_specs=(IN_VMEM,) * len(shapes),
        scratch_shapes=list(scratch),
        cost_estimate=pl.CostEstimate(flops=flops, bytes_accessed=10**6, transcendentals=0),
        compiler_params=pltpu.CompilerParams(vmem_limit_bytes=VMEM_BYTES),
        name=name,
    )(*operands)


def split_two(value):
    high = value.astype(BF16)
    return high, (value - high.astype(F32)).astype(BF16)


def split_three(value):
    high = value.astype(BF16)
    rest = value - high.astype(F32)
    middle = rest.astype(BF16)
    return high, middle, (rest - middle.astype(F32)).astype(BF16)


def spread(value, order, axis):
    pieces = split_three(value)
    return jnp.concatenate([pieces[at] for at in order], axis=axis)


def square(left, right):
    return jnp.dot(
        spread(left, (0, 0, 1, 0, 2, 1), 1), spread(right, (0, 1, 0, 2, 0, 1), 0), preferred_element_type=F32
    )


def eye_of(size):
    return lax.broadcasted_iota(jnp.int32, (size, size), 0) == lax.broadcasted_iota(jnp.int32, (size, size), 1)


def tree_sum(values):
    while len(values) > 1:
        values = [values[at] + values[at + 1] for at in range(0, len(values), 2)]
    return values[0]


def lower_inverse(grams):
    size = grams[0].shape[0]
    tiles = size // TILE
    rows = lax.broadcasted_iota(jnp.int32, (TILE, LANES), 0)
    lanes = lax.broadcasted_iota(jnp.int32, (TILE, LANES), 1)
    columns, inverses, scales = [], [], []
    for gram in grams:
        wide = [jnp.broadcast_to(gram[:, at : at + 1], (size, LANES)) for at in range(size)]
        columns.append([[one[TILE * tile : TILE * (tile + 1)] for tile in range(tiles)] for one in wide])
        inverses.append([(rows + TILE * tile == lanes).astype(F32) for tile in range(tiles)])
        scales.append([jnp.zeros((TILE, LANES), F32) for _ in range(tiles)])
    for step in range(size):
        top, place = divmod(step, TILE)
        for cols, inverse, scale in zip(columns, inverses, scales):
            pivot = cols[step][top][place : place + 1]
            reciprocal = 1.0 / pivot
            ratio = [None] * top + [cols[step][tile] * reciprocal for tile in range(top, tiles)]
            for later in range(step + 1, size):
                first, inner = divmod(later, TILE)
                factor = ratio[first][inner : inner + 1]
                for tile in range(first, tiles):
                    cols[later][tile] = cols[later][tile] - cols[step][tile] * factor
            own = inverse[top][place : place + 1]
            for tile in range(top, tiles):
                factor = jnp.where(rows > place, ratio[tile], 0.0) if tile == top else ratio[tile]
                inverse[tile] = inverse[tile] - factor * own
            scale[top] = jnp.where(rows == place, lax.rsqrt(pivot), scale[top])
    return [
        jnp.concatenate([one * down for one, down in zip(inverse, scale)], axis=0)[:, :size]
        for inverse, scale in zip(inverses, scales)
    ]


def gram_pieces(images):
    return with_pieces(lax.dot_general(images, images, ROWS_BY_ROWS, preferred_element_type=F32))


def tall_of(rows, *sizes):
    return next(size for size in (*sizes, rows) if rows % size == 0)


def partner(axis, mask):
    return lax.bitwise_xor(lax.axis_index(axis).astype(jnp.int32), jnp.int32(mask))


def block_at(index, size):
    return pl.ds(pl.multiple_of(index * size, size), size)


def first_kernel(tall, d_ref, x_ref, out_ref, gram_ref, wide):
    wide[...] = x_ref[...].astype(BF16)

    def body(at, carry):
        rows = block_at(at, tall)
        product = lax.dot_general(d_ref[rows, :], wide[...], ROWS_BY_ROWS, preferred_element_type=F32)
        out_ref[:, rows] = product.T.astype(BF16)
        return carry

    lax.fori_loop(0, d_ref.shape[0] // tall, body, 0)
    gram_ref[...] = gram_pieces(out_ref[...])


def first(held, start):
    rows, cols = held.shape
    rank = start.shape[0]
    return call(
        functools.partial(first_kernel, tall_of(rows, 1792, 896, 512, 256, 128)),
        "first",
        [start],
        [shape_of((rank, rows), BF16), shape_of((rank, LANES), BF16)],
        [pltpu.VMEM((rank, cols), BF16)],
        held=held,
        flops=2 * rows * cols * 384,
    )


def with_pieces(gram):
    rank = gram.shape[0]
    return jnp.concatenate([*split_three(gram), jnp.zeros((rank, LANES - 3 * rank), BF16)], axis=1)


def from_pieces(pieces):
    rank = pieces.shape[0]
    pieces = pieces.astype(F32)
    return pieces[:, :rank] + pieces[:, rank : 2 * rank] + pieces[:, 2 * rank : 3 * rank]


def backs_kernel(mask, d_ref, images_ref, gram_ref, *refs):
    out_ref = refs[-1]
    chunk = out_ref.shape[1] - LANES
    across = tall_of(chunk, 512)
    out_ref[:, :LANES] = gram_ref[...].astype(out_ref.dtype)
    for at in range(0, chunk, across):
        span = block_at(lax.div(partner("row", mask), 2) * (chunk // across) + at // across, across)
        out_ref[:, LANES + at : LANES + at + across] = jnp.dot(
            images_ref[...], d_ref[:, span], preferred_element_type=F32
        ).astype(out_ref.dtype)


def backs(held, panel, gram, mask, count, *after):
    rows, cols = held.shape
    rank = panel.shape[0]
    return call(
        functools.partial(backs_kernel, mask),
        "backs",
        [panel, gram],
        [shape_of((rank, LANES + cols // count), BF16 if mask else F32)],
        held=held,
        idle=after,
        flops=10**6,
    )[0]


def combine_kernel(_, *refs):
    *in_refs, out_ref = refs
    gram = tree_sum([from_pieces(ref[:, :LANES]) for ref in in_refs])
    out_ref[:, :LANES] = with_pieces(gram)
    out_ref[:, LANES:] = tree_sum([ref[:, LANES:].astype(F32) for ref in in_refs]).astype(BF16)


def settle_kernel(_, one_ref, other_ref, out_ref):
    rank = one_ref.shape[0]
    gram = from_pieces(one_ref[:, :LANES]) + from_pieces(other_ref[:, :LANES])
    total = one_ref[:, LANES:].astype(F32) + other_ref[:, LANES:].astype(F32)
    out_ref[...] = square(lower_inverse([gram])[0], total).astype(BF16)


def combine(held, pieces):
    return call(combine_kernel, "combine", pieces, [shape_of(pieces[0].shape, BF16)], held=held)[0]


def settle(held, one, other):
    rank, wide = one.shape
    return call(settle_kernel, "settle", [one, other], [shape_of((rank, wide - LANES), BF16)], held=held)[0]


def images_kernel(masks, tall, partial, tasks, d_ref, *refs):
    x_refs, refs = refs[: len(masks)], refs[len(masks) :]
    if partial:
        sum_ref, refs = refs[0], refs[1:]
    target = refs[1] if tasks else refs[0]
    chunk = x_refs[0].shape[1]

    def body(at, carry):
        rows = block_at(at, tall)
        product = None
        for mask, x_ref in zip(masks, x_refs):
            span = block_at(lax.div(partner("row", mask), 2), chunk)
            term = lax.dot_general(d_ref[rows, span], x_ref[...], ROWS_BY_ROWS, preferred_element_type=F32)
            product = term if product is None else product + term
        product = product.T
        if partial:
            product = product + sum_ref[:, rows]
        target[:, rows] = product.astype(target.dtype)
        return carry

    lax.fori_loop(0, d_ref.shape[0] // tall, body, 0)
    if tasks:
        out_ref, flat = refs
        each = out_ref.shape[2]
        for at in range(tasks):
            out_ref[at] = flat[:, at * each : (at + 1) * each]
    elif len(refs) == 2:
        refs[1][...] = gram_pieces(refs[0][...])


def images(held, blocks, masks, partial=None, last=False, tasks=0):
    rows, cols = held.shape
    rank, chunk = blocks[0].shape
    scratch = ()
    if tasks:
        shapes = [shape_of((tasks, rank, rows // tasks), BF16)]
        scratch = [pltpu.VMEM((rank, rows), BF16)]
    elif last:
        shapes = [shape_of((rank, rows), BF16), shape_of((rank, LANES), BF16)]
    else:
        shapes = [shape_of((rank, rows), F32)]
    return call(
        functools.partial(images_kernel, masks, tall_of(rows, 896, 512, 256, 128), partial is not None, tasks),
        "images",
        [*blocks] + ([] if partial is None else [partial]),
        shapes,
        scratch,
        held=held,
        flops=2 * rows * chunk * 384 * len(masks),
    )


def join_kernel(first, *refs):
    in_refs, out_ref = refs[first : first + 2], refs[-1]
    if len(out_ref.shape) == 2:
        out_ref[...] = jnp.concatenate([ref[...] for ref in in_refs], axis=1)
    else:
        for at, ref in enumerate(in_refs):
            out_ref[at * ref.shape[0] : (at + 1) * ref.shape[0]] = ref[...]


def join(one, other, held=None, axis=0, after=()):
    shape = list(one.shape)
    shape[axis] *= 2
    kernel = functools.partial(join_kernel, 0 if held is None else 1)
    return call(kernel, "join", [one, other], [shape_of(tuple(shape), one.dtype)], held=held, idle=after)[0]


def pack_kernel(masks, _, *refs):
    in_refs, out_ref = refs[: len(masks)], refs[-1]
    chunk = in_refs[0].shape[1]
    for mask, in_ref in zip(masks, in_refs):
        out_ref[0, :, block_at(lax.div(partner("row", mask), 2), chunk)] = in_ref[...]


def left_kernel(groups, *refs):
    in_refs, (gram_ref, panel_ref, whole) = refs[: len(groups)], refs[-3:]
    tasks, rank, each = in_refs[0].shape[-3:]
    for masks, in_ref in zip(groups, in_refs):
        for place, mask in enumerate(masks):
            down = block_at(partner("task", mask), rank)
            for at in range(tasks):
                whole[down, at * each : (at + 1) * each] = in_ref[place, at]
            panel_ref[down, :] = in_ref[place, partner("task", 0)]
    gram_ref[...] = lax.dot_general(whole[...], whole[...], ROWS_BY_ROWS, preferred_element_type=F32)


def left(blocks, groups, after):
    _, tasks, rank, each = blocks[0].shape
    size = tasks * rank
    return call(
        functools.partial(left_kernel, groups),
        "left",
        blocks,
        [shape_of((size, size), F32), shape_of((size, each), BF16)],
        [pltpu.VMEM((size, tasks * each), BF16)],
        idle=[after],
    )


def add_kernel(count, *refs):
    refs[-1][...] = tree_sum([ref[...] for ref in refs[:count]])


def add(terms, *after):
    kernel = functools.partial(add_kernel, len(terms))
    return call(kernel, "add", terms, [shape_of(terms[0].shape, F32)], idle=after, flops=10**6)[0]


def root_begin(gram):
    return gram / jnp.sqrt(jnp.sum(gram * gram)), eye_of(gram.shape[0]).astype(F32)


def root_steps(state, count):
    identity = eye_of(state[0].shape[0]).astype(F32)

    def step(_, state):
        upper, lower = state
        middle = 0.5 * (3.0 * identity - square(lower, upper))
        both = square(middle, jnp.concatenate([upper, lower], axis=1))
        return both[:, : identity.shape[0]], both[:, identity.shape[0] :]

    return lax.fori_loop(0, count, step, state)


def root_end(state, gram):
    return state[1] / jnp.sqrt(jnp.sqrt(jnp.sum(gram * gram)))


def right_first_kernel(groups, *refs):
    in_refs, (wide_ref, lower_ref, gram_ref) = refs[: len(groups)], refs[-3:]
    rank = in_refs[0].shape[1]
    for masks, in_ref in zip(groups, in_refs):
        for place, mask in enumerate(masks):
            wide_ref[block_at(partner("task", mask), rank), :] = in_ref[place]
    wide = wide_ref[...]
    raw = lax.dot_general(wide, wide, ROWS_BY_ROWS, preferred_element_type=F32)
    spans = [slice(task * rank, (task + 1) * rank) for task in range(wide.shape[0] // rank)]
    lower_ref[...] = jnp.zeros_like(lower_ref)
    for span, inverse in zip(spans, lower_inverse([raw[span, span] for span in spans])):
        lower_ref[span, span] = inverse
    lower = lower_ref[...]
    gram_ref[...] = square(square(lower, raw), lower.T)


def right_begin_kernel(count, gram_ref, upper_ref, lower_ref):
    upper_ref[...], lower_ref[...] = root_steps(root_begin(gram_ref[...]), count)


def right_steps_kernel(count, upper_in, lower_in, upper_ref, lower_ref):
    upper_ref[...], lower_ref[...] = root_steps((upper_in[...], lower_in[...]), count)


def right_end_kernel(count, gram_ref, upper_ref, lower_ref, change_ref, *refs):
    state = root_steps((upper_ref[...], lower_ref[...]), count)
    refs[-1][...] = square(root_end(state, gram_ref[...]).T, change_ref[...])


def finish_kernel(across, one_ref, other_ref, panel_ref, wide_ref, lower_ref, right_ref, out_ref, made, sems):
    size, cols = wide_ref.shape
    lower = lower_ref[...]
    gram = square(square(lower, one_ref[...] + other_ref[...]), lower.T)
    diagonal = jnp.where(eye_of(size), gram, 0.0)
    down = jnp.sqrt(jnp.sum(diagonal, axis=1, keepdims=True))
    over = jnp.sqrt(jnp.sum(diagonal, axis=0, keepdims=True))
    normed = gram / (down * over)
    mixing = root_end(root_steps(root_begin(normed), ROOT_STEPS), normed) / down * over
    mixed = square(square(lower.T, mixing), right_ref[...])
    panel = panel_ref[...].T
    product = jnp.dot(
        jnp.concatenate([panel, panel], axis=1),
        jnp.concatenate(split_two(mixed), axis=0),
        preferred_element_type=F32,
    )
    side = jnp.concatenate(split_two(product), axis=1)
    copies = []
    for at in range(cols // across):
        span = slice(at * across, (at + 1) * across)
        wide = wide_ref[:, span]
        made[at] = jnp.dot(side, jnp.concatenate([wide, wide], axis=0), preferred_element_type=F32).astype(BF16)
        copies.append(pltpu.make_async_copy(made.at[at], out_ref.at[:, span], sems.at[at]))
        copies[-1].start()
    for copy in copies:
        copy.wait()


def finish(one, other, panel, wide, lower, right_side):
    size, rows = panel.shape
    cols = wide.shape[1]
    across = 512
    return pl.pallas_call(
        functools.partial(finish_kernel, across),
        out_shape=shape_of((rows, cols), BF16),
        in_specs=[IN_VMEM] * 6,
        out_specs=ANYWHERE,
        scratch_shapes=[
            pltpu.VMEM((cols // across, rows, across), BF16),
            pltpu.SemaphoreType.DMA((cols // across,)),
        ],
        compiler_params=pltpu.CompilerParams(vmem_limit_bytes=VMEM_BYTES),
        name="finish",
    )(one, other, panel, wide, lower, right_side)


def send(piece, axis, mask, count):
    return lax.ppermute(piece, axis, [(at, at ^ mask) for at in range(count)])


def gather(piece, axis, count, joining):
    masks, groups, blocks, block = [0], [(0,)], [piece], piece
    bit = count // 2
    while bit:
        received = send(block, axis, bit, count)
        groups.append(tuple(mask ^ bit for mask in masks))
        blocks.append(received)
        masks = masks + [mask ^ bit for mask in masks]
        bit //= 2
        if bit:
            block = joining(block, received)
    return groups, blocks


def local(tasks, parts, task_delta, start_block):
    masks = tuple(range(0, parts, 2))
    nearest, farther = masks[1], masks[2:]
    count = len(masks)
    order = (*reversed(masks[1:]), 0)
    held = pltpu.with_memory_space_constraint(task_delta[0], pltpu.VMEM)
    panel, gram = first(held, start_block[0].T)
    for step in range(ITERS):
        last = step == ITERS - 1
        received, after = {}, []
        for mask in order[:-1]:
            piece = backs(held, panel, gram, mask, count, *after)
            received[mask] = send(piece, "row", mask, parts)
            after = [piece]
        keep = backs(held, panel, gram, 0, count, *after, received[order[0]])
        sums = combine(held, [keep, *[received[mask] for mask in masks[1:]]])
        block = settle(held, sums, send(sums, "row", 1, parts))
        blocks = {mask: send(block, "row", mask, parts) for mask in order[:-1]}
        blocks[0] = block
        (partial,) = images(held, [block, blocks[nearest]], (0, nearest))
        rest = [blocks[mask] for mask in farther]
        if last:
            (own,) = call(
                functools.partial(pack_kernel, masks),
                "pack",
                [blocks[mask] for mask in masks],
                [shape_of((1, block.shape[0], held.shape[1]), BF16)],
                held=held,
                idle=[partial],
            )
            (panel,) = images(held, rest, farther, partial, tasks=tasks)
        else:
            panel, gram = images(held, rest, farther, partial, last=True)
    task_groups, bases = gather(own, "task", tasks, lambda one, other: join(one, other, after=[panel]))
    size = tasks * start_block.shape[2]
    square_shape = shape_of((size, size), F32)
    wide, lower, right_gram = call(
        functools.partial(right_first_kernel, task_groups),
        "right_first",
        bases,
        [shape_of((size, held.shape[1]), BF16), square_shape, square_shape],
    )
    begin, middle = ROOT_STEPS // 2, ROOT_STEPS // 6
    state = call(functools.partial(right_begin_kernel, begin), "right_begin", [right_gram], [square_shape] * 2)
    _, panels = gather(panel[None], "task", tasks, lambda one, other: join(one, other, after=[state[0]]))
    state = call(functools.partial(right_steps_kernel, middle), "right_steps", state, [square_shape] * 2)
    gram, panel = left(panels, task_groups, state[0])
    received = {mask: send(gram, "row", mask, parts) for mask in order[:-1]}
    (right_side,) = call(
        functools.partial(right_end_kernel, ROOT_STEPS - begin - middle),
        "right_end",
        [right_gram, *state, lower],
        [square_shape],
        idle=[gram],
    )
    gram = add([gram, *[received[mask] for mask in masks[1:]]], right_side)
    other = send(gram, "row", 1, parts)
    return finish(gram, other, panel, wide, lower, right_side)


def solution(mesh):
    tasks, parts = mesh.shape["task"], mesh.shape["row"]
    placed = (P("task", "row", None), P("task", None, None))
    return jax.shard_map(
        functools.partial(local, tasks, parts),
        mesh=mesh,
        in_specs=placed,
        out_specs=P(("row", "task"), None),
        check_vma=False,
    )
```

```python
import functools

import jax
import jax.numpy as jnp
from jax import lax
from jax.experimental import pallas as pl
from jax.experimental.pallas import tpu as pltpu
from jax.sharding import PartitionSpec as P

ITERS = 4
ROOT_STEPS = 12
LANES = 128
TILE = 8
F32 = jnp.float32
BF16 = jnp.bfloat16
ROWS_BY_ROWS = (((1,), (1,)), ((), ()))
VMEM_BYTES = 16 * 1024 * 1024
IN_VMEM = pl.BlockSpec(memory_space=pltpu.VMEM)
ANYWHERE = pl.BlockSpec(memory_space=pl.ANY)


def shape_of(shape, kind):
    return jax.ShapeDtypeStruct(shape, kind)


def call(kernel, name, operands, shapes, scratch=(), held=None, idle=(), flops=10**8):
    operands = [*operands, *idle]
    specs = [IN_VMEM] * (len(operands) - len(idle)) + [ANYWHERE] * len(idle)
    if held is not None:
        operands, specs = [held, *operands], [IN_VMEM, *specs]
    return pl.pallas_call(
        kernel,
        out_shape=tuple(shapes),
        in_specs=specs,
        out_specs=(IN_VMEM,) * len(shapes),
        scratch_shapes=list(scratch),
        cost_estimate=pl.CostEstimate(flops=flops, bytes_accessed=10**6, transcendentals=0),
        compiler_params=pltpu.CompilerParams(vmem_limit_bytes=VMEM_BYTES),
        name=name,
    )(*operands)


def split_two(value):
    high = value.astype(BF16)
    return high, (value - high.astype(F32)).astype(BF16)


def split_three(value):
    high = value.astype(BF16)
    rest = value - high.astype(F32)
    middle = rest.astype(BF16)
    return high, middle, (rest - middle.astype(F32)).astype(BF16)


def spread(value, order, axis):
    pieces = split_three(value)
    return jnp.concatenate([pieces[at] for at in order], axis=axis)


def square(left, right):
    return jnp.dot(
        spread(left, (0, 0, 1, 0, 2, 1), 1), spread(right, (0, 1, 0, 2, 0, 1), 0), preferred_element_type=F32
    )


def eye_of(size):
    return lax.broadcasted_iota(jnp.int32, (size, size), 0) == lax.broadcasted_iota(jnp.int32, (size, size), 1)


def tree_sum(values):
    while len(values) > 1:
        values = [values[at] + values[at + 1] for at in range(0, len(values), 2)]
    return values[0]


def lower_inverse(grams):
    size = grams[0].shape[0]
    tiles = size // TILE
    rows = lax.broadcasted_iota(jnp.int32, (TILE, LANES), 0)
    lanes = lax.broadcasted_iota(jnp.int32, (TILE, LANES), 1)
    columns, inverses, scales = [], [], []
    for gram in grams:
        wide = [jnp.broadcast_to(gram[:, at : at + 1], (size, LANES)) for at in range(size)]
        columns.append([[one[TILE * tile : TILE * (tile + 1)] for tile in range(tiles)] for one in wide])
        inverses.append([(rows + TILE * tile == lanes).astype(F32) for tile in range(tiles)])
        scales.append([jnp.zeros((TILE, LANES), F32) for _ in range(tiles)])
    for step in range(size):
        top, place = divmod(step, TILE)
        for cols, inverse, scale in zip(columns, inverses, scales):
            pivot = cols[step][top][place : place + 1]
            reciprocal = 1.0 / pivot
            ratio = [None] * top + [cols[step][tile] * reciprocal for tile in range(top, tiles)]
            for later in range(step + 1, size):
                first, inner = divmod(later, TILE)
                factor = ratio[first][inner : inner + 1]
                for tile in range(first, tiles):
                    cols[later][tile] = cols[later][tile] - cols[step][tile] * factor
            own = inverse[top][place : place + 1]
            for tile in range(top, tiles):
                factor = jnp.where(rows > place, ratio[tile], 0.0) if tile == top else ratio[tile]
                inverse[tile] = inverse[tile] - factor * own
            scale[top] = jnp.where(rows == place, lax.rsqrt(pivot), scale[top])
    return [
        jnp.concatenate([one * down for one, down in zip(inverse, scale)], axis=0)[:, :size]
        for inverse, scale in zip(inverses, scales)
    ]


def gram_pieces(images):
    return with_pieces(lax.dot_general(images, images, ROWS_BY_ROWS, preferred_element_type=F32))


def tall_of(rows, *sizes):
    return next(size for size in (*sizes, rows) if rows % size == 0)


def partner(axis, mask):
    return lax.bitwise_xor(lax.axis_index(axis).astype(jnp.int32), jnp.int32(mask))


def block_at(index, size):
    return pl.ds(pl.multiple_of(index * size, size), size)


def first_kernel(tall, d_ref, x_ref, out_ref, gram_ref, wide):
    wide[...] = x_ref[...].astype(BF16)

    def body(at, carry):
        rows = block_at(at, tall)
        product = lax.dot_general(d_ref[rows, :], wide[...], ROWS_BY_ROWS, preferred_element_type=F32)
        out_ref[:, rows] = product.T.astype(BF16)
        return carry

    lax.fori_loop(0, d_ref.shape[0] // tall, body, 0)
    gram_ref[...] = gram_pieces(out_ref[...])


def first(held, start):
    rows, cols = held.shape
    rank = start.shape[0]
    return call(
        functools.partial(first_kernel, tall_of(rows, 1792, 896, 512, 256, 128)),
        "first",
        [start],
        [shape_of((rank, rows), BF16), shape_of((rank, LANES), BF16)],
        [pltpu.VMEM((rank, cols), BF16)],
        held=held,
        flops=2 * rows * cols * 384,
    )


def with_pieces(gram):
    rank = gram.shape[0]
    return jnp.concatenate([*split_three(gram), jnp.zeros((rank, LANES - 3 * rank), BF16)], axis=1)


def from_pieces(pieces):
    rank = pieces.shape[0]
    pieces = pieces.astype(F32)
    return pieces[:, :rank] + pieces[:, rank : 2 * rank] + pieces[:, 2 * rank : 3 * rank]


def backs_kernel(mask, d_ref, images_ref, gram_ref, *refs):
    out_ref = refs[-1]
    chunk = out_ref.shape[1] - LANES
    across = tall_of(chunk, 512)
    out_ref[:, :LANES] = gram_ref[...].astype(out_ref.dtype)
    for at in range(0, chunk, across):
        span = block_at(lax.div(partner("row", mask), 2) * (chunk // across) + at // across, across)
        out_ref[:, LANES + at : LANES + at + across] = jnp.dot(
            images_ref[...], d_ref[:, span], preferred_element_type=F32
        ).astype(out_ref.dtype)


def backs(held, panel, gram, mask, count, *after):
    rows, cols = held.shape
    rank = panel.shape[0]
    return call(
        functools.partial(backs_kernel, mask),
        "backs",
        [panel, gram],
        [shape_of((rank, LANES + cols // count), BF16 if mask else F32)],
        held=held,
        idle=after,
        flops=10**6,
    )[0]


def combine_kernel(_, *refs):
    own_ref, *in_refs, out_ref = refs
    in_refs = [own_ref, *reversed(in_refs)]
    gram = tree_sum([from_pieces(ref[:, :LANES]) for ref in in_refs])
    out_ref[:, :LANES] = with_pieces(gram)
    out_ref[:, LANES:] = tree_sum([ref[:, LANES:].astype(F32) for ref in in_refs]).astype(BF16)


def settle_kernel(_, one_ref, other_ref, out_ref):
    rank = one_ref.shape[0]
    gram = from_pieces(one_ref[:, :LANES]) + from_pieces(other_ref[:, :LANES])
    total = one_ref[:, LANES:].astype(F32) + other_ref[:, LANES:].astype(F32)
    out_ref[...] = square(lower_inverse([gram])[0], total).astype(BF16)


def combine(held, pieces):
    return call(combine_kernel, "combine", pieces, [shape_of(pieces[0].shape, BF16)], held=held)[0]


def settle(held, one, other):
    rank, wide = one.shape
    return call(settle_kernel, "settle", [one, other], [shape_of((rank, wide - LANES), BF16)], held=held)[0]


def images_kernel(masks, tall, partial, tasks, d_ref, *refs):
    x_refs, refs = refs[: len(masks)], refs[len(masks) :]
    if partial:
        sum_ref, refs = refs[0], refs[1:]
    target = refs[1] if tasks else refs[0]
    chunk = x_refs[0].shape[1]

    def body(at, carry):
        rows = block_at(at, tall)
        product = None
        for mask, x_ref in zip(masks, x_refs):
            span = block_at(lax.div(partner("row", mask), 2), chunk)
            term = lax.dot_general(d_ref[rows, span], x_ref[...], ROWS_BY_ROWS, preferred_element_type=F32)
            product = term if product is None else product + term
        product = product.T
        if partial:
            product = product + sum_ref[:, rows]
        target[:, rows] = product.astype(target.dtype)
        return carry

    lax.fori_loop(0, d_ref.shape[0] // tall, body, 0)
    if tasks:
        out_ref, flat = refs
        each = out_ref.shape[2]
        for at in range(tasks):
            out_ref[at] = flat[:, at * each : (at + 1) * each]
    elif len(refs) == 2:
        refs[1][...] = gram_pieces(refs[0][...])


def images(held, blocks, masks, partial=None, last=False, tasks=0):
    rows, cols = held.shape
    rank, chunk = blocks[0].shape
    scratch = ()
    if tasks:
        shapes = [shape_of((tasks, rank, rows // tasks), BF16)]
        scratch = [pltpu.VMEM((rank, rows), BF16)]
    elif last:
        shapes = [shape_of((rank, rows), BF16), shape_of((rank, LANES), BF16)]
    else:
        shapes = [shape_of((rank, rows), F32)]
    return call(
        functools.partial(images_kernel, masks, tall_of(rows, 896, 512, 256, 128), partial is not None, tasks),
        "images",
        [*blocks] + ([] if partial is None else [partial]),
        shapes,
        scratch,
        held=held,
        flops=2 * rows * chunk * 384 * len(masks),
    )


def join_kernel(first, *refs):
    in_refs, out_ref = refs[first : first + 2], refs[-1]
    if len(out_ref.shape) == 2:
        out_ref[...] = jnp.concatenate([ref[...] for ref in in_refs], axis=1)
    else:
        for at, ref in enumerate(in_refs):
            out_ref[at * ref.shape[0] : (at + 1) * ref.shape[0]] = ref[...]


def join(one, other, held=None, axis=0, after=()):
    shape = list(one.shape)
    shape[axis] *= 2
    kernel = functools.partial(join_kernel, 0 if held is None else 1)
    return call(kernel, "join", [one, other], [shape_of(tuple(shape), one.dtype)], held=held, idle=after)[0]


def pack_kernel(masks, _, *refs):
    in_refs, out_ref = refs[: len(masks)], refs[-1]
    chunk = in_refs[0].shape[1]
    for mask, in_ref in zip(masks, in_refs):
        out_ref[0, :, block_at(lax.div(partner("row", mask), 2), chunk)] = in_ref[...]


def left_kernel(groups, *refs):
    in_refs, (gram_ref, panel_ref, whole) = refs[: len(groups)], refs[-3:]
    tasks, rank, each = in_refs[0].shape[-3:]
    for masks, in_ref in zip(groups, in_refs):
        for place, mask in enumerate(masks):
            down = block_at(partner("task", mask), rank)
            for at in range(tasks):
                whole[down, at * each : (at + 1) * each] = in_ref[place, at]
            panel_ref[down, :] = in_ref[place, partner("task", 0)]
    gram_ref[...] = lax.dot_general(whole[...], whole[...], ROWS_BY_ROWS, preferred_element_type=F32)


def left(blocks, groups, after):
    _, tasks, rank, each = blocks[0].shape
    size = tasks * rank
    return call(
        functools.partial(left_kernel, groups),
        "left",
        blocks,
        [shape_of((size, size), F32), shape_of((size, each), BF16)],
        [pltpu.VMEM((size, tasks * each), BF16)],
        idle=[after],
    )


def add_kernel(count, *refs):
    refs[-1][...] = tree_sum([ref[...] for ref in refs[:count]])


def add(terms, *after):
    kernel = functools.partial(add_kernel, len(terms))
    return call(kernel, "add", terms, [shape_of(terms[0].shape, F32)], idle=after, flops=10**6)[0]


def root_begin(gram):
    upper = gram / jnp.sqrt(jnp.sum(gram * gram))
    middle = 0.5 * (3.0 * eye_of(gram.shape[0]).astype(F32) - upper)
    return square(upper, middle), middle


def root_steps(state, count, each=1):
    size = state[0].shape[0]
    identity = eye_of(size).astype(F32)

    def step(_, state):
        upper, lower = state
        for _ in range(each):
            middle = 0.5 * (3.0 * identity - square(lower, upper))
            both = square(middle, jnp.concatenate([upper, lower], axis=1))
            upper, lower = both[:, :size], both[:, size:]
        return upper, lower

    return lax.fori_loop(0, count // each, step, state)


def root_end(state, gram):
    return state[1] / jnp.sqrt(jnp.sqrt(jnp.sum(gram * gram)))


def right_first_kernel(groups, *refs):
    in_refs, (wide_ref, lower_ref, gram_ref) = refs[: len(groups)], refs[-3:]
    rank = in_refs[0].shape[1]
    for masks, in_ref in zip(groups, in_refs):
        for place, mask in enumerate(masks):
            wide_ref[block_at(partner("task", mask), rank), :] = in_ref[place]
    wide = wide_ref[...]
    raw = lax.dot_general(wide, wide, ROWS_BY_ROWS, preferred_element_type=F32)
    spans = [slice(task * rank, (task + 1) * rank) for task in range(wide.shape[0] // rank)]
    lower_ref[...] = jnp.zeros_like(lower_ref)
    for span, inverse in zip(spans, lower_inverse([raw[span, span] for span in spans])):
        lower_ref[span, span] = inverse
    lower = lower_ref[...]
    gram_ref[...] = square(square(lower, raw), lower.T)


def right_begin_kernel(count, gram_ref, upper_ref, lower_ref):
    upper_ref[...], lower_ref[...] = root_steps(root_begin(gram_ref[...]), count - 1)


def right_steps_kernel(count, upper_in, lower_in, upper_ref, lower_ref):
    upper_ref[...], lower_ref[...] = root_steps((upper_in[...], lower_in[...]), count)


def right_end_kernel(count, gram_ref, upper_ref, lower_ref, change_ref, *refs):
    state = root_steps((upper_ref[...], lower_ref[...]), count)
    refs[-1][...] = square(root_end(state, gram_ref[...]).T, change_ref[...])


def finish_kernel(across, one_ref, other_ref, panel_ref, wide_ref, lower_ref, right_ref, out_ref, made, sems):
    size, cols = wide_ref.shape
    lower = lower_ref[...]
    gram = square(square(lower, one_ref[...] + other_ref[...]), lower.T)
    diagonal = jnp.where(eye_of(size), gram, 0.0)
    down = jnp.sqrt(jnp.sum(diagonal, axis=1, keepdims=True))
    over = jnp.sqrt(jnp.sum(diagonal, axis=0, keepdims=True))
    normed = gram / (down * over)
    state = root_steps(root_begin(normed), (ROOT_STEPS - 1) // 2 * 2, 2)
    state = root_steps(state, (ROOT_STEPS - 1) % 2)
    mixing = root_end(state, normed) / down * over
    mixed = square(square(lower.T, mixing), right_ref[...])
    panel = panel_ref[...].T
    product = jnp.dot(
        jnp.concatenate([panel, panel], axis=1),
        jnp.concatenate(split_two(mixed), axis=0),
        preferred_element_type=F32,
    )
    side = jnp.concatenate(split_two(product), axis=1)
    copies = []
    for at in range(cols // across):
        span = slice(at * across, (at + 1) * across)
        wide = wide_ref[:, span]
        made[at] = jnp.dot(side, jnp.concatenate([wide, wide], axis=0), preferred_element_type=F32).astype(BF16)
        copies.append(pltpu.make_async_copy(made.at[at], out_ref.at[:, span], sems.at[at]))
        copies[-1].start()
    for copy in copies:
        copy.wait()


def finish(one, other, panel, wide, lower, right_side):
    size, rows = panel.shape
    cols = wide.shape[1]
    across = 512
    return pl.pallas_call(
        functools.partial(finish_kernel, across),
        out_shape=shape_of((rows, cols), BF16),
        in_specs=[IN_VMEM] * 6,
        out_specs=ANYWHERE,
        scratch_shapes=[
            pltpu.VMEM((cols // across, rows, across), BF16),
            pltpu.SemaphoreType.DMA((cols // across,)),
        ],
        compiler_params=pltpu.CompilerParams(vmem_limit_bytes=VMEM_BYTES),
        name="finish",
    )(one, other, panel, wide, lower, right_side)


def send(piece, axis, mask, count):
    return lax.ppermute(piece, axis, [(at, at ^ mask) for at in range(count)])


def gather(piece, axis, count, joining):
    masks, groups, blocks, block = [0], [(0,)], [piece], piece
    bit = count // 2
    while bit:
        received = send(block, axis, bit, count)
        groups.append(tuple(mask ^ bit for mask in masks))
        blocks.append(received)
        masks = masks + [mask ^ bit for mask in masks]
        bit //= 2
        if bit:
            block = joining(block, received)
    return groups, blocks


def local(tasks, parts, task_delta, start_block):
    masks = tuple(range(0, parts, 2))
    nearest, farther = masks[1], masks[2:]
    count = len(masks)
    order = (*reversed(masks[1:]), 0)
    held = pltpu.with_memory_space_constraint(task_delta[0], pltpu.VMEM)
    panel, gram = first(held, start_block[0].T)
    for step in range(ITERS):
        last = step == ITERS - 1
        received, after = {}, []
        for mask in order[:-1]:
            piece = backs(held, panel, gram, mask, count, *after)
            received[mask] = send(piece, "row", mask, parts)
            after = [piece]
        keep = backs(held, panel, gram, 0, count, *after, received[order[0]])
        sums = combine(held, [keep, *[received[mask] for mask in reversed(masks[1:])]])
        block = settle(held, sums, send(sums, "row", 1, parts))
        blocks = {mask: send(block, "row", mask, parts) for mask in order[:-1]}
        blocks[0] = block
        (partial,) = images(held, [block, blocks[nearest]], (0, nearest))
        rest = [blocks[mask] for mask in farther]
        if last:
            (own,) = call(
                functools.partial(pack_kernel, masks),
                "pack",
                [blocks[mask] for mask in masks],
                [shape_of((1, block.shape[0], held.shape[1]), BF16)],
                held=held,
                idle=[partial],
            )
            (panel,) = images(held, rest, farther, partial, tasks=tasks)
        else:
            panel, gram = images(held, rest, farther, partial, last=True)
    task_groups, bases = gather(own, "task", tasks, lambda one, other: join(one, other, after=[panel]))
    size = tasks * start_block.shape[2]
    square_shape = shape_of((size, size), F32)
    wide, lower, right_gram = call(
        functools.partial(right_first_kernel, task_groups),
        "right_first",
        bases,
        [shape_of((size, held.shape[1]), BF16), square_shape, square_shape],
    )
    begin, middle = ROOT_STEPS // 2, ROOT_STEPS // 6
    state = call(functools.partial(right_begin_kernel, begin), "right_begin", [right_gram], [square_shape] * 2)
    _, panels = gather(panel[None], "task", tasks, lambda one, other: join(one, other, after=[state[0]]))
    state = call(functools.partial(right_steps_kernel, middle), "right_steps", state, [square_shape] * 2)
    gram, panel = left(panels, task_groups, state[0])
    received = {mask: send(gram, "row", mask, parts) for mask in order[:-1]}
    (right_side,) = call(
        functools.partial(right_end_kernel, ROOT_STEPS - begin - middle),
        "right_end",
        [right_gram, *state, lower],
        [square_shape],
        idle=[gram],
    )
    gram = add([gram, *[received[mask] for mask in masks[1:]]], right_side)
    other = send(gram, "row", 1, parts)
    return finish(gram, other, panel, wide, lower, right_side)


def solution(mesh):
    tasks, parts = mesh.shape["task"], mesh.shape["row"]
    placed = (P("task", "row", None), P("task", None, None))
    return jax.shard_map(
        functools.partial(local, tasks, parts),
        mesh=mesh,
        in_specs=placed,
        out_specs=P(("row", "task"), None),
        check_vma=False,
    )
```

```python
import functools

import jax
import jax.numpy as jnp
from jax import lax
from jax.experimental import pallas as pl
from jax.experimental.pallas import tpu as pltpu
from jax.sharding import PartitionSpec as P

ITERS = 4
ROOT_STEPS = 12
LANES = 128
TILE = 8
F32 = jnp.float32
BF16 = jnp.bfloat16
ROWS_BY_ROWS = (((1,), (1,)), ((), ()))
VMEM_BYTES = 16 * 1024 * 1024
IN_VMEM = pl.BlockSpec(memory_space=pltpu.VMEM)
ANYWHERE = pl.BlockSpec(memory_space=pl.ANY)


def shape_of(shape, kind):
    return jax.ShapeDtypeStruct(shape, kind)


def call(kernel, name, operands, shapes, scratch=(), held=None, idle=(), flops=10**8):
    operands = [*operands, *idle]
    specs = [IN_VMEM] * (len(operands) - len(idle)) + [ANYWHERE] * len(idle)
    if held is not None:
        operands, specs = [held, *operands], [IN_VMEM, *specs]
    return pl.pallas_call(
        kernel,
        out_shape=tuple(shapes),
        in_specs=specs,
        out_specs=(IN_VMEM,) * len(shapes),
        scratch_shapes=list(scratch),
        cost_estimate=pl.CostEstimate(flops=flops, bytes_accessed=10**6, transcendentals=0),
        compiler_params=pltpu.CompilerParams(vmem_limit_bytes=VMEM_BYTES),
        name=name,
    )(*operands)


def split_two(value):
    high = value.astype(BF16)
    return high, (value - high.astype(F32)).astype(BF16)


def split_three(value):
    high = value.astype(BF16)
    rest = value - high.astype(F32)
    middle = rest.astype(BF16)
    return high, middle, (rest - middle.astype(F32)).astype(BF16)


def spread(value, order, axis):
    pieces = split_three(value)
    return jnp.concatenate([pieces[at] for at in order], axis=axis)


def square(left, right):
    return jnp.dot(
        spread(left, (0, 0, 1, 0, 2, 1), 1), spread(right, (0, 1, 0, 2, 0, 1), 0), preferred_element_type=F32
    )


def eye_of(size):
    return lax.broadcasted_iota(jnp.int32, (size, size), 0) == lax.broadcasted_iota(jnp.int32, (size, size), 1)


def tree_sum(values):
    while len(values) > 1:
        values = [values[at] + values[at + 1] for at in range(0, len(values), 2)]
    return values[0]


def lower_inverse(grams):
    size = grams[0].shape[0]
    tiles = size // TILE
    rows = lax.broadcasted_iota(jnp.int32, (TILE, LANES), 0)
    lanes = lax.broadcasted_iota(jnp.int32, (TILE, LANES), 1)
    columns, inverses, scales = [], [], []
    for gram in grams:
        wide = [jnp.broadcast_to(gram[:, at : at + 1], (size, LANES)) for at in range(size)]
        columns.append([[one[TILE * tile : TILE * (tile + 1)] for tile in range(tiles)] for one in wide])
        inverses.append([(rows + TILE * tile == lanes).astype(F32) for tile in range(tiles)])
        scales.append([jnp.zeros((TILE, LANES), F32) for _ in range(tiles)])
    for step in range(size):
        top, place = divmod(step, TILE)
        for cols, inverse, scale in zip(columns, inverses, scales):
            pivot = cols[step][top][place : place + 1]
            reciprocal = 1.0 / pivot
            ratio = [None] * top + [cols[step][tile] * reciprocal for tile in range(top, tiles)]
            for later in range(step + 1, size):
                first, inner = divmod(later, TILE)
                factor = ratio[first][inner : inner + 1]
                for tile in range(first, tiles):
                    cols[later][tile] = cols[later][tile] - cols[step][tile] * factor
            own = inverse[top][place : place + 1]
            for tile in range(top, tiles):
                factor = jnp.where(rows > place, ratio[tile], 0.0) if tile == top else ratio[tile]
                inverse[tile] = inverse[tile] - factor * own
            scale[top] = jnp.where(rows == place, lax.rsqrt(pivot), scale[top])
    return [
        jnp.concatenate([one * down for one, down in zip(inverse, scale)], axis=0)[:, :size]
        for inverse, scale in zip(inverses, scales)
    ]


def gram_pieces(images):
    return with_pieces(lax.dot_general(images, images, ROWS_BY_ROWS, preferred_element_type=F32))


def tall_of(rows, *sizes):
    return next(size for size in (*sizes, rows) if rows % size == 0)


def partner(axis, mask):
    return lax.bitwise_xor(lax.axis_index(axis).astype(jnp.int32), jnp.int32(mask))


def block_at(index, size):
    return pl.ds(pl.multiple_of(index * size, size), size)


def first_kernel(tall, d_ref, x_ref, out_ref, gram_ref, wide):
    wide[...] = x_ref[...].astype(BF16)

    def body(at, carry):
        rows = block_at(at, tall)
        product = lax.dot_general(d_ref[rows, :], wide[...], ROWS_BY_ROWS, preferred_element_type=F32)
        out_ref[:, rows] = product.T.astype(BF16)
        return carry

    lax.fori_loop(0, d_ref.shape[0] // tall, body, 0)
    gram_ref[...] = gram_pieces(out_ref[...])


def first(held, start):
    rows, cols = held.shape
    rank = start.shape[0]
    return call(
        functools.partial(first_kernel, tall_of(rows, 1792, 896, 512, 256, 128)),
        "first",
        [start],
        [shape_of((rank, rows), BF16), shape_of((rank, LANES), BF16)],
        [pltpu.VMEM((rank, cols), BF16)],
        held=held,
        flops=2 * rows * cols * 384,
    )


def with_pieces(gram):
    rank = gram.shape[0]
    return jnp.concatenate([*split_three(gram), jnp.zeros((rank, LANES - 3 * rank), BF16)], axis=1)


def from_pieces(pieces):
    rank = pieces.shape[0]
    pieces = pieces.astype(F32)
    return pieces[:, :rank] + pieces[:, rank : 2 * rank] + pieces[:, 2 * rank : 3 * rank]


def backs_kernel(mask, d_ref, images_ref, gram_ref, *refs):
    out_ref = refs[-1]
    chunk = out_ref.shape[1] - LANES
    across = tall_of(chunk, 512)
    out_ref[:, :LANES] = gram_ref[...].astype(out_ref.dtype)
    for at in range(0, chunk, across):
        span = block_at(lax.div(partner("row", mask), 2) * (chunk // across) + at // across, across)
        out_ref[:, LANES + at : LANES + at + across] = jnp.dot(
            images_ref[...], d_ref[:, span], preferred_element_type=F32
        ).astype(out_ref.dtype)


def backs(held, panel, gram, mask, count, *after):
    rows, cols = held.shape
    rank = panel.shape[0]
    return call(
        functools.partial(backs_kernel, mask),
        "backs",
        [panel, gram],
        [shape_of((rank, LANES + cols // count), BF16 if mask else F32)],
        held=held,
        idle=after,
        flops=10**6,
    )[0]


def far_kernel(_, *refs):
    *in_refs, out_ref = refs
    rank = out_ref.shape[0]
    out_ref[:, :rank] = tree_sum([from_pieces(ref[:, :LANES]) for ref in in_refs])
    out_ref[:, LANES:] = tree_sum([ref[:, LANES:].astype(F32) for ref in in_refs])


def combine_kernel(_, *refs):
    *in_refs, far_ref, out_ref = refs
    rank = out_ref.shape[0]
    gram = tree_sum([from_pieces(ref[:, :LANES]) for ref in in_refs]) + far_ref[:, :rank]
    total = tree_sum([ref[:, LANES:].astype(F32) for ref in in_refs]) + far_ref[:, LANES:]
    out_ref[:, :LANES] = with_pieces(gram)
    out_ref[:, LANES:] = total.astype(BF16)


def settle_kernel(_, one_ref, other_ref, out_ref):
    rank = one_ref.shape[0]
    gram = from_pieces(one_ref[:, :LANES]) + from_pieces(other_ref[:, :LANES])
    total = one_ref[:, LANES:].astype(F32) + other_ref[:, LANES:].astype(F32)
    out_ref[...] = square(lower_inverse([gram])[0], total).astype(BF16)


def combine(held, pieces):
    near, far = pieces[: len(pieces) // 2], pieces[len(pieces) // 2 :]
    (far,) = call(far_kernel, "far", far, [shape_of(far[0].shape, F32)], held=held)
    return call(combine_kernel, "combine", [*near, far], [shape_of(near[0].shape, BF16)], held=held)[0]


def settle(held, one, other):
    rank, wide = one.shape
    return call(settle_kernel, "settle", [one, other], [shape_of((rank, wide - LANES), BF16)], held=held)[0]


def images_kernel(masks, tall, partial, tasks, d_ref, *refs):
    x_refs, refs = refs[: len(masks)], refs[len(masks) :]
    if partial:
        sum_ref, refs = refs[0], refs[1:]
    target = refs[1] if tasks else refs[0]
    chunk = x_refs[0].shape[1]

    def body(at, carry):
        rows = block_at(at, tall)
        product = None
        for mask, x_ref in zip(masks, x_refs):
            span = block_at(lax.div(partner("row", mask), 2), chunk)
            term = lax.dot_general(d_ref[rows, span], x_ref[...], ROWS_BY_ROWS, preferred_element_type=F32)
            product = term if product is None else product + term
        product = product.T
        if partial:
            product = product + sum_ref[:, rows]
        target[:, rows] = product.astype(target.dtype)
        return carry

    lax.fori_loop(0, d_ref.shape[0] // tall, body, 0)
    if tasks:
        out_ref, flat = refs
        each = out_ref.shape[2]
        for at in range(tasks):
            out_ref[at] = flat[:, at * each : (at + 1) * each]
    elif len(refs) == 2:
        refs[1][...] = gram_pieces(refs[0][...])


def images(held, blocks, masks, partial=None, last=False, tasks=0):
    rows, cols = held.shape
    rank, chunk = blocks[0].shape
    scratch = ()
    if tasks:
        shapes = [shape_of((tasks, rank, rows // tasks), BF16)]
        scratch = [pltpu.VMEM((rank, rows), BF16)]
    elif last:
        shapes = [shape_of((rank, rows), BF16), shape_of((rank, LANES), BF16)]
    else:
        shapes = [shape_of((rank, rows), F32)]
    return call(
        functools.partial(images_kernel, masks, tall_of(rows, 896, 512, 256, 128), partial is not None, tasks),
        "images",
        [*blocks] + ([] if partial is None else [partial]),
        shapes,
        scratch,
        held=held,
        flops=2 * rows * chunk * 384 * len(masks),
    )


def join_kernel(first, *refs):
    in_refs, out_ref = refs[first : first + 2], refs[-1]
    if len(out_ref.shape) == 2:
        out_ref[...] = jnp.concatenate([ref[...] for ref in in_refs], axis=1)
    else:
        for at, ref in enumerate(in_refs):
            out_ref[at * ref.shape[0] : (at + 1) * ref.shape[0]] = ref[...]


def join(one, other, held=None, axis=0, after=()):
    shape = list(one.shape)
    shape[axis] *= 2
    kernel = functools.partial(join_kernel, 0 if held is None else 1)
    return call(kernel, "join", [one, other], [shape_of(tuple(shape), one.dtype)], held=held, idle=after)[0]


def pack_kernel(masks, _, *refs):
    in_refs, out_ref = refs[: len(masks)], refs[-1]
    chunk = in_refs[0].shape[1]
    for mask, in_ref in zip(masks, in_refs):
        out_ref[0, :, block_at(lax.div(partner("row", mask), 2), chunk)] = in_ref[...]


def left_kernel(groups, *refs):
    in_refs, (gram_ref, panel_ref, whole) = refs[: len(groups)], refs[-3:]
    tasks, rank, each = in_refs[0].shape[-3:]
    for masks, in_ref in zip(groups, in_refs):
        for place, mask in enumerate(masks):
            down = block_at(partner("task", mask), rank)
            for at in range(tasks):
                whole[down, at * each : (at + 1) * each] = in_ref[place, at]
            panel_ref[down, :] = in_ref[place, partner("task", 0)]
    gram_ref[...] = lax.dot_general(whole[...], whole[...], ROWS_BY_ROWS, preferred_element_type=F32)


def left(blocks, groups, after):
    _, tasks, rank, each = blocks[0].shape
    size = tasks * rank
    return call(
        functools.partial(left_kernel, groups),
        "left",
        blocks,
        [shape_of((size, size), F32), shape_of((size, each), BF16)],
        [pltpu.VMEM((size, tasks * each), BF16)],
        idle=[after],
    )


def add_kernel(count, *refs):
    refs[-1][...] = tree_sum([ref[...] for ref in refs[:count]])


def add(terms, *after):
    kernel = functools.partial(add_kernel, len(terms))
    return call(kernel, "add", terms, [shape_of(terms[0].shape, F32)], idle=after, flops=10**6)[0]


def root_begin(gram):
    upper = gram / jnp.sqrt(jnp.sum(gram * gram))
    middle = 0.5 * (3.0 * eye_of(gram.shape[0]).astype(F32) - upper)
    return square(upper, middle), middle


def root_steps(state, count):
    size = state[0].shape[0]
    identity = eye_of(size).astype(F32)

    def step(_, state):
        upper, lower = state
        middle = 0.5 * (3.0 * identity - square(lower, upper))
        both = square(middle, jnp.concatenate([upper, lower], axis=1))
        return both[:, :size], both[:, size:]

    return lax.fori_loop(0, count, step, state)


def root_end(state, gram):
    return state[1] / jnp.sqrt(jnp.sqrt(jnp.sum(gram * gram)))


def right_first_kernel(groups, *refs):
    in_refs, (wide_ref, lower_ref, gram_ref, blocks) = refs[: len(groups)], refs[-4:]
    rank = in_refs[0].shape[1]
    for masks, in_ref in zip(groups, in_refs):
        for place, mask in enumerate(masks):
            wide_ref[block_at(partner("task", mask), rank), :] = in_ref[place]
    wide = wide_ref[...]
    raw = lax.dot_general(wide, wide, ROWS_BY_ROWS, preferred_element_type=F32)
    spans = [slice(task * rank, (task + 1) * rank) for task in range(wide.shape[0] // rank)]
    for task, span in enumerate(spans):
        blocks[task] = raw[span, span]

    def two(at, carry):
        for task, inverse in enumerate(lower_inverse([blocks[2 * at], blocks[2 * at + 1]])):
            blocks[2 * at + task] = inverse
        return carry

    lax.fori_loop(0, len(spans) // 2, two, 0)
    lower_ref[...] = jnp.zeros_like(lower_ref)
    for task, span in enumerate(spans):
        lower_ref[span, span] = blocks[task]
    lower = lower_ref[...]
    gram_ref[...] = square(square(lower, raw), lower.T)


def right_begin_kernel(count, gram_ref, upper_ref, lower_ref):
    upper_ref[...], lower_ref[...] = root_steps(root_begin(gram_ref[...]), count - 1)


def right_steps_kernel(count, upper_in, lower_in, upper_ref, lower_ref):
    upper_ref[...], lower_ref[...] = root_steps((upper_in[...], lower_in[...]), count)


def right_end_kernel(count, gram_ref, upper_ref, lower_ref, change_ref, *refs):
    state = root_steps((upper_ref[...], lower_ref[...]), count)
    refs[-1][...] = square(root_end(state, gram_ref[...]).T, change_ref[...])


def finish_kernel(across, one_ref, other_ref, panel_ref, wide_ref, lower_ref, right_ref, out_ref, made, sems):
    size, cols = wide_ref.shape
    lower = lower_ref[...]
    gram = square(square(lower, one_ref[...] + other_ref[...]), lower.T)
    diagonal = jnp.where(eye_of(size), gram, 0.0)
    down = jnp.sqrt(jnp.sum(diagonal, axis=1, keepdims=True))
    over = jnp.sqrt(jnp.sum(diagonal, axis=0, keepdims=True))
    normed = gram / (down * over)
    mixing = root_end(root_steps(root_begin(normed), ROOT_STEPS - 1), normed) / down * over
    mixed = square(square(lower.T, mixing), right_ref[...])
    panel = panel_ref[...].T
    product = jnp.dot(
        jnp.concatenate([panel, panel], axis=1),
        jnp.concatenate(split_two(mixed), axis=0),
        preferred_element_type=F32,
    )
    side = jnp.concatenate(split_two(product), axis=1)
    copies = []
    for at in range(cols // across):
        span = slice(at * across, (at + 1) * across)
        wide = wide_ref[:, span]
        made[at] = jnp.dot(side, jnp.concatenate([wide, wide], axis=0), preferred_element_type=F32).astype(BF16)
        copies.append(pltpu.make_async_copy(made.at[at], out_ref.at[:, span], sems.at[at]))
        copies[-1].start()
    for copy in copies:
        copy.wait()


def finish(one, other, panel, wide, lower, right_side):
    size, rows = panel.shape
    cols = wide.shape[1]
    across = 512
    return pl.pallas_call(
        functools.partial(finish_kernel, across),
        out_shape=shape_of((rows, cols), BF16),
        in_specs=[IN_VMEM] * 6,
        out_specs=ANYWHERE,
        scratch_shapes=[
            pltpu.VMEM((cols // across, rows, across), BF16),
            pltpu.SemaphoreType.DMA((cols // across,)),
        ],
        compiler_params=pltpu.CompilerParams(vmem_limit_bytes=VMEM_BYTES),
        name="finish",
    )(one, other, panel, wide, lower, right_side)


def send(piece, axis, mask, count):
    return lax.ppermute(piece, axis, [(at, at ^ mask) for at in range(count)])


def gather(piece, axis, count, joining):
    masks, groups, blocks, block = [0], [(0,)], [piece], piece
    bit = count // 2
    while bit:
        received = send(block, axis, bit, count)
        groups.append(tuple(mask ^ bit for mask in masks))
        blocks.append(received)
        masks = masks + [mask ^ bit for mask in masks]
        bit //= 2
        if bit:
            block = joining(block, received)
    return groups, blocks


def local(tasks, parts, task_delta, start_block):
    masks = tuple(range(0, parts, 2))
    nearest, farther = masks[1], masks[2:]
    count = len(masks)
    order = (*reversed(masks[1:]), 0)
    held = pltpu.with_memory_space_constraint(task_delta[0], pltpu.VMEM)
    panel, gram = first(held, start_block[0].T)
    for step in range(ITERS):
        last = step == ITERS - 1
        received, after = {}, []
        for mask in order[:-1]:
            piece = backs(held, panel, gram, mask, count, *after)
            received[mask] = send(piece, "row", mask, parts)
            after = [piece]
        keep = backs(held, panel, gram, 0, count, *after, received[order[0]])
        sums = combine(held, [keep, *[received[mask] for mask in masks[1:]]])
        block = settle(held, sums, send(sums, "row", 1, parts))
        blocks = {mask: send(block, "row", mask, parts) for mask in order[:-1]}
        blocks[0] = block
        (partial,) = images(held, [block, blocks[nearest]], (0, nearest))
        rest = [blocks[mask] for mask in farther]
        if last:
            (own,) = call(
                functools.partial(pack_kernel, masks),
                "pack",
                [blocks[mask] for mask in masks],
                [shape_of((1, block.shape[0], held.shape[1]), BF16)],
                held=held,
                idle=[partial],
            )
            (panel,) = images(held, rest, farther, partial, tasks=tasks)
        else:
            panel, gram = images(held, rest, farther, partial, last=True)
    task_groups, bases = gather(own, "task", tasks, lambda one, other: join(one, other, after=[panel]))
    size = tasks * start_block.shape[2]
    square_shape = shape_of((size, size), F32)
    wide, lower, right_gram = call(
        functools.partial(right_first_kernel, task_groups),
        "right_first",
        bases,
        [shape_of((size, held.shape[1]), BF16), square_shape, square_shape],
        [pltpu.VMEM((tasks, size // tasks, size // tasks), F32)],
    )
    begin, middle = ROOT_STEPS // 2, ROOT_STEPS // 6
    state = call(functools.partial(right_begin_kernel, begin), "right_begin", [right_gram], [square_shape] * 2)
    _, panels = gather(panel[None], "task", tasks, lambda one, other: join(one, other, after=[state[0]]))
    state = call(functools.partial(right_steps_kernel, middle), "right_steps", state, [square_shape] * 2)
    gram, panel = left(panels, task_groups, state[0])
    received = {mask: send(gram, "row", mask, parts) for mask in order[:-1]}
    (right_side,) = call(
        functools.partial(right_end_kernel, ROOT_STEPS - begin - middle),
        "right_end",
        [right_gram, *state, lower],
        [square_shape],
        idle=[gram],
    )
    gram = add([gram, *[received[mask] for mask in masks[1:]]], right_side)
    other = send(gram, "row", 1, parts)
    return finish(gram, other, panel, wide, lower, right_side)


def solution(mesh):
    tasks, parts = mesh.shape["task"], mesh.shape["row"]
    placed = (P("task", "row", None), P("task", None, None))
    return jax.shard_map(
        functools.partial(local, tasks, parts),
        mesh=mesh,
        in_specs=placed,
        out_specs=P(("row", "task"), None),
        check_vma=False,
    )
```

```python
import functools

import jax
import jax.numpy as jnp
from jax import lax
from jax.experimental import pallas as pl
from jax.experimental.pallas import tpu as pltpu
from jax.sharding import PartitionSpec as P

ITERS = 4
ROOT_STEPS = 12
LANES = 128
TILE = 8
F32 = jnp.float32
BF16 = jnp.bfloat16
ROWS_BY_ROWS = (((1,), (1,)), ((), ()))
VMEM_BYTES = 16 * 1024 * 1024
IN_VMEM = pl.BlockSpec(memory_space=pltpu.VMEM)
ANYWHERE = pl.BlockSpec(memory_space=pl.ANY)


def shape_of(shape, kind):
    return jax.ShapeDtypeStruct(shape, kind)


def call(kernel, name, operands, shapes, scratch=(), held=None, idle=(), flops=10**8):
    operands = [*operands, *idle]
    specs = [IN_VMEM] * (len(operands) - len(idle)) + [ANYWHERE] * len(idle)
    if held is not None:
        operands, specs = [held, *operands], [IN_VMEM, *specs]
    return pl.pallas_call(
        kernel,
        out_shape=tuple(shapes),
        in_specs=specs,
        out_specs=(IN_VMEM,) * len(shapes),
        scratch_shapes=list(scratch),
        cost_estimate=pl.CostEstimate(flops=flops, bytes_accessed=10**6, transcendentals=0),
        compiler_params=pltpu.CompilerParams(vmem_limit_bytes=VMEM_BYTES),
        name=name,
    )(*operands)


def split_two(value):
    high = value.astype(BF16)
    return high, (value - high.astype(F32)).astype(BF16)


def split_three(value):
    high = value.astype(BF16)
    rest = value - high.astype(F32)
    middle = rest.astype(BF16)
    return high, middle, (rest - middle.astype(F32)).astype(BF16)


def spread(value, order, axis):
    pieces = split_three(value)
    return jnp.concatenate([pieces[at] for at in order], axis=axis)


def square(left, right):
    return jnp.dot(
        spread(left, (0, 0, 1, 0, 2, 1), 1), spread(right, (0, 1, 0, 2, 0, 1), 0), preferred_element_type=F32
    )


def eye_of(size):
    return lax.broadcasted_iota(jnp.int32, (size, size), 0) == lax.broadcasted_iota(jnp.int32, (size, size), 1)


def tree_sum(values):
    while len(values) > 1:
        values = [values[at] + values[at + 1] for at in range(0, len(values), 2)]
    return values[0]


def lower_inverse(grams):
    size = grams[0].shape[0]
    tiles = size // TILE
    rows = lax.broadcasted_iota(jnp.int32, (TILE, LANES), 0)
    lanes = lax.broadcasted_iota(jnp.int32, (TILE, LANES), 1)
    columns, inverses, scales = [], [], []
    for gram in grams:
        wide = [jnp.broadcast_to(gram[:, at : at + 1], (size, LANES)) for at in range(size)]
        columns.append([[one[TILE * tile : TILE * (tile + 1)] for tile in range(tiles)] for one in wide])
        inverses.append([(rows + TILE * tile == lanes).astype(F32) for tile in range(tiles)])
        scales.append([jnp.zeros((TILE, LANES), F32) for _ in range(tiles)])
    for step in range(size):
        top, place = divmod(step, TILE)
        for cols, inverse, scale in zip(columns, inverses, scales):
            pivot = cols[step][top][place : place + 1]
            reciprocal = 1.0 / pivot
            ratio = [None] * top + [cols[step][tile] * reciprocal for tile in range(top, tiles)]
            for later in range(step + 1, size):
                first, inner = divmod(later, TILE)
                factor = ratio[first][inner : inner + 1]
                for tile in range(first, tiles):
                    cols[later][tile] = cols[later][tile] - cols[step][tile] * factor
            own = inverse[top][place : place + 1]
            for tile in range(top, tiles):
                factor = jnp.where(rows > place, ratio[tile], 0.0) if tile == top else ratio[tile]
                inverse[tile] = inverse[tile] - factor * own
            scale[top] = jnp.where(rows == place, lax.rsqrt(pivot), scale[top])
    return [
        jnp.concatenate([one * down for one, down in zip(inverse, scale)], axis=0)[:, :size]
        for inverse, scale in zip(inverses, scales)
    ]


def gram_pieces(images):
    return with_pieces(lax.dot_general(images, images, ROWS_BY_ROWS, preferred_element_type=F32))


def tall_of(rows, *sizes):
    return next(size for size in (*sizes, rows) if rows % size == 0)


def partner(axis, mask):
    return lax.bitwise_xor(lax.axis_index(axis).astype(jnp.int32), jnp.int32(mask))


def block_at(index, size):
    return pl.ds(pl.multiple_of(index * size, size), size)


def first_kernel(tall, d_ref, x_ref, out_ref, gram_ref, wide):
    wide[...] = x_ref[...].astype(BF16)

    def body(at, carry):
        rows = block_at(at, tall)
        product = lax.dot_general(d_ref[rows, :], wide[...], ROWS_BY_ROWS, preferred_element_type=F32)
        out_ref[:, rows] = product.T.astype(BF16)
        return carry

    lax.fori_loop(0, d_ref.shape[0] // tall, body, 0)
    gram_ref[...] = gram_pieces(out_ref[...])


def first(held, start):
    rows, cols = held.shape
    rank = start.shape[0]
    return call(
        functools.partial(first_kernel, tall_of(rows, 1792, 896, 512, 256, 128)),
        "first",
        [start],
        [shape_of((rank, rows), BF16), shape_of((rank, LANES), BF16)],
        [pltpu.VMEM((rank, cols), BF16)],
        held=held,
        flops=2 * rows * cols * 384,
    )


def with_pieces(gram):
    rank = gram.shape[0]
    return jnp.concatenate([*split_three(gram), jnp.zeros((rank, LANES - 3 * rank), BF16)], axis=1)


def from_pieces(pieces):
    rank = pieces.shape[0]
    pieces = pieces.astype(F32)
    return pieces[:, :rank] + pieces[:, rank : 2 * rank] + pieces[:, 2 * rank : 3 * rank]


def backs_kernel(mask, d_ref, images_ref, gram_ref, *refs):
    out_ref = refs[-1]
    chunk = out_ref.shape[1] - LANES
    across = tall_of(chunk, 512)
    out_ref[:, :LANES] = gram_ref[...].astype(out_ref.dtype)
    for at in range(0, chunk, across):
        span = block_at(lax.div(partner("row", mask), 2) * (chunk // across) + at // across, across)
        out_ref[:, LANES + at : LANES + at + across] = jnp.dot(
            images_ref[...], d_ref[:, span], preferred_element_type=F32
        ).astype(out_ref.dtype)


def backs(held, panel, gram, mask, count, *after):
    rows, cols = held.shape
    rank = panel.shape[0]
    return call(
        functools.partial(backs_kernel, mask),
        "backs",
        [panel, gram],
        [shape_of((rank, LANES + cols // count), BF16 if mask else F32)],
        held=held,
        idle=after,
        flops=10**6,
    )[0]


def far_kernel(_, *refs):
    *in_refs, out_ref = refs
    rank = out_ref.shape[0]
    out_ref[:, :rank] = tree_sum([from_pieces(ref[:, :LANES]) for ref in in_refs])
    out_ref[:, LANES:] = tree_sum([ref[:, LANES:].astype(F32) for ref in in_refs])


def combine_kernel(_, *refs):
    *in_refs, far_ref, out_ref = refs
    rank = out_ref.shape[0]
    gram = tree_sum([from_pieces(ref[:, :LANES]) for ref in in_refs]) + far_ref[:, :rank]
    total = tree_sum([ref[:, LANES:].astype(F32) for ref in in_refs]) + far_ref[:, LANES:]
    out_ref[:, :LANES] = with_pieces(gram)
    out_ref[:, LANES:] = total.astype(BF16)


def settle_kernel(_, one_ref, other_ref, out_ref):
    rank = one_ref.shape[0]
    gram = from_pieces(one_ref[:, :LANES]) + from_pieces(other_ref[:, :LANES])
    total = one_ref[:, LANES:].astype(F32) + other_ref[:, LANES:].astype(F32)
    out_ref[...] = square(lower_inverse([gram])[0], total).astype(BF16)


def combine(held, pieces):
    near, far = pieces[: len(pieces) // 2], pieces[len(pieces) // 2 :]
    (far,) = call(far_kernel, "far", far, [shape_of(far[0].shape, F32)], held=held)
    return call(combine_kernel, "combine", [*near, far], [shape_of(near[0].shape, BF16)], held=held)[0]


def settle(held, one, other):
    rank, wide = one.shape
    return call(settle_kernel, "settle", [one, other], [shape_of((rank, wide - LANES), BF16)], held=held)[0]


def images_kernel(masks, tall, partial, tasks, d_ref, *refs):
    x_refs, refs = refs[: len(masks)], refs[len(masks) :]
    if partial:
        sum_ref, refs = refs[0], refs[1:]
    target = refs[1] if tasks else refs[0]
    chunk = x_refs[0].shape[1]

    def body(at, carry):
        rows = block_at(at, tall)
        product = None
        for mask, x_ref in zip(masks, x_refs):
            span = block_at(lax.div(partner("row", mask), 2), chunk)
            term = lax.dot_general(d_ref[rows, span], x_ref[...], ROWS_BY_ROWS, preferred_element_type=F32)
            product = term if product is None else product + term
        product = product.T
        if partial:
            product = product + sum_ref[:, rows]
        target[:, rows] = product.astype(target.dtype)
        return carry

    lax.fori_loop(0, d_ref.shape[0] // tall, body, 0)
    if tasks:
        out_ref, flat = refs
        each = out_ref.shape[2]
        for at in range(tasks):
            out_ref[at] = flat[:, at * each : (at + 1) * each]
    elif len(refs) == 2:
        refs[1][...] = gram_pieces(refs[0][...])


def images(held, blocks, masks, partial=None, last=False, tasks=0):
    rows, cols = held.shape
    rank, chunk = blocks[0].shape
    scratch = ()
    if tasks:
        shapes = [shape_of((tasks, rank, rows // tasks), BF16)]
        scratch = [pltpu.VMEM((rank, rows), BF16)]
    elif last:
        shapes = [shape_of((rank, rows), BF16), shape_of((rank, LANES), BF16)]
    else:
        shapes = [shape_of((rank, rows), F32)]
    return call(
        functools.partial(images_kernel, masks, tall_of(rows, 896, 512, 256, 128), partial is not None, tasks),
        "images",
        [*blocks] + ([] if partial is None else [partial]),
        shapes,
        scratch,
        held=held,
        flops=2 * rows * chunk * 384 * len(masks),
    )


def join_kernel(first, *refs):
    in_refs, out_ref = refs[first : first + 2], refs[-1]
    if len(out_ref.shape) == 2:
        out_ref[...] = jnp.concatenate([ref[...] for ref in in_refs], axis=1)
    else:
        for at, ref in enumerate(in_refs):
            out_ref[at * ref.shape[0] : (at + 1) * ref.shape[0]] = ref[...]


def join(one, other, held=None, axis=0, after=()):
    shape = list(one.shape)
    shape[axis] *= 2
    kernel = functools.partial(join_kernel, 0 if held is None else 1)
    return call(kernel, "join", [one, other], [shape_of(tuple(shape), one.dtype)], held=held, idle=after)[0]


def pack_kernel(masks, _, *refs):
    in_refs, out_ref = refs[: len(masks)], refs[-1]
    chunk = in_refs[0].shape[1]
    for mask, in_ref in zip(masks, in_refs):
        out_ref[0, :, block_at(lax.div(partner("row", mask), 2), chunk)] = in_ref[...]


def left_kernel(groups, *refs):
    in_refs, (gram_ref, panel_ref, whole) = refs[: len(groups)], refs[-3:]
    tasks, rank, each = in_refs[0].shape[-3:]
    for masks, in_ref in zip(groups, in_refs):
        for place, mask in enumerate(masks):
            down = block_at(partner("task", mask), rank)
            for at in range(tasks):
                whole[down, at * each : (at + 1) * each] = in_ref[place, at]
            panel_ref[down, :] = in_ref[place, partner("task", 0)]
    gram = lax.dot_general(whole[...], whole[...], ROWS_BY_ROWS, preferred_element_type=F32)
    half = gram.shape[0] // 2
    gram_ref[:half] = gram[:half]
    gram_ref[half:, :half] = gram[half : half + half // 2, half:]
    gram_ref[half:, half:] = gram[half + half // 2 :, half:]


def left(blocks, groups, after):
    _, tasks, rank, each = blocks[0].shape
    size = tasks * rank
    return call(
        functools.partial(left_kernel, groups),
        "left",
        blocks,
        [shape_of((size // 4 * 3, size), F32), shape_of((size, each), BF16)],
        [pltpu.VMEM((size, tasks * each), BF16)],
        idle=[after],
    )


def add_kernel(count, *refs):
    refs[-1][...] = tree_sum([ref[...] for ref in refs[:count]])


def add(terms, *after):
    kernel = functools.partial(add_kernel, len(terms))
    return call(kernel, "add", terms, [shape_of(terms[0].shape, F32)], idle=after, flops=10**6)[0]


def root_begin(gram):
    upper = gram / jnp.sqrt(jnp.sum(gram * gram))
    middle = 0.5 * (3.0 * eye_of(gram.shape[0]).astype(F32) - upper)
    return square(upper, middle), middle


def root_steps(state, count):
    size = state[0].shape[0]
    identity = eye_of(size).astype(F32)

    def step(_, state):
        upper, lower = state
        middle = 0.5 * (3.0 * identity - square(lower, upper))
        both = square(middle, jnp.concatenate([upper, lower], axis=1))
        return both[:, :size], both[:, size:]

    return lax.fori_loop(0, count, step, state)


def root_end(state, gram):
    return state[1] / jnp.sqrt(jnp.sqrt(jnp.sum(gram * gram)))


def right_first_kernel(groups, *refs):
    in_refs, (wide_ref, lower_ref, gram_ref, blocks) = refs[: len(groups)], refs[-4:]
    rank = in_refs[0].shape[1]
    for masks, in_ref in zip(groups, in_refs):
        for place, mask in enumerate(masks):
            wide_ref[block_at(partner("task", mask), rank), :] = in_ref[place]
    wide = wide_ref[...]
    raw = lax.dot_general(wide, wide, ROWS_BY_ROWS, preferred_element_type=F32)
    spans = [slice(task * rank, (task + 1) * rank) for task in range(wide.shape[0] // rank)]
    for task, span in enumerate(spans):
        blocks[task] = raw[span, span]

    def two(at, carry):
        for task, inverse in enumerate(lower_inverse([blocks[2 * at], blocks[2 * at + 1]])):
            blocks[2 * at + task] = inverse
        return carry

    lax.fori_loop(0, len(spans) // 2, two, 0)
    lower_ref[...] = jnp.zeros_like(lower_ref)
    for task, span in enumerate(spans):
        lower_ref[span, span] = blocks[task]
    lower = lower_ref[...]
    gram_ref[...] = square(square(lower, raw), lower.T)


def right_begin_kernel(count, gram_ref, upper_ref, lower_ref):
    upper_ref[...], lower_ref[...] = root_steps(root_begin(gram_ref[...]), count - 1)


def right_steps_kernel(count, upper_in, lower_in, upper_ref, lower_ref):
    upper_ref[...], lower_ref[...] = root_steps((upper_in[...], lower_in[...]), count)


def right_end_kernel(count, gram_ref, upper_ref, lower_ref, change_ref, *refs):
    state = root_steps((upper_ref[...], lower_ref[...]), count)
    refs[-1][...] = square(root_end(state, gram_ref[...]).T, change_ref[...])


def finish_kernel(across, one_ref, other_ref, panel_ref, wide_ref, lower_ref, right_ref, out_ref, made, sems):
    size, cols = wide_ref.shape
    lower = lower_ref[...]
    packed = one_ref[...] + other_ref[...]
    half = size // 2
    corner = jnp.concatenate([packed[half:, :half], packed[half:, half:]], axis=0)
    below = jnp.concatenate([packed[:half, half:].T, corner], axis=1)
    raw = jnp.concatenate([packed[:half], below], axis=0)
    gram = square(square(lower, raw), lower.T)
    diagonal = jnp.where(eye_of(size), gram, 0.0)
    down = jnp.sqrt(jnp.sum(diagonal, axis=1, keepdims=True))
    over = jnp.sqrt(jnp.sum(diagonal, axis=0, keepdims=True))
    normed = gram / (down * over)
    mixing = root_end(root_steps(root_begin(normed), ROOT_STEPS - 1), normed) / down * over
    mixed = square(square(lower.T, mixing), right_ref[...])
    panel = panel_ref[...].T
    product = jnp.dot(
        jnp.concatenate([panel, panel], axis=1),
        jnp.concatenate(split_two(mixed), axis=0),
        preferred_element_type=F32,
    )
    side = jnp.concatenate(split_two(product), axis=1)
    copies = []
    for at in range(cols // across):
        span = slice(at * across, (at + 1) * across)
        wide = wide_ref[:, span]
        made[at] = jnp.dot(side, jnp.concatenate([wide, wide], axis=0), preferred_element_type=F32).astype(BF16)
        copies.append(pltpu.make_async_copy(made.at[at], out_ref.at[:, span], sems.at[at]))
        copies[-1].start()
    for copy in copies:
        copy.wait()


def finish(one, other, panel, wide, lower, right_side):
    size, rows = panel.shape
    cols = wide.shape[1]
    across = 512
    return pl.pallas_call(
        functools.partial(finish_kernel, across),
        out_shape=shape_of((rows, cols), BF16),
        in_specs=[IN_VMEM] * 6,
        out_specs=ANYWHERE,
        scratch_shapes=[
            pltpu.VMEM((cols // across, rows, across), BF16),
            pltpu.SemaphoreType.DMA((cols // across,)),
        ],
        compiler_params=pltpu.CompilerParams(vmem_limit_bytes=VMEM_BYTES),
        name="finish",
    )(one, other, panel, wide, lower, right_side)


def send(piece, axis, mask, count):
    return lax.ppermute(piece, axis, [(at, at ^ mask) for at in range(count)])


def gather(piece, axis, count, joining):
    masks, groups, blocks, block = [0], [(0,)], [piece], piece
    bit = count // 2
    while bit:
        received = send(block, axis, bit, count)
        groups.append(tuple(mask ^ bit for mask in masks))
        blocks.append(received)
        masks = masks + [mask ^ bit for mask in masks]
        bit //= 2
        if bit:
            block = joining(block, received)
    return groups, blocks


def local(tasks, parts, task_delta, start_block):
    masks = tuple(range(0, parts, 2))
    nearest, farther = masks[1], masks[2:]
    count = len(masks)
    order = (*reversed(masks[1:]), 0)
    held = pltpu.with_memory_space_constraint(task_delta[0], pltpu.VMEM)
    panel, gram = first(held, start_block[0].T)
    for step in range(ITERS):
        last = step == ITERS - 1
        received, after = {}, []
        for mask in order[:-1]:
            piece = backs(held, panel, gram, mask, count, *after)
            received[mask] = send(piece, "row", mask, parts)
            after = [piece]
        keep = backs(held, panel, gram, 0, count, *after, received[order[0]])
        sums = combine(held, [keep, *[received[mask] for mask in masks[1:]]])
        block = settle(held, sums, send(sums, "row", 1, parts))
        blocks = {mask: send(block, "row", mask, parts) for mask in order[:-1]}
        blocks[0] = block
        (partial,) = images(held, [block, blocks[nearest]], (0, nearest))
        rest = [blocks[mask] for mask in farther]
        if last:
            (own,) = call(
                functools.partial(pack_kernel, masks),
                "pack",
                [blocks[mask] for mask in masks],
                [shape_of((1, block.shape[0], held.shape[1]), BF16)],
                held=held,
                idle=[partial],
            )
            (panel,) = images(held, rest, farther, partial, tasks=tasks)
        else:
            panel, gram = images(held, rest, farther, partial, last=True)
    task_groups, bases = gather(own, "task", tasks, lambda one, other: join(one, other, after=[panel]))
    size = tasks * start_block.shape[2]
    square_shape = shape_of((size, size), F32)
    wide, lower, right_gram = call(
        functools.partial(right_first_kernel, task_groups),
        "right_first",
        bases,
        [shape_of((size, held.shape[1]), BF16), square_shape, square_shape],
        [pltpu.VMEM((tasks, size // tasks, size // tasks), F32)],
    )
    begin, middle = ROOT_STEPS // 2, ROOT_STEPS // 6
    state = call(functools.partial(right_begin_kernel, begin), "right_begin", [right_gram], [square_shape] * 2)
    _, panels = gather(panel[None], "task", tasks, lambda one, other: join(one, other, after=[state[0]]))
    state = call(functools.partial(right_steps_kernel, middle), "right_steps", state, [square_shape] * 2)
    gram, panel = left(panels, task_groups, state[0])
    received = {mask: send(gram, "row", mask, parts) for mask in order[:-1]}
    (right_side,) = call(
        functools.partial(right_end_kernel, ROOT_STEPS - begin - middle),
        "right_end",
        [right_gram, *state, lower],
        [square_shape],
        idle=[gram],
    )
    gram = add([gram, *[received[mask] for mask in masks[1:]]], right_side)
    other = send(gram, "row", 1, parts)
    return finish(gram, other, panel, wide, lower, right_side)


def solution(mesh):
    tasks, parts = mesh.shape["task"], mesh.shape["row"]
    placed = (P("task", "row", None), P("task", None, None))
    return jax.shard_map(
        functools.partial(local, tasks, parts),
        mesh=mesh,
        in_specs=placed,
        out_specs=P(("row", "task"), None),
        check_vma=False,
    )
```

```python
import functools

import jax
import jax.numpy as jnp
from jax import lax
from jax.experimental import pallas as pl
from jax.experimental.pallas import tpu as pltpu
from jax.sharding import PartitionSpec as P

ITERS = 4
ROOT_STEPS = 12
LANES = 128
TILE = 8
F32 = jnp.float32
BF16 = jnp.bfloat16
ROWS_BY_ROWS = (((1,), (1,)), ((), ()))
VMEM_BYTES = 16 * 1024 * 1024
IN_VMEM = pl.BlockSpec(memory_space=pltpu.VMEM)
ANYWHERE = pl.BlockSpec(memory_space=pl.ANY)


def shape_of(shape, kind):
    return jax.ShapeDtypeStruct(shape, kind)


def call(kernel, name, operands, shapes, scratch=(), held=None, idle=(), flops=10**8):
    operands = [*operands, *idle]
    specs = [IN_VMEM] * (len(operands) - len(idle)) + [ANYWHERE] * len(idle)
    if held is not None:
        operands, specs = [held, *operands], [IN_VMEM, *specs]
    return pl.pallas_call(
        kernel,
        out_shape=tuple(shapes),
        in_specs=specs,
        out_specs=(IN_VMEM,) * len(shapes),
        scratch_shapes=list(scratch),
        cost_estimate=pl.CostEstimate(flops=flops, bytes_accessed=10**6, transcendentals=0),
        compiler_params=pltpu.CompilerParams(vmem_limit_bytes=VMEM_BYTES),
        name=name,
    )(*operands)


def split_two(value):
    high = value.astype(BF16)
    return high, (value - high.astype(F32)).astype(BF16)


def split_three(value):
    high = value.astype(BF16)
    rest = value - high.astype(F32)
    middle = rest.astype(BF16)
    return high, middle, (rest - middle.astype(F32)).astype(BF16)


def spread(value, order, axis):
    pieces = split_three(value)
    return jnp.concatenate([pieces[at] for at in order], axis=axis)


def spread_left(value):
    return spread(value, (0, 0, 1, 0, 2, 1), 1)


def spread_right(value):
    return spread(value, (0, 1, 0, 2, 0, 1), 0)


def square(left, right):
    return jnp.dot(spread_left(left), spread_right(right), preferred_element_type=F32)


def eye_of(size):
    return lax.broadcasted_iota(jnp.int32, (size, size), 0) == lax.broadcasted_iota(jnp.int32, (size, size), 1)


def tree_sum(values):
    while len(values) > 1:
        values = [values[at] + values[at + 1] for at in range(0, len(values), 2)]
    return values[0]


def lower_inverse(grams):
    size = grams[0].shape[0]
    tiles = size // TILE
    rows = lax.broadcasted_iota(jnp.int32, (TILE, LANES), 0)
    lanes = lax.broadcasted_iota(jnp.int32, (TILE, LANES), 1)
    columns, inverses, scales = [], [], []
    for gram in grams:
        wide = [jnp.broadcast_to(gram[:, at : at + 1], (size, LANES)) for at in range(size)]
        columns.append([[one[TILE * tile : TILE * (tile + 1)] for tile in range(tiles)] for one in wide])
        inverses.append([(rows + TILE * tile == lanes).astype(F32) for tile in range(tiles)])
        scales.append([jnp.zeros((TILE, LANES), F32) for _ in range(tiles)])
    for step in range(size):
        top, place = divmod(step, TILE)
        for cols, inverse, scale in zip(columns, inverses, scales):
            pivot = cols[step][top][place : place + 1]
            reciprocal = 1.0 / pivot
            ratio = [None] * top + [cols[step][tile] * reciprocal for tile in range(top, tiles)]
            for later in range(step + 1, size):
                first, inner = divmod(later, TILE)
                factor = ratio[first][inner : inner + 1]
                for tile in range(first, tiles):
                    cols[later][tile] = cols[later][tile] - cols[step][tile] * factor
            own = inverse[top][place : place + 1]
            for tile in range(top, tiles):
                factor = jnp.where(rows > place, ratio[tile], 0.0) if tile == top else ratio[tile]
                inverse[tile] = inverse[tile] - factor * own
            scale[top] = jnp.where(rows == place, lax.rsqrt(pivot), scale[top])
    return [
        jnp.concatenate([one * down for one, down in zip(inverse, scale)], axis=0)[:, :size]
        for inverse, scale in zip(inverses, scales)
    ]


def gram_pieces(images):
    return with_pieces(lax.dot_general(images, images, ROWS_BY_ROWS, preferred_element_type=F32))


def tall_of(rows, *sizes):
    return next(size for size in (*sizes, rows) if rows % size == 0)


def partner(axis, mask):
    return lax.bitwise_xor(lax.axis_index(axis).astype(jnp.int32), jnp.int32(mask))


def block_at(index, size):
    return pl.ds(pl.multiple_of(index * size, size), size)


def first_kernel(tall, d_ref, x_ref, out_ref, gram_ref, start, wide, sem):
    copy = pltpu.make_async_copy(x_ref, start, sem)
    copy.start()
    copy.wait()
    wide[...] = start[...].astype(BF16)

    def body(at, carry):
        rows = block_at(at, tall)
        product = lax.dot_general(d_ref[rows, :], wide[...], ROWS_BY_ROWS, preferred_element_type=F32)
        out_ref[:, rows] = product.T.astype(BF16)
        return carry

    lax.fori_loop(0, d_ref.shape[0] // tall, body, 0)
    gram_ref[...] = gram_pieces(out_ref[...])


def first(held, start):
    rows, cols = held.shape
    rank = start.shape[0]
    return call(
        functools.partial(first_kernel, tall_of(rows, 1792, 896, 512, 256, 128)),
        "first",
        [],
        [shape_of((rank, rows), BF16), shape_of((rank, LANES), BF16)],
        [pltpu.VMEM((rank, cols), F32), pltpu.VMEM((rank, cols), BF16), pltpu.SemaphoreType.DMA],
        held=held,
        idle=[start],
        flops=2 * rows * cols * 384,
    )


def with_pieces(gram):
    rank = gram.shape[0]
    return jnp.concatenate([*split_three(gram), jnp.zeros((rank, LANES - 3 * rank), BF16)], axis=1)


def from_pieces(pieces):
    rank = pieces.shape[0]
    pieces = pieces.astype(F32)
    return pieces[:, :rank] + pieces[:, rank : 2 * rank] + pieces[:, 2 * rank : 3 * rank]


def backs_kernel(mask, d_ref, images_ref, gram_ref, *refs):
    out_ref = refs[-1]
    chunk = out_ref.shape[1] - LANES
    across = tall_of(chunk, 512)
    out_ref[:, :LANES] = gram_ref[...].astype(out_ref.dtype)
    for at in range(0, chunk, across):
        span = block_at(lax.div(partner("row", mask), 2) * (chunk // across) + at // across, across)
        out_ref[:, LANES + at : LANES + at + across] = jnp.dot(
            images_ref[...], d_ref[:, span], preferred_element_type=F32
        ).astype(out_ref.dtype)


def backs(held, panel, gram, mask, count, *after):
    rows, cols = held.shape
    rank = panel.shape[0]
    return call(
        functools.partial(backs_kernel, mask),
        "backs",
        [panel, gram],
        [shape_of((rank, LANES + cols // count), BF16 if mask else F32)],
        held=held,
        idle=after,
        flops=10**6,
    )[0]


def far_kernel(_, *refs):
    *in_refs, out_ref = refs
    rank = out_ref.shape[0]
    out_ref[:, :rank] = tree_sum([from_pieces(ref[:, :LANES]) for ref in in_refs])
    out_ref[:, LANES:] = tree_sum([ref[:, LANES:].astype(F32) for ref in in_refs])


def combine_kernel(_, *refs):
    *in_refs, far_ref, out_ref = refs
    rank = out_ref.shape[0]
    gram = tree_sum([from_pieces(ref[:, :LANES]) for ref in in_refs]) + far_ref[:, :rank]
    total = tree_sum([ref[:, LANES:].astype(F32) for ref in in_refs]) + far_ref[:, LANES:]
    out_ref[:, :LANES] = with_pieces(gram)
    out_ref[:, LANES:] = total.astype(BF16)


def settle_kernel(_, one_ref, other_ref, out_ref):
    rank = one_ref.shape[0]
    gram = from_pieces(one_ref[:, :LANES]) + from_pieces(other_ref[:, :LANES])
    total = one_ref[:, LANES:].astype(F32) + other_ref[:, LANES:].astype(F32)
    out_ref[...] = square(lower_inverse([gram])[0], total).astype(BF16)


def combine(held, pieces):
    near, far = pieces[: len(pieces) // 2], pieces[len(pieces) // 2 :]
    (far,) = call(far_kernel, "far", far, [shape_of(far[0].shape, F32)], held=held)
    return call(combine_kernel, "combine", [*near, far], [shape_of(near[0].shape, BF16)], held=held)[0]


def settle(held, one, other):
    rank, wide = one.shape
    return call(settle_kernel, "settle", [one, other], [shape_of((rank, wide - LANES), BF16)], held=held)[0]


def images_kernel(masks, tall, partial, tasks, d_ref, *refs):
    x_refs, refs = refs[: len(masks)], refs[len(masks) :]
    if partial:
        sum_ref, refs = refs[0], refs[1:]
    target = refs[1] if tasks else refs[0]
    chunk = x_refs[0].shape[1]

    def body(at, carry):
        rows = block_at(at, tall)
        product = None
        for mask, x_ref in zip(masks, x_refs):
            span = block_at(lax.div(partner("row", mask), 2), chunk)
            term = lax.dot_general(d_ref[rows, span], x_ref[...], ROWS_BY_ROWS, preferred_element_type=F32)
            product = term if product is None else product + term
        product = product.T
        if partial:
            product = product + sum_ref[:, rows]
        target[:, rows] = product.astype(target.dtype)
        return carry

    lax.fori_loop(0, d_ref.shape[0] // tall, body, 0)
    if tasks:
        out_ref, flat = refs
        each = out_ref.shape[2]
        for at in range(tasks):
            out_ref[at] = flat[:, at * each : (at + 1) * each]
    elif len(refs) == 2:
        refs[1][...] = gram_pieces(refs[0][...])


def images(held, blocks, masks, partial=None, last=False, tasks=0):
    rows, cols = held.shape
    rank, chunk = blocks[0].shape
    scratch = ()
    if tasks:
        shapes = [shape_of((tasks, rank, rows // tasks), BF16)]
        scratch = [pltpu.VMEM((rank, rows), BF16)]
    elif last:
        shapes = [shape_of((rank, rows), BF16), shape_of((rank, LANES), BF16)]
    else:
        shapes = [shape_of((rank, rows), F32)]
    return call(
        functools.partial(images_kernel, masks, tall_of(rows, 896, 512, 256, 128), partial is not None, tasks),
        "images",
        [*blocks] + ([] if partial is None else [partial]),
        shapes,
        scratch,
        held=held,
        flops=2 * rows * chunk * 384 * len(masks),
    )


def join_kernel(first, *refs):
    in_refs, out_ref = refs[first : first + 2], refs[-1]
    if len(out_ref.shape) == 2:
        out_ref[...] = jnp.concatenate([ref[...] for ref in in_refs], axis=1)
    else:
        for at, ref in enumerate(in_refs):
            out_ref[at * ref.shape[0] : (at + 1) * ref.shape[0]] = ref[...]


def join(one, other, held=None, axis=0, after=()):
    shape = list(one.shape)
    shape[axis] *= 2
    kernel = functools.partial(join_kernel, 0 if held is None else 1)
    return call(kernel, "join", [one, other], [shape_of(tuple(shape), one.dtype)], held=held, idle=after)[0]


def pack_kernel(masks, _, *refs):
    in_refs, out_ref = refs[: len(masks)], refs[-1]
    chunk = in_refs[0].shape[1]
    for mask, in_ref in zip(masks, in_refs):
        out_ref[0, :, block_at(lax.div(partner("row", mask), 2), chunk)] = in_ref[...]


def left_kernel(groups, *refs):
    in_refs, (gram_ref, panel_ref, whole) = refs[: len(groups)], refs[-3:]
    tasks, rank, each = in_refs[0].shape[-3:]
    for masks, in_ref in zip(groups, in_refs):
        for place, mask in enumerate(masks):
            down = block_at(partner("task", mask), rank)
            for at in range(tasks):
                whole[down, at * each : (at + 1) * each] = in_ref[place, at]
            panel_ref[down, :] = in_ref[place, partner("task", 0)]
    gram = lax.dot_general(whole[...], whole[...], ROWS_BY_ROWS, preferred_element_type=F32)
    half = gram.shape[0] // 2
    gram_ref[:half] = gram[:half]
    gram_ref[half:, :half] = gram[half : half + half // 2, half:]
    gram_ref[half:, half:] = gram[half + half // 2 :, half:]


def left(blocks, groups, after):
    _, tasks, rank, each = blocks[0].shape
    size = tasks * rank
    return call(
        functools.partial(left_kernel, groups),
        "left",
        blocks,
        [shape_of((size // 4 * 3, size), F32), shape_of((size, each), BF16)],
        [pltpu.VMEM((size, tasks * each), BF16)],
        idle=[after],
    )


def add_kernel(count, *refs):
    refs[-1][...] = tree_sum([ref[...] for ref in refs[:count]])


def add(terms, *after):
    kernel = functools.partial(add_kernel, len(terms))
    return call(kernel, "add", terms, [shape_of(terms[0].shape, F32)], idle=after, flops=10**6)[0]


def root_begin(gram):
    upper = gram / jnp.sqrt(jnp.sum(gram * gram))
    middle = 0.5 * (3.0 * eye_of(gram.shape[0]).astype(F32) - upper)
    return square(upper, middle), middle


def root_steps(state, count):
    size = state[0].shape[0]
    identity = eye_of(size).astype(F32)

    def step(_, state):
        upper, lower = state
        right = spread_right(upper)
        middle = 0.5 * (3.0 * identity - jnp.dot(spread_left(lower), right, preferred_element_type=F32))
        both = jnp.dot(
            spread_left(middle),
            jnp.concatenate([right, spread_right(lower)], axis=1),
            preferred_element_type=F32,
        )
        return both[:, :size], both[:, size:]

    return lax.fori_loop(0, count, step, state)


def root_end(state, gram):
    return state[1] / jnp.sqrt(jnp.sqrt(jnp.sum(gram * gram)))


def right_first_kernel(groups, *refs):
    in_refs, (wide_ref, lower_ref, gram_ref, blocks) = refs[: len(groups)], refs[-4:]
    rank = in_refs[0].shape[1]
    for masks, in_ref in zip(groups, in_refs):
        for place, mask in enumerate(masks):
            wide_ref[block_at(partner("task", mask), rank), :] = in_ref[place]
    wide = wide_ref[...]
    raw = lax.dot_general(wide, wide, ROWS_BY_ROWS, preferred_element_type=F32)
    spans = [slice(task * rank, (task + 1) * rank) for task in range(wide.shape[0] // rank)]
    for task, span in enumerate(spans):
        blocks[task] = raw[span, span]

    def two(at, carry):
        for task, inverse in enumerate(lower_inverse([blocks[2 * at], blocks[2 * at + 1]])):
            blocks[2 * at + task] = inverse
        return carry

    lax.fori_loop(0, len(spans) // 2, two, 0)
    lower_ref[...] = jnp.zeros_like(lower_ref)
    for task, span in enumerate(spans):
        lower_ref[span, span] = blocks[task]
    lower = lower_ref[...]
    gram_ref[...] = square(square(lower, raw), lower.T)


def right_begin_kernel(count, gram_ref, upper_ref, lower_ref):
    upper_ref[...], lower_ref[...] = root_steps(root_begin(gram_ref[...]), count - 1)


def right_steps_kernel(count, upper_in, lower_in, upper_ref, lower_ref):
    upper_ref[...], lower_ref[...] = root_steps((upper_in[...], lower_in[...]), count)


def right_end_kernel(count, gram_ref, upper_ref, lower_ref, change_ref, *refs):
    state = root_steps((upper_ref[...], lower_ref[...]), count)
    refs[-1][...] = square(root_end(state, gram_ref[...]).T, change_ref[...])


def finish_kernel(across, one_ref, other_ref, panel_ref, wide_ref, lower_ref, right_ref, out_ref, made, sems):
    size, cols = wide_ref.shape
    lower = lower_ref[...]
    packed = one_ref[...] + other_ref[...]
    half = size // 2
    corner = jnp.concatenate([packed[half:, :half], packed[half:, half:]], axis=0)
    below = jnp.concatenate([packed[:half, half:].T, corner], axis=1)
    raw = jnp.concatenate([packed[:half], below], axis=0)
    gram = square(square(lower, raw), lower.T)
    diagonal = jnp.where(eye_of(size), gram, 0.0)
    down = jnp.sqrt(jnp.sum(diagonal, axis=1, keepdims=True))
    over = jnp.sqrt(jnp.sum(diagonal, axis=0, keepdims=True))
    normed = gram / (down * over)
    mixing = root_end(root_steps(root_begin(normed), ROOT_STEPS - 1), normed) / down * over
    mixed = square(square(lower.T, mixing), right_ref[...])
    panel = panel_ref[...].T
    product = jnp.dot(
        jnp.concatenate([panel, panel], axis=1),
        jnp.concatenate(split_two(mixed), axis=0),
        preferred_element_type=F32,
    )
    side = jnp.concatenate(split_two(product), axis=1)
    copies = []
    for at in range(cols // across):
        span = slice(at * across, (at + 1) * across)
        wide = wide_ref[:, span]
        made[at] = jnp.dot(side, jnp.concatenate([wide, wide], axis=0), preferred_element_type=F32).astype(BF16)
        copies.append(pltpu.make_async_copy(made.at[at], out_ref.at[:, span], sems.at[at]))
        copies[-1].start()
    for copy in copies:
        copy.wait()


def finish(one, other, panel, wide, lower, right_side):
    size, rows = panel.shape
    cols = wide.shape[1]
    across = 512
    return pl.pallas_call(
        functools.partial(finish_kernel, across),
        out_shape=shape_of((rows, cols), BF16),
        in_specs=[IN_VMEM] * 6,
        out_specs=ANYWHERE,
        scratch_shapes=[
            pltpu.VMEM((cols // across, rows, across), BF16),
            pltpu.SemaphoreType.DMA((cols // across,)),
        ],
        compiler_params=pltpu.CompilerParams(vmem_limit_bytes=VMEM_BYTES),
        name="finish",
    )(one, other, panel, wide, lower, right_side)


def send(piece, axis, mask, count):
    return lax.ppermute(piece, axis, [(at, at ^ mask) for at in range(count)])


def gather(piece, axis, count, joining):
    masks, groups, blocks, block = [0], [(0,)], [piece], piece
    bit = count // 2
    while bit:
        received = send(block, axis, bit, count)
        groups.append(tuple(mask ^ bit for mask in masks))
        blocks.append(received)
        masks = masks + [mask ^ bit for mask in masks]
        bit //= 2
        if bit:
            block = joining(block, received)
    return groups, blocks


def local(tasks, parts, task_delta, start_block):
    masks = tuple(range(0, parts, 2))
    nearest, farther = masks[1], masks[2:]
    count = len(masks)
    order = (*reversed(masks[1:]), 0)
    held = pltpu.with_memory_space_constraint(task_delta[0], pltpu.VMEM)
    panel, gram = first(held, pltpu.with_memory_space_constraint(start_block[0].T, pltpu.HBM))
    for step in range(ITERS):
        last = step == ITERS - 1
        received, after = {}, []
        for mask in order[:-1]:
            piece = backs(held, panel, gram, mask, count, *after)
            received[mask] = send(piece, "row", mask, parts)
            after = [piece]
        keep = backs(held, panel, gram, 0, count, *after, received[order[0]])
        sums = combine(held, [keep, *[received[mask] for mask in masks[1:]]])
        block = settle(held, sums, send(sums, "row", 1, parts))
        blocks = {mask: send(block, "row", mask, parts) for mask in order[:-1]}
        blocks[0] = block
        (partial,) = images(held, [block, blocks[nearest]], (0, nearest))
        rest = [blocks[mask] for mask in farther]
        if last:
            (own,) = call(
                functools.partial(pack_kernel, masks),
                "pack",
                [blocks[mask] for mask in masks],
                [shape_of((1, block.shape[0], held.shape[1]), BF16)],
                held=held,
                idle=[partial],
            )
            (panel,) = images(held, rest, farther, partial, tasks=tasks)
        else:
            panel, gram = images(held, rest, farther, partial, last=True)
    task_groups, bases = gather(own, "task", tasks, lambda one, other: join(one, other, after=[panel]))
    size = tasks * start_block.shape[2]
    square_shape = shape_of((size, size), F32)
    wide, lower, right_gram = call(
        functools.partial(right_first_kernel, task_groups),
        "right_first",
        bases,
        [shape_of((size, held.shape[1]), BF16), square_shape, square_shape],
        [pltpu.VMEM((tasks, size // tasks, size // tasks), F32)],
    )
    begin, middle = ROOT_STEPS // 2, ROOT_STEPS // 6
    state = call(functools.partial(right_begin_kernel, begin), "right_begin", [right_gram], [square_shape] * 2)
    _, panels = gather(panel[None], "task", tasks, lambda one, other: join(one, other, after=[state[0]]))
    state = call(functools.partial(right_steps_kernel, middle), "right_steps", state, [square_shape] * 2)
    gram, panel = left(panels, task_groups, state[0])
    received = {mask: send(gram, "row", mask, parts) for mask in order[:-1]}
    (right_side,) = call(
        functools.partial(right_end_kernel, ROOT_STEPS - begin - middle),
        "right_end",
        [right_gram, *state, lower],
        [square_shape],
        idle=[gram],
    )
    gram = add([gram, *[received[mask] for mask in masks[1:]]], right_side)
    other = send(gram, "row", 1, parts)
    return finish(gram, other, panel, wide, lower, right_side)


def solution(mesh):
    tasks, parts = mesh.shape["task"], mesh.shape["row"]
    placed = (P("task", "row", None), P("task", None, None))
    return jax.shard_map(
        functools.partial(local, tasks, parts),
        mesh=mesh,
        in_specs=placed,
        out_specs=P(("row", "task"), None),
        check_vma=False,
    )
```
